32 devices in a mesh: sweep: 8 (over z, x), span: 4 (over y, core).
Axes of the slice: x: 2, y: 2, z: 4, core: 2. Of those that a mesh axis runs over, the one named last changes fastest.
Arguments:
- residual_in: float32 [8, 4, 4, 100, 128], P('sweep', 'span'), may hold values from -6 to 6
- diag_inverse: bfloat16 [8, 4, 100, 100, 128], P('sweep', 'span'), may hold values from -2 to 2
- up_block: bfloat16 [8, 4, 100, 100, 128], P('sweep', 'span'), may hold values from -0.4375 to 0.4375
- side_blocks: bfloat16 [8, 4, 3, 100, 100, 128], P('sweep', 'span'), may hold values from -1 to 1
- up_cols: int32 [8, 4, 128], P('sweep', 'span'), may hold values from 0 to 127, as said below
- down_cols: int32 [8, 4, 128], P('sweep', 'span'), may hold values from 0 to 127, as said below
- left_cols: int32 [8, 4, 128], P('sweep', 'span'), may hold values from 0 to 127, as said below
- right_cols: int32 [8, 4, 128], P('sweep', 'span'), may hold values from 0 to 127, as said below
Outputs:
- smoothed: float32 [8, 4, 4, 100, 128], P('sweep', 'span')
The draws below stay inside these ranges and needn't reach their ends.
Inputs may be any that keep to these rules, and one draw needn't show every extreme that they name: For each slab and partition, a permutation of the 128 positions; down_cols of slab s is the inverse of up_cols of slab s + 1. `down_cols`: for each slab and partition, a permutation of the 128 positions. For each slab and partition, a permutation of the 128 positions; right_cols of partition p is the inverse of left_cols of partition p + 1. `right_cols`: for each slab and partition, a permutation of the 128 positions.
All inputs are finite; a program needn't handle non-finite values.
Results may differ from the reference program's by a relative error of at most 0.0003.
Values sent between devices are 32-bit elements; how exact they have to be, the bound alone decides.
No kernel may reach another device: no remote copies, remote signals or barrier semaphores. Data moves between devices by JAX's collectives and lax.ppermute only.
A program may use at most 128 MiB of HBM per device.

```python
import math
import jax
import jax.numpy as jnp
from jax import lax

B = 100
K = 4
M = 128
SLABS = 8
PARTS_SIZE = 4


def many_perms(key, count):
    keys = jax.random.split(key, count)
    return jax.vmap(lambda single: jax.random.permutation(single, M))(keys).astype(jnp.int32)


def flow_perms(key):
    return many_perms(jax.random.fold_in(key, 501), SLABS * PARTS_SIZE).reshape(SLABS, PARTS_SIZE, M)


def span_perms(key):
    return many_perms(jax.random.fold_in(key, 502), SLABS * PARTS_SIZE).reshape(SLABS, PARTS_SIZE, M)


def draw_up_cols(key, part):
    return flow_perms(key)


def draw_down_cols(key, part):
    shared = flow_perms(key)
    return jnp.argsort(jnp.roll(shared, -1, axis=0), axis=-1, stable=True).astype(jnp.int32)


def draw_left_cols(key, part):
    return span_perms(key)


def draw_right_cols(key, part):
    shared = span_perms(key)
    return jnp.argsort(jnp.roll(shared, -1, axis=1), axis=-1, stable=True).astype(jnp.int32)


def draw_residual_in(key, part):
    key = jax.random.fold_in(key, 11)
    shape = (SLABS, PARTS_SIZE, K, B, M)
    values = jax.random.normal(key, shape, jnp.float32)
    return jnp.clip(values, -5.0, 5.0)


def draw_diag_inverse(key, part):
    key = jax.random.fold_in(key, 13)
    scale_key, noise_key = jax.random.split(key)
    identity = jnp.eye(B, dtype=jnp.float32)[:, :, None]
    scales = jax.random.uniform(scale_key, (SLABS, PARTS_SIZE, 1, 1, M), jnp.float32, 0.7, 1.3)
    noise = 0.03 * jax.random.normal(noise_key, (SLABS, PARTS_SIZE, B, B, M), jnp.float32)
    return (scales * (identity + noise)).astype(jnp.bfloat16)


def one_face(key, spread):
    shape = (SLABS, PARTS_SIZE, B, B, M)
    values = jax.random.normal(key, shape, jnp.float32)
    return jnp.clip(values * (spread / math.sqrt(B)), -1.0, 1.0).astype(jnp.bfloat16)


def draw_side_blocks(key, part):
    key = jax.random.fold_in(key, 17)
    faces = [one_face(jax.random.fold_in(key, 0), 0.8), one_face(jax.random.fold_in(key, 1), 0.2), one_face(jax.random.fold_in(key, 2), 0.2)]
    return jnp.stack(faces, axis=2)


def levels(own_key, extent, cuts, smallest, top_value):
    def one(dim, parts):
        steps = jax.random.uniform(jax.random.fold_in(jax.random.fold_in(own_key, 6), dim), (parts,), jnp.float32, smallest / len(cuts), top_value / len(cuts))
        return jnp.repeat(jnp.exp(steps), extent[dim] // parts).reshape((-1,) + (1,) * (len(extent) - dim - 1))

    gain = one(*cuts[0])
    for cut in cuts[1:]:
        gain = gain * one(*cut)
    return gain


def gaussian(key, shape, width, most, pieces=(), kind=jnp.bfloat16):
    values = width * jax.random.normal(key, shape, jnp.float32)
    if pieces:
        values = values * levels(key, shape, pieces, -0.22, 0.18)
    return jnp.clip(values, -most, most).astype(kind)


def setup_inputs(seed: int = 0) -> dict:
    splits = jax.random.split(jax.random.key(seed), 9)
    residual_in = draw_residual_in(jax.random.fold_in(splits[8], 71), 0)
    diag_inverse = draw_diag_inverse(jax.random.fold_in(splits[8], 71), 0)
    up_block = gaussian(splits[2], (SLABS, PARTS_SIZE, B, B, M), (2 * B) ** -0.5, 0.4375, ((0, 8), (1, 4)))
    side_blocks = draw_side_blocks(jax.random.fold_in(splits[8], 71), 0)
    up_cols = draw_up_cols(jax.random.fold_in(splits[8], 71), 0)
    down_cols = draw_down_cols(jax.random.fold_in(splits[8], 71), 0)
    left_cols = draw_left_cols(jax.random.fold_in(splits[8], 71), 0)
    right_cols = draw_right_cols(jax.random.fold_in(splits[8], 71), 0)
    return {"residual_in": residual_in, "diag_inverse": diag_inverse, "up_block": up_block, "side_blocks": side_blocks, "up_cols": up_cols, "down_cols": down_cols, "left_cols": left_cols, "right_cols": right_cols}


def product(block, field):
    return jnp.einsum("pijm,pkjm->pkim", block.astype(jnp.float32), field.astype(jnp.float32), precision=lax.Precision.HIGHEST)


def select(field, columns):
    return jnp.take_along_axis(field, columns[:, None, None, :], axis=3)


def half_sweep(residual_in, diag_inverse, up_block, side_blocks, up_cols, down_cols, left_cols, right_cols, old_field, forward):
    zero_slab = jnp.zeros_like(old_field[:1])
    next_old = jnp.concatenate([old_field[1:], zero_slab], 0)
    prev_old = jnp.concatenate([zero_slab, old_field[:-1]], 0)

    def advance(carried, inputs):
        source, inverse, upward, sideway, upc, downc, leftc, rightc, current, next_slab, prev_slab = inputs
        zero_part = jnp.zeros_like(current[:1])
        left_src = jnp.concatenate([zero_part, current[:-1]], 0)
        right_src = jnp.concatenate([current[1:], zero_part], 0)
        if forward:
            up_src = carried
            down_src = next_slab
        else:
            up_src = prev_slab
            down_src = carried
        total = source - product(upward, select(up_src, upc))
        total = total - product(sideway[:, 0], select(down_src, downc))
        total = total - product(sideway[:, 1], select(left_src, leftc))
        total = total - product(sideway[:, 2], select(right_src, rightc))
        fresh_value = product(inverse, total)
        return fresh_value, fresh_value

    inputs = (residual_in, diag_inverse, up_block, side_blocks, up_cols, down_cols, left_cols, right_cols, old_field, next_old, prev_old)
    start = jnp.zeros(old_field.shape[1:], jnp.float32)
    _, result = lax.scan(advance, start, inputs, reverse=not forward)
    return result


def reference(residual_in, diag_inverse, up_block, side_blocks, up_cols, down_cols, left_cols, right_cols):
    field = jnp.zeros(residual_in.shape, jnp.float32)
    for forward in (True, False, True, False):
        field = half_sweep(residual_in, diag_inverse, up_block, side_blocks, up_cols, down_cols, left_cols, right_cols, field, forward)
    return field
```

```python
import functools

import jax
import jax.numpy as jnp
from jax import lax
from jax.experimental import pallas as pl
from jax.experimental.pallas import tpu as pltpu
from jax.sharding import PartitionSpec as P

LANES = 128
SUBLANES = 8
VMEM_LIMIT = 16 * 1024 * 1024


def product(matrix, vector, rows, unroll=10):
    count = matrix.shape[0]

    def body(step, total):
        for inner in range(unroll):
            j = step * unroll + inner
            total = total + matrix[j] * vector[pl.ds(j, 1), :]
        return total

    start = jnp.zeros((rows, matrix.shape[2]), jnp.float32)
    return lax.fori_loop(0, count // unroll, body, start)


def gathered(value, columns):
    index = jnp.broadcast_to(columns, value.shape)
    return jnp.take_along_axis(value, index, axis=1, mode="promise_in_bounds")


def lateral_sum(left, right, from_left, from_right, index, spare):
    rows = spare.shape[0]
    spare[...] = gathered(from_left[...], index[2:3, :])
    total = product(left, spare, rows)
    spare[...] = gathered(from_right[...], index[3:4, :])
    return total + product(right, spare, rows)


def task_kernel(
    flags, diag, up, down, left, right, index, source, incoming, from_left, from_right, chain_in, side_in,
    value, chain, side, spare
):
    rows = spare.shape[0]
    vector = flags[1]

    @pl.when(flags[5] == 1)
    def _():
        side[flags[7]] = lateral_sum(left, right, from_left, from_right, index, spare)

    @pl.when(flags[0] == 1)
    def _():
        base = source[vector] - chain[vector] - side[vector]
        value[...] = base
        chain[vector] = jnp.zeros_like(base)

        def take_chain(matrix, row):
            spare[...] = gathered(incoming[...], index[row : row + 1, :])
            term = product(matrix, spare, rows)
            chain[vector] = term
            value[...] = value[...] - term

        @pl.when((flags[2] == 1) & (flags[3] == 1))
        def _():
            take_chain(up, 0)

        @pl.when((flags[2] == 1) & (flags[3] == 0))
        def _():
            take_chain(down, 1)

        spare[...] = value[...]
        value[...] = product(diag, spare, rows)


def side_kernel(flags, left, right, index, from_left, from_right, side_in, side, spare):
    @pl.when(flags[6] == 1)
    def _():
        side[flags[7]] = lateral_sum(left, right, from_left, from_right, index, spare)


def in_vmem(count):
    return [pl.BlockSpec(memory_space=pltpu.VMEM)] * count


def run_task(flags, mats, index, source, incoming, sides, chain, side):
    shape = incoming.shape
    return pl.pallas_call(
        task_kernel,
        out_shape=(
            pltpu.VMEM(shape, jnp.float32),
            pltpu.VMEM(chain.shape, jnp.float32),
            pltpu.VMEM(side.shape, jnp.float32),
        ),
        in_specs=[pl.BlockSpec(memory_space=pltpu.SMEM)] + in_vmem(12),
        out_specs=tuple(in_vmem(3)),
        scratch_shapes=[pltpu.VMEM(shape, jnp.float32)],
        input_output_aliases={11: 1, 12: 2},
        compiler_params=pltpu.CompilerParams(vmem_limit_bytes=VMEM_LIMIT),
        name="task",
    )(flags, *mats, index, source, incoming, *sides, chain, side)


def run_side(flags, mats, index, sides, side):
    shape = sides[0].shape
    return pl.pallas_call(
        side_kernel,
        out_shape=pltpu.VMEM(side.shape, jnp.float32),
        in_specs=[pl.BlockSpec(memory_space=pltpu.SMEM)] + in_vmem(6),
        out_specs=pl.BlockSpec(memory_space=pltpu.VMEM),
        scratch_shapes=[pltpu.VMEM(shape, jnp.float32)],
        input_output_aliases={6: 0},
        compiler_params=pltpu.CompilerParams(vmem_limit_bytes=VMEM_LIMIT),
        name="side",
    )(flags, mats[3], mats[4], index, *sides, side)


def turned(block):
    padded = -block.shape[0] % SUBLANES
    out = jnp.pad(jnp.transpose(block, (1, 0, 2)), ((0, 0), (0, padded), (0, 0))).astype(jnp.float32)
    return pltpu.with_memory_space_constraint(out, pltpu.VMEM)


def at_tick(tick, place, count, vectors):
    forward = lax.rem(tick - place + 2 * count, 2) == 0
    rank = jnp.where(forward, place, count - 1 - place)
    since = jnp.where(forward, tick - place, tick - rank - count)
    late = since >= 2 * count
    since = jnp.where(late, since - 2 * count, since)
    active = (since >= 0) & (since < 2 * vectors)
    vector = jnp.clip(since // 2, 0, vectors - 1)
    half = jnp.where(forward, 0, 1) + jnp.where(late, 2, 0)
    return active, vector, rank, forward, half


def per_device(
    residual_in, diag_inverse, up_block, side_blocks, up_cols, down_cols, left_cols, right_cols
):
    source = residual_in[0, 0]
    vectors, size, _ = source.shape
    rows = size + -size % SUBLANES
    source = jnp.pad(source, ((0, 0), (0, rows - size), (0, 0)))
    mats = tuple(
        turned(block)
        for block in (
            diag_inverse[0, 0], up_block[0, 0], side_blocks[0, 0, 0], side_blocks[0, 0, 1], side_blocks[0, 0, 2]
        )
    )
    index = jnp.stack([up_cols[0, 0], down_cols[0, 0], left_cols[0, 0], right_cols[0, 0]])
    place = lax.axis_index("sweep")
    count = lax.axis_size("sweep")
    parts = lax.axis_size("span")
    ticks = 4 * count + 2 * (vectors - 1)

    def one_tick(tick, parity, state):
        incoming, from_left, from_right, chain, side, out = state
        active, vector, rank, forward, half = at_tick(tick, place, count, vectors)
        was_active, was_vector, _, _, was_half = at_tick(tick - 1, place, count, vectors)
        crossing = was_active & (was_half < 3)
        first = crossing & active & (rank == 0) & (half > 0) & (vector == was_vector)
        flags = jnp.stack(
            [
                jnp.where(flag, 1, 0) if flag.dtype == jnp.bool_ else flag
                for flag in (
                    active, vector, rank > 0, forward, half == 3, first, crossing & ~first, was_vector
                )
            ]
        ).astype(jnp.int32)
        value, chain, side = run_task(
            flags, mats, index, source, incoming, (from_left, from_right), chain, side
        )
        swap = [(s, s + 1) for s in range(parity, count - 1, 2)]
        incoming = lax.ppermute(value, "sweep", swap + [(b, a) for a, b in swap])
        new_left = lax.ppermute(value, "span", [(p, p + 1) for p in range(parts - 1)])
        new_right = lax.ppermute(value, "span", [(p + 1, p) for p in range(parts - 1)])
        side = run_side(flags, mats, index, (from_left, from_right), side)
        out = jnp.where(
            (active & (half == 3) & (jnp.arange(vectors) == vector))[:, None, None], value[:size], out
        )
        return incoming, new_left, new_right, chain, side, out

    def two_ticks(pair, state):
        state = one_tick(2 * pair, 0, state)
        return one_tick(2 * pair + 1, 1, state)

    single = jnp.zeros((rows, LANES), jnp.float32)
    several = jnp.zeros((vectors, rows, LANES), jnp.float32)
    state = (single, single, single, several, several, jnp.zeros_like(residual_in[0, 0]))
    state = lax.fori_loop(0, ticks // 2, two_ticks, state)
    return state[5][None, None]


def solution(mesh):
    return jax.shard_map(
        per_device,
        mesh=mesh,
        in_specs=(
            P("sweep", "span", None, None, None),
            P("sweep", "span", None, None, None),
            P("sweep", "span", None, None, None),
            P("sweep", "span", None, None, None, None),
            P("sweep", "span", None),
            P("sweep", "span", None),
            P("sweep", "span", None),
            P("sweep", "span", None),
        ),
        out_specs=P("sweep", "span", None, None, None),
        check_vma=False,
    )
```

```python
import functools

import jax
import jax.numpy as jnp
from jax import lax
from jax.experimental import pallas as pl
from jax.experimental.pallas import tpu as pltpu
from jax.sharding import PartitionSpec as P

LANES = 128
SUBLANES = 8
VMEM_LIMIT = 8 * 1024 * 1024


def product(matrix, vector, rows, unroll=10):
    count = matrix.shape[0]

    def body(step, total):
        for inner in range(unroll):
            j = step * unroll + inner
            total = total + matrix[j] * vector[pl.ds(j, 1), :]
        return total

    start = jnp.zeros((rows, matrix.shape[2]), jnp.float32)
    return lax.fori_loop(0, count // unroll, body, start)


def gathered(value, columns):
    index = jnp.broadcast_to(columns, value.shape)
    return jnp.take_along_axis(value, index, axis=1, mode="promise_in_bounds")


def lateral_sum(flags, left, right, from_left, from_right, index, spare, slot):
    rows = spare.shape[0]
    spare[...] = gathered(from_left[slot], index[2:3, :])
    total = product(left, spare, rows)
    total = jnp.where(flags[8] == 1, total, 0.0)
    spare[...] = gathered(from_right[slot], index[3:4, :])
    return total + jnp.where(flags[9] == 1, product(right, spare, rows), 0.0)


def task_kernel(
    flags, index, source, incoming, from_left, from_right,
    diag_in, up_in, down_in, left_in, right_in, pair_in, chain_in, side_in,
    value, diag, up, down, left, right, pair, chain, side, spare
):
    rows = spare.shape[0]
    vector = flags[1]

    @pl.when(flags[5] == 1)
    def _():
        side[flags[7]] = lateral_sum(flags, left, right, from_left, from_right, index, spare, 1)

    @pl.when(flags[0] == 1)
    def _():
        base = source[vector] - chain[vector] - side[vector]
        value[...] = base
        chain[vector] = jnp.zeros_like(base)

        def take_chain(matrix, row):
            spare[...] = gathered(incoming[...], index[row : row + 1, :])
            term = product(matrix, spare, rows)
            chain[vector] = term
            value[...] = value[...] - term

        @pl.when((flags[2] == 1) & (flags[3] == 1))
        def _():
            take_chain(up, 0)

        @pl.when((flags[2] == 1) & (flags[3] == 0))
        def _():
            take_chain(down, 1)

        spare[...] = value[...]
        fresh = product(diag, spare, rows)
        value[...] = fresh
        pair[flags[4]] = fresh


def side_kernel(flags, index, from_left, from_right, left_in, right_in, side_in, left, right, side, spare):
    @pl.when(flags[6] == 1)
    def _():
        side[flags[7]] = lateral_sum(flags, left, right, from_left, from_right, index, spare, flags[4])


def in_vmem(count):
    return [pl.BlockSpec(memory_space=pltpu.VMEM)] * count


def held(*arrays):
    return tuple(pltpu.VMEM(array.shape, array.dtype) for array in arrays)


def run_task(flags, index, source, incoming, sides, kept):
    return pl.pallas_call(
        task_kernel,
        out_shape=held(incoming, *kept),
        in_specs=[pl.BlockSpec(memory_space=pltpu.SMEM)] + in_vmem(5 + len(kept)),
        out_specs=tuple(in_vmem(1 + len(kept))),
        scratch_shapes=[pltpu.VMEM(incoming.shape, jnp.float32)],
        input_output_aliases={6 + n: 1 + n for n in range(len(kept))},
        compiler_params=pltpu.CompilerParams(vmem_limit_bytes=VMEM_LIMIT),
        name="task",
    )(flags, index, source, incoming, *sides, *kept)


def run_side(flags, index, sides, kept):
    return pl.pallas_call(
        side_kernel,
        out_shape=held(*kept),
        in_specs=[pl.BlockSpec(memory_space=pltpu.SMEM)] + in_vmem(3 + len(kept)),
        out_specs=tuple(in_vmem(len(kept))),
        scratch_shapes=[pltpu.VMEM(sides[0].shape[1:], jnp.float32)],
        input_output_aliases={4 + n: n for n in range(len(kept))},
        compiler_params=pltpu.CompilerParams(vmem_limit_bytes=VMEM_LIMIT),
        name="side",
    )(flags, index, *sides, *kept)


def turned(block):
    padded = -block.shape[0] % SUBLANES
    return jnp.pad(jnp.transpose(block, (1, 0, 2)), ((0, 0), (0, padded), (0, 0))).astype(jnp.float32)


def at_tick(tick, place, count, vectors):
    forward = lax.rem(tick - place + 2 * count, 2) == 0
    rank = jnp.where(forward, place, count - 1 - place)
    since = jnp.where(forward, tick - place, tick - rank - count)
    late = since >= 2 * count
    since = jnp.where(late, since - 2 * count, since)
    active = (since >= 0) & (since < 2 * vectors)
    vector = jnp.clip(since // 2, 0, vectors - 1)
    half = jnp.where(forward, 0, 1) + jnp.where(late, 2, 0)
    return active, vector, rank, forward, half


def per_device(
    residual_in, diag_inverse, up_block, side_blocks, up_cols, down_cols, left_cols, right_cols
):
    source = residual_in[0, 0]
    vectors, size, _ = source.shape
    rows = size + -size % SUBLANES
    source = jnp.pad(source, ((0, 0), (0, rows - size), (0, 0)))
    mats = tuple(
        turned(block)
        for block in (
            diag_inverse[0, 0], up_block[0, 0], side_blocks[0, 0, 0], side_blocks[0, 0, 1], side_blocks[0, 0, 2]
        )
    )
    index = jnp.stack([up_cols[0, 0], down_cols[0, 0], left_cols[0, 0], right_cols[0, 0]])
    place = lax.axis_index("sweep")
    count = lax.axis_size("sweep")
    parts = lax.axis_size("span")
    part = lax.axis_index("span")
    ticks = 4 * count + 2 * (vectors - 1)

    def one_tick(tick, parity, state):
        incoming, from_left, from_right, kept, out = state
        active, vector, rank, forward, half = at_tick(tick, place, count, vectors)
        was_active, was_vector, _, _, was_half = at_tick(tick - 2, place, count, vectors)
        crossing = was_active & (was_half < 3)
        if parity == 0:
            last_active, last_vector, _, _, last_half = at_tick(tick - 1, place, count, vectors)
            first = last_active & (last_half < 3) & active & (rank == 0) & (vector == last_vector)
            later = crossing
        else:
            first = jnp.zeros((), jnp.bool_)
            now_active, now_vector, now_rank, _, _ = at_tick(tick - 1, place, count, vectors)
            later = crossing & ~(now_active & (now_rank == 0) & (now_vector == was_vector))
        side_vector = jnp.where(first, vector, was_vector)
        flags = [
            active, vector, rank > 0, forward, parity, first, later, side_vector, part > 0, part < parts - 1
        ]
        later_flags = list(flags)
        later_flags[7] = was_vector
        flags, later_flags = (
            jnp.stack([jnp.asarray(flag).astype(jnp.int32) for flag in group]) for group in (flags, later_flags)
        )
        value, *kept = run_task(flags, index, source, incoming, (from_left, from_right), kept)
        diag, up, down, left, right, pair, chain, side = kept
        swap = [(s, s + 1) for s in range(parity, count - 1, 2)]
        alone = [s for s in range(count) if all(s not in two for two in swap)]
        incoming = lax.ppermute(value, "sweep", swap + [(b, a) for a, b in swap] + [(s, s) for s in alone])
        left, right, side = run_side(later_flags, index, (from_left, from_right), (left, right, side))
        if parity == 1:
            from_left = lax.ppermute(pair, "span", [(p, (p + 1) % parts) for p in range(parts)])
            from_right = lax.ppermute(pair, "span", [((p + 1) % parts, p) for p in range(parts)])
        out = jnp.where(
            (active & (half == 3) & (jnp.arange(vectors) == vector))[:, None, None], value[:size], out
        )
        return incoming, from_left, from_right, [diag, up, down, left, right, pair, chain, side], out

    def two_ticks(pair, state):
        state = one_tick(2 * pair, 0, state)
        return one_tick(2 * pair + 1, 1, state)

    single = jnp.zeros((rows, LANES), jnp.float32)
    double = jnp.zeros((2, rows, LANES), jnp.float32)
    several = jnp.zeros((vectors, rows, LANES), jnp.float32)
    state = (single, double, double, [*mats, double, several, several], jnp.zeros_like(residual_in[0, 0]))
    state = lax.fori_loop(0, ticks // 2, two_ticks, state)
    return state[4][None, None]


def solution(mesh):
    return jax.shard_map(
        per_device,
        mesh=mesh,
        in_specs=(
            P("sweep", "span", None, None, None),
            P("sweep", "span", None, None, None),
            P("sweep", "span", None, None, None),
            P("sweep", "span", None, None, None, None),
            P("sweep", "span", None),
            P("sweep", "span", None),
            P("sweep", "span", None),
            P("sweep", "span", None),
        ),
        out_specs=P("sweep", "span", None, None, None),
        check_vma=False,
    )
```

```python
import functools

import jax
import jax.numpy as jnp
from jax import lax
from jax.experimental import pallas as pl
from jax.experimental.pallas import tpu as pltpu
from jax.sharding import PartitionSpec as P

SUBLANES = 8
VMEM_LIMIT = 8 * 1024 * 1024


def task_at(tick, place, count, vectors, choose=jnp.where):
    forward = ((tick - place) & 1) == 0
    rank = choose(forward, place, count - 1 - place)
    since = tick - rank - choose(forward, 0, count)
    late = since >= 2 * count
    since = choose(late, since - 2 * count, since)
    active = (since >= 0) & (since < 2 * vectors)
    half = choose(forward, 0, 1) + choose(late, 2, 0)
    return active, choose(active, since >> 1, 0), rank, forward, half


def turns(task):
    active, _, rank, _, half = task
    return active & (rank == 0) & (half > 0)


def crosses(task):
    return task[0] & (task[4] < 3)


def left_for_later(tick, at):
    taken = turns(at(tick - 1)) if tick & 1 else False
    return crosses(at(tick - 2)) & (taken ^ True)


def product(matrix, vector, rows, unroll=10):
    def body(step, total):
        for inner in range(unroll):
            j = step * unroll + inner
            total = total + matrix[j] * vector[pl.ds(j, 1), :]
        return total

    start = jnp.zeros((rows, matrix.shape[2]), jnp.float32)
    return lax.fori_loop(0, matrix.shape[0] // unroll, body, start)


def gathered(value, columns):
    index = jnp.broadcast_to(columns, value.shape)
    return jnp.take_along_axis(value, index, axis=1, mode="promise_in_bounds")


def add_lateral(side, vector, left, right, from_left, from_right, index, spare, slot):
    rows = spare.shape[0]
    part = lax.axis_index("span")
    side[vector] = jnp.zeros(side.shape[1:], jnp.float32)

    @pl.when(part > 0)
    def _():
        spare[...] = gathered(from_left[slot], index[2:3, :])
        side[vector] = product(left, spare, rows)

    @pl.when(part < lax.axis_size("span") - 1)
    def _():
        spare[...] = gathered(from_right[slot], index[3:4, :])
        side[vector] = side[vector] + product(right, spare, rows)


def task_kernel(
    tick, tasks, index, source, incoming, from_left, from_right,
    diag_in, up_in, down_in, left_in, right_in, pair_in, chain_in, side_in, out_in,
    value, diag, up, down, left, right, pair, chain, side, out, spare
):
    rows = spare.shape[0]
    vectors, size, _ = out.shape
    task = task_at(tick, lax.axis_index("sweep"), lax.axis_size("sweep"), vectors)
    active, vector, rank, forward, half = task

    if any(turns(one) for one in tasks):

        @pl.when(turns(task))
        def _():
            add_lateral(side, vector, left, right, from_left, from_right, index, spare, 1)

    @pl.when(active)
    def _():
        base = source[vector] - chain[vector] - side[vector]
        value[...] = base
        chain[vector] = jnp.zeros_like(base)

        def take_chain(matrix, row):
            spare[...] = gathered(incoming[...], index[row : row + 1, :])
            term = product(matrix, spare, rows)
            chain[vector] = term
            value[...] = value[...] - term

        if any(one[0] and one[2] > 0 and one[3] for one in tasks):

            @pl.when((rank > 0) & forward)
            def _():
                take_chain(up, 0)

        if any(one[0] and one[2] > 0 and not one[3] for one in tasks):

            @pl.when((rank > 0) & (forward ^ True))
            def _():
                take_chain(down, 1)

        spare[...] = value[...]
        fresh = product(diag, spare, rows)
        value[...] = fresh
        pair[tick & 1] = fresh

        if any(one[0] and one[4] == 3 for one in tasks):

            @pl.when(half == 3)
            def _():
                out[vector] = fresh[:size]


def side_kernel(tick, vectors, index, from_left, from_right, left_in, right_in, side_in, left, right, side, spare):
    def at(when):
        return task_at(when, lax.axis_index("sweep"), lax.axis_size("sweep"), vectors)

    @pl.when(left_for_later(tick, at))
    def _():
        add_lateral(side, at(tick - 2)[1], left, right, from_left, from_right, index, spare, tick & 1)


def in_vmem(count):
    return [pl.BlockSpec(memory_space=pltpu.VMEM)] * count


def call(kernel, name, fixed, kept, fresh, spare):
    return pl.pallas_call(
        kernel,
        out_shape=tuple(pltpu.VMEM(a.shape, a.dtype) for a in (*fresh, *kept)),
        in_specs=in_vmem(len(fixed) + len(kept)),
        out_specs=tuple(in_vmem(len(fresh) + len(kept))),
        scratch_shapes=[pltpu.VMEM(spare, jnp.float32)],
        input_output_aliases={len(fixed) + n: len(fresh) + n for n in range(len(kept))},
        compiler_params=pltpu.CompilerParams(vmem_limit_bytes=VMEM_LIMIT),
        name=name,
    )(*fixed, *kept)


def turned(block):
    padded = -block.shape[0] % SUBLANES
    return jnp.pad(jnp.transpose(block, (1, 0, 2)), ((0, 0), (0, padded), (0, 0))).astype(jnp.float32)


def per_device(
    residual_in, diag_inverse, up_block, side_blocks, up_cols, down_cols, left_cols, right_cols
):
    source = residual_in[0, 0]
    vectors, size, lanes = source.shape
    rows = size + -size % SUBLANES
    single = (rows, lanes)
    source = jnp.pad(source, ((0, 0), (0, rows - size), (0, 0)))
    diag, up, down, left, right = (
        turned(block)
        for block in (
            diag_inverse[0, 0], up_block[0, 0], side_blocks[0, 0, 0], side_blocks[0, 0, 1], side_blocks[0, 0, 2]
        )
    )
    index = jnp.stack([up_cols[0, 0], down_cols[0, 0], left_cols[0, 0], right_cols[0, 0]])
    count = lax.axis_size("sweep")
    parts = lax.axis_size("span")
    ticks = 4 * count + 2 * (vectors - 1)

    incoming = jnp.zeros(single, jnp.float32)
    pair = from_left = from_right = jnp.zeros((2, *single), jnp.float32)
    chain = side = jnp.zeros((vectors, *single), jnp.float32)
    out = jnp.zeros((vectors, size, lanes), jnp.float32)

    def at(place):
        return lambda when: task_at(when, place, count, vectors, lambda which, a, b: a if which else b)

    def any_task(when, test):
        return any(test(at(place)(when)) for place in range(count))

    for tick in range(ticks):
        value, diag, up, down, left, right, pair, chain, side, out = call(
            functools.partial(task_kernel, tick, [at(place)(tick) for place in range(count)]),
            "task",
            (index, source, incoming, from_left, from_right),
            (diag, up, down, left, right, pair, chain, side, out),
            (incoming,),
            single,
        )
        if any_task(tick + 1, lambda one: one[0] and one[2] > 0):
            swap = [(s, s + 1) for s in range(tick & 1, count - 1, 2)]
            alone = [s for s in range(count) if all(s not in two for two in swap)]
            incoming = lax.ppermute(value, "sweep", swap + [(b, a) for a, b in swap] + [(s, s) for s in alone])
        if any(left_for_later(tick, at(place)) for place in range(count)):
            left, right, side = call(
                functools.partial(side_kernel, tick, vectors),
                "side",
                (index, from_left, from_right),
                (left, right, side),
                (),
                single,
            )
        if tick & 1 and (any_task(tick, crosses) or any_task(tick - 1, crosses)):
            from_left = lax.ppermute(pair, "span", [(p, (p + 1) % parts) for p in range(parts)])
            from_right = lax.ppermute(pair, "span", [((p + 1) % parts, p) for p in range(parts)])
    return out[None, None]


def solution(mesh):
    return jax.shard_map(
        per_device,
        mesh=mesh,
        in_specs=(
            P("sweep", "span", None, None, None),
            P("sweep", "span", None, None, None),
            P("sweep", "span", None, None, None),
            P("sweep", "span", None, None, None, None),
            P("sweep", "span", None),
            P("sweep", "span", None),
            P("sweep", "span", None),
            P("sweep", "span", None),
        ),
        out_specs=P("sweep", "span", None, None, None),
        check_vma=False,
    )
```

```python
import functools

import jax
import jax.numpy as jnp
from jax import lax
from jax.experimental import pallas as pl
from jax.experimental.pallas import tpu as pltpu
from jax.sharding import PartitionSpec as P

SUBLANES = 8
VMEM_LIMIT = 16 * 1024 * 1024
LATERAL_START = 4


def task_at(tick, place, count, vectors, choose=jnp.where):
    forward = ((tick - place) & 1) == 0
    rank = choose(forward, place, count - 1 - place)
    since = tick - rank - choose(forward, 0, count)
    late = since >= 2 * count
    since = choose(late, since - 2 * count, since)
    active = (since >= 0) & (since < 2 * vectors)
    half = choose(forward, 0, 1) + choose(late, 2, 0)
    return active, choose(active, since >> 1, 0), rank, forward, half


def turns(task):
    active, _, rank, _, half = task
    return active & (rank == 0) & (half > 0)


def lateral_plan(count, vectors):
    ticks = 4 * count + 2 * (vectors - 1)
    sent = [[-1] * count for _ in range(ticks)]
    urgent = [[False] * count for _ in range(ticks)]
    for slab in range(count):
        waiting = []
        for half in range(3):
            rank = count - 1 - slab if half & 1 else slab
            for vector in range(vectors):
                made = 2 * vector + half * count + rank
                used = 2 * vector + (half + 1) * count + count - 1 - rank
                if used == made + 1:
                    sent[made][slab] = vector
                    urgent[made][slab] = True
                else:
                    waiting.append((used, made, vector))
        for parity in range(2):
            left = sorted(waiting)
            for tick in range(LATERAL_START + parity, ticks, 2):
                ready = [one for one in left if one[1] <= tick]
                if sent[tick][slab] >= 0 or not ready:
                    continue
                assert tick <= ready[0][0] - 2
                sent[tick][slab] = ready[0][2]
                left.remove(ready[0])
            assert not left
    return sent, urgent


def pick(values, place):
    result = jnp.int32(values[0])
    for at, value in enumerate(values):
        if value != values[0]:
            result = jnp.where(place == at, value, result)
    return result


def product(matrix, vector, rows, unroll=20):
    def body(step, total):
        for inner in range(unroll):
            j = step * unroll + inner
            total = total + matrix[j] * vector[pl.ds(j, 1), :]
        return total

    start = jnp.zeros((rows, matrix.shape[2]), jnp.float32)
    return lax.fori_loop(0, matrix.shape[0] // unroll, body, start)


def gathered(value, columns):
    index = jnp.broadcast_to(columns, value.shape)
    return jnp.take_along_axis(value, index, axis=1, mode="promise_in_bounds")


def take_lateral(base, vector, left, right, left_cols, right_cols, arrived, spare, parity):
    rows = spare.shape[0]
    part = lax.axis_index("span")
    on_right = (part & 1) == parity

    @pl.when(on_right & (part < lax.axis_size("span") - 1))
    def _():
        spare[...] = gathered(arrived[...], right_cols[...])
        base[vector] = base[vector] - product(right, spare, rows)

    @pl.when((on_right ^ True) & (part > 0))
    def _():
        spare[...] = gathered(arrived[...], left_cols[...])
        base[vector] = base[vector] - product(left, spare, rows)


def prepare_kernel(block, ready, wide):
    size, _, lanes = block.shape[-3:]
    rows = ready.shape[1]
    lead = (0,) * (len(block.shape) - 3)
    wide[pl.ds(size * rows, (rows - size) * rows), :] = jnp.zeros(((rows - size) * rows, lanes), jnp.float32)

    def widen(i, _):
        wide[pl.ds(pl.multiple_of(i * rows, SUBLANES), size), :] = block[(*lead, i)].astype(jnp.float32)
        return 0

    lax.fori_loop(0, size, widen, 0, unroll=4)

    def turn(j, _):
        for i in range(0, rows, SUBLANES):
            ready[j, pl.ds(i, SUBLANES), :] = wide[pl.ds(i * rows + j, SUBLANES, stride=rows), :]
        return 0

    lax.fori_loop(0, size, turn, 0, unroll=4)


def first_kernel(block, residual, ready, base, source, blank, wide):
    prepare_kernel(block, ready, wide)
    vectors, size, lanes = residual.shape
    rows = base.shape[1]
    base[:, pl.ds(rows - SUBLANES, SUBLANES), :] = jnp.zeros((vectors, SUBLANES, lanes), jnp.float32)
    base[:, pl.ds(0, size), :] = residual[...]
    source[...] = base[...]
    blank[...] = jnp.zeros_like(blank)


def later_kernel(block, base_in, ready, base, wide):
    prepare_kernel(block, ready, wide)


def task_kernel(
    tick, tasks, sent, columns_and_inputs, kept, values, spare
):
    up_cols, down_cols, left_cols, right_cols, source, incoming, arrived = columns_and_inputs
    value, cross = values
    diag, up, down, left, right, base, latest, out = kept
    rows = spare.shape[0]
    vectors, size, _ = out.shape
    place = lax.axis_index("sweep")
    task = task_at(tick, place, lax.axis_size("sweep"), vectors)
    active, vector, rank, forward, half = task

    if any(turns(one) for one in tasks):

        @pl.when(turns(task))
        def _():
            take_lateral(base, vector, left, right, left_cols, right_cols, incoming, spare, 0)
            take_lateral(base, vector, left, right, left_cols, right_cols, arrived, spare, 1)

    @pl.when(active)
    def _():
        known = base[vector]
        value[...] = known
        base[vector] = source[vector]

        def take_chain(matrix, columns):
            spare[...] = gathered(incoming[...], columns[...])
            term = product(matrix, spare, rows)
            value[...] = known - term
            base[vector] = source[vector] - term

        if any(one[0] and one[2] > 0 and one[3] for one in tasks):

            @pl.when((rank > 0) & forward)
            def _():
                take_chain(up, up_cols)

        if any(one[0] and one[2] > 0 and not one[3] for one in tasks):

            @pl.when((rank > 0) & (forward ^ True))
            def _():
                take_chain(down, down_cols)

        spare[...] = value[...]
        fresh = product(diag, spare, rows)
        value[...] = fresh
        latest[vector] = fresh

        if any(one[0] and one[4] == 3 for one in tasks):

            @pl.when(half == 3)
            def _():
                out[vector] = fresh[:size]

    if any(one >= 0 for one in sent):
        chosen = pick(sent, place)

        @pl.when(chosen >= 0)
        def _():
            cross[...] = latest[chosen]


def side_kernel(parity, sent, columns_and_inputs, kept, values, spare):
    left_cols, right_cols, arrived = columns_and_inputs
    left, right, base = kept
    vector = pick(sent, lax.axis_index("sweep"))

    @pl.when(vector >= 0)
    def _():
        take_lateral(base, vector, left, right, left_cols, right_cols, arrived, spare, parity)


def in_vmem(count):
    return [pl.BlockSpec(memory_space=pltpu.VMEM)] * count


def held(shape):
    return pltpu.VMEM(shape, jnp.float32)


def call(kernel, name, fixed, kept, fresh, spare):
    def body(*refs):
        inputs, outputs = refs[: len(fixed)], refs[len(fixed) + len(kept) : -1]
        kernel(inputs, outputs[: len(kept)], outputs[len(kept) :], refs[-1])

    return pl.pallas_call(
        body,
        out_shape=tuple(held(shape) for shape in [*(a.shape for a in kept), *fresh]),
        in_specs=in_vmem(len(fixed) + len(kept)),
        out_specs=tuple(in_vmem(len(fresh) + len(kept))),
        scratch_shapes=[held(spare)],
        input_output_aliases={len(fixed) + n: n for n in range(len(kept))},
        compiler_params=pltpu.CompilerParams(vmem_limit_bytes=VMEM_LIMIT),
        name=name,
    )(*fixed, *kept)


def first_call(block, residual, rows):
    vectors, size, lanes = residual.shape
    several = (vectors, rows, lanes)
    return pl.pallas_call(
        first_kernel,
        out_shape=(held((size, rows, lanes)), held(several), held(several), held((rows, lanes))),
        in_specs=in_vmem(2),
        out_specs=tuple(in_vmem(4)),
        scratch_shapes=[held((rows * rows, lanes))],
        compiler_params=pltpu.CompilerParams(vmem_limit_bytes=VMEM_LIMIT),
        name="first",
    )(block, residual)


def later_call(block, face, base):
    size, _, lanes = block.shape[-3:]
    rows = base.shape[1]
    lead = block.shape[:-3]
    spec = pl.BlockSpec(
        (1,) * len(lead) + block.shape[-3:], lambda step: (0,) * (len(lead) - 1) + (face, 0, 0, 0), memory_space=pltpu.VMEM
    )
    whole = pl.BlockSpec(memory_space=pltpu.VMEM)
    return pl.pallas_call(
        later_kernel,
        grid=(1,),
        out_shape=(held((size, rows, lanes)), held(base.shape)),
        in_specs=[spec, whole],
        out_specs=(whole, whole),
        scratch_shapes=[held((rows * rows, lanes))],
        input_output_aliases={1: 1},
        compiler_params=pltpu.CompilerParams(vmem_limit_bytes=VMEM_LIMIT),
        name="later",
    )(block, base)


def per_device(
    residual_in, diag_inverse, up_block, side_blocks, up_cols, down_cols, left_cols, right_cols
):
    vectors, size, lanes = residual_in.shape[2:]
    rows = size + -size % SUBLANES
    columns = [one.reshape(1, lanes) for one in (up_cols, down_cols, left_cols, right_cols)]
    count = lax.axis_size("sweep")
    parts = lax.axis_size("span")
    ticks = 4 * count + 2 * (vectors - 1)
    sent, urgent = lateral_plan(count, vectors)
    even_pairs = [(p, p + 1) for p in range(0, parts - 1, 2)]
    odd_pairs = [(p, p + 1) for p in range(1, parts - 1, 2)]

    def closed(pairs, members):
        alone = [one for one in members if all(one not in two for two in pairs)]
        return [*pairs, *((b, a) for a, b in pairs), *((one, one) for one in alone)]

    def device(slab, part):
        return slab * parts + part

    diag, base, source, blank = first_call(diag_inverse[0, 0], residual_in[0, 0], rows)
    up = down = left = right = None
    latest, out = pl.pallas_call(
        lambda *refs: None,
        out_shape=(held((vectors, rows, lanes)), held((vectors, size, lanes))),
        out_specs=tuple(in_vmem(2)),
        name="room",
    )()
    incoming = arrived = blank
    late_blocks = [(up_block, 0), (side_blocks, 0), (side_blocks, 1), (side_blocks, 2)]
    mats = [diag, blank, blank, blank, blank]

    for tick in range(ticks):
        tasks = [task_at(tick, place, count, vectors, lambda which, a, b: a if which else b) for place in range(count)]
        used = 1 + sum(mat is not blank for mat in mats[1:])
        *kept, value, cross = call(
            lambda fixed, kept, fresh, spare, used=used, tick=tick, tasks=tasks: task_kernel(
                tick, tasks, sent[tick], fixed, [*kept[:used], *[None] * (5 - used), *kept[used:]], fresh, spare
            ),
            "task",
            (*columns, source, incoming, arrived),
            (*mats[:used], base, latest, out),
            ((rows, lanes), (rows, lanes)),
            (rows, lanes),
        )
        mats[:used] = kept[:used]
        base, latest, out = kept[used:]

        after = [
            task_at(tick + 1, place, count, vectors, lambda which, a, b: a if which else b) for place in range(count)
        ]
        previous, crossing = (arrived, sent[tick - 1] if tick else [-1] * count)
        if any(urgent[tick]) or any(one[0] and one[2] > 0 for one in after):
            swap = [(s, s + 1) for s in range(tick & 1, count - 1, 2)]
            alone = [s for s in range(count) if all(s not in two for two in swap)]
            pairs = [(device(a, p), device(b, p)) for a, b in swap for p in range(parts)]
            pairs += [(device(s, a), device(s, b)) for s in alone for a, b in even_pairs]
            incoming = lax.ppermute(value, ("sweep", "span"), closed(pairs, range(count * parts)))
        if any(one >= 0 for one in sent[tick]):
            arrived = lax.ppermute(cross, "span", closed(odd_pairs if tick & 1 else even_pairs, range(parts)))
        crossing = [-1 if tick and urgent[tick - 1][s] else one for s, one in enumerate(crossing)]
        if any(one >= 0 for one in crossing):
            mats[3], mats[4], base = call(
                functools.partial(side_kernel, (tick - 1) & 1, crossing),
                "side",
                (columns[2], columns[3], previous),
                (mats[3], mats[4], base),
                (),
                (rows, lanes),
            )
        if tick < len(late_blocks):
            mats[1 + tick], base = later_call(*late_blocks[tick], base)
    return out[None, None]


def solution(mesh):
    return jax.shard_map(
        per_device,
        mesh=mesh,
        in_specs=(
            P("sweep", "span", None, None, None),
            P("sweep", "span", None, None, None),
            P("sweep", "span", None, None, None),
            P("sweep", "span", None, None, None, None),
            P("sweep", "span", None),
            P("sweep", "span", None),
            P("sweep", "span", None),
            P("sweep", "span", None),
        ),
        out_specs=P("sweep", "span", None, None, None),
        check_vma=False,
    )
```

```python
import functools

import jax
import jax.numpy as jnp
from jax import lax
from jax.experimental import pallas as pl
from jax.experimental.pallas import tpu as pltpu
from jax.sharding import PartitionSpec as P

SUBLANES = 8
VMEM_LIMIT = 2 * 1024 * 1024
PREPARE_LIMIT = 12 * 1024 * 1024
LATERAL_START = 4
CHUNKS = 4


def task_at(tick, place, count, vectors, choose=jnp.where):
    forward = ((tick - place) & 1) == 0
    rank = choose(forward, place, count - 1 - place)
    since = tick - rank - choose(forward, 0, count)
    late = since >= 2 * count
    since = choose(late, since - 2 * count, since)
    active = (since >= 0) & (since < 2 * vectors)
    half = choose(forward, 0, 1) + choose(late, 2, 0)
    return active, choose(active, since >> 1, 0), rank, forward, half


def turns(task):
    active, _, rank, _, half = task
    return active & (rank == 0) & (half > 0)


def lateral_plan(count, vectors):
    ticks = 4 * count + 2 * (vectors - 1)
    sent = [[-1] * count for _ in range(ticks)]
    urgent = [[False] * count for _ in range(ticks)]
    for slab in range(count):
        waiting = []
        for half in range(3):
            rank = count - 1 - slab if half & 1 else slab
            for vector in range(vectors):
                made = 2 * vector + half * count + rank
                used = 2 * vector + (half + 1) * count + count - 1 - rank
                if used == made + 1:
                    sent[made][slab] = vector
                    urgent[made][slab] = True
                else:
                    waiting.append((used, made, vector))
        for parity in range(2):
            left = sorted(waiting)
            for tick in range(LATERAL_START + parity, ticks, 2):
                ready = [one for one in left if one[1] <= tick]
                if sent[tick][slab] >= 0 or not ready:
                    continue
                assert tick <= ready[0][0] - 2
                sent[tick][slab] = ready[0][2]
                left.remove(ready[0])
            assert not left
    return sent, urgent


def pick(values, place):
    result = jnp.int32(values[0])
    for at, value in enumerate(values):
        if value != values[0]:
            result = jnp.where(place == at, value, result)
    return result


def product(matrix, vector, rows, unroll=20):
    def body(step, total):
        for inner in range(unroll):
            j = step * unroll + inner
            total = total + matrix[j] * vector[pl.ds(j, 1), :]
        return total

    start = jnp.zeros((rows, matrix.shape[2]), jnp.float32)
    return lax.fori_loop(0, matrix.shape[0] // unroll, body, start)


def gathered(value, columns):
    index = jnp.broadcast_to(columns, value.shape)
    return jnp.take_along_axis(value, index, axis=1, mode="promise_in_bounds")


def take_lateral(base, vector, left, right, left_cols, right_cols, arrived, spare, parity):
    rows = spare.shape[0]
    part = lax.axis_index("span")
    on_right = (part & 1) == parity

    @pl.when(on_right & (part < lax.axis_size("span") - 1))
    def _():
        spare[...] = gathered(arrived[...], right_cols[...])
        base[vector] = base[vector] - product(right, spare, rows)

    @pl.when((on_right ^ True) & (part > 0))
    def _():
        spare[...] = gathered(arrived[...], left_cols[...])
        base[vector] = base[vector] - product(left, spare, rows)


def prepare(block, ready, narrow, wide, sems):
    size, _, lanes = block.shape
    rows = ready.shape[1]
    share = size // CHUNKS
    copies = [
        pltpu.make_async_copy(block.at[pl.ds(n * share, share)], narrow.at[pl.ds(n * share, share)], sems.at[n])
        for n in range(CHUNKS)
    ]
    for copy in copies:
        copy.start()
    wide[pl.ds(size * rows, (rows - size) * rows), :] = jnp.zeros(((rows - size) * rows, lanes), jnp.float32)

    def widen(i, _):
        wide[pl.ds(pl.multiple_of(i * rows, SUBLANES), size), :] = narrow[i].astype(jnp.float32)
        return 0

    for n, copy in enumerate(copies):
        copy.wait()
        lax.fori_loop(n * share, (n + 1) * share, widen, 0, unroll=5)

    def turn(j, _):
        for i in range(0, rows, SUBLANES):
            ready[j, pl.ds(i, SUBLANES), :] = wide[pl.ds(i * rows + j, SUBLANES, stride=rows), :]
        return 0

    lax.fori_loop(0, size, turn, 0, unroll=4)


def first_kernel(block, residual, *refs):
    hbm_columns, (ready, base, source, blank, *columns), (narrow, wide, sems, column_sems) = (
        refs[:4], refs[4:12], refs[12:]
    )
    copies = [
        pltpu.make_async_copy(there, here, column_sems.at[n])
        for n, (there, here) in enumerate(zip(hbm_columns, columns))
    ]
    for copy in copies:
        copy.start()
    prepare(block, ready, narrow, wide, sems)
    vectors, size, lanes = residual.shape
    rows = base.shape[1]
    base[:, pl.ds(rows - SUBLANES, SUBLANES), :] = jnp.zeros((vectors, SUBLANES, lanes), jnp.float32)
    base[:, pl.ds(0, size), :] = residual[...]
    source[...] = base[...]
    blank[...] = jnp.zeros_like(blank)
    for copy in copies:
        copy.wait()


def later_kernel(face, block, base_in, ready, base, narrow, wide, sems):
    prepare(block.at[(0,) * (len(block.shape) - 4) + (face,)], ready, narrow, wide, sems)


def task_kernel(
    tick, tasks, sent, columns_and_inputs, kept, values, spare
):
    up_cols, down_cols, left_cols, right_cols, source, incoming, arrived = columns_and_inputs
    value, cross = values
    diag, up, down, left, right, base, latest, out = kept
    rows = spare.shape[0]
    vectors, size, _ = out.shape
    place = lax.axis_index("sweep")
    task = task_at(tick, place, lax.axis_size("sweep"), vectors)
    active, vector, rank, forward, half = task

    if any(turns(one) for one in tasks):

        @pl.when(turns(task))
        def _():
            take_lateral(base, vector, left, right, left_cols, right_cols, incoming, spare, 0)
            take_lateral(base, vector, left, right, left_cols, right_cols, arrived, spare, 1)

    @pl.when(active)
    def _():
        known = base[vector]
        value[...] = known
        base[vector] = source[vector]

        def take_chain(matrix, columns):
            spare[...] = gathered(incoming[...], columns[...])
            term = product(matrix, spare, rows)
            value[...] = known - term
            base[vector] = source[vector] - term

        if any(one[0] and one[2] > 0 and one[3] for one in tasks):

            @pl.when((rank > 0) & forward)
            def _():
                take_chain(up, up_cols)

        if any(one[0] and one[2] > 0 and not one[3] for one in tasks):

            @pl.when((rank > 0) & (forward ^ True))
            def _():
                take_chain(down, down_cols)

        spare[...] = value[...]
        fresh = product(diag, spare, rows)
        value[...] = fresh
        latest[vector] = fresh

        if any(one[0] and one[4] == 3 for one in tasks):

            @pl.when(half == 3)
            def _():
                out[vector] = fresh[:size]

    if any(one >= 0 for one in sent):
        chosen = pick(sent, place)

        @pl.when(chosen >= 0)
        def _():
            cross[...] = latest[chosen]


def side_kernel(parity, sent, columns_and_inputs, kept, values, spare):
    left_cols, right_cols, arrived = columns_and_inputs
    left, right, base = kept
    vector = pick(sent, lax.axis_index("sweep"))

    @pl.when(vector >= 0)
    def _():
        take_lateral(base, vector, left, right, left_cols, right_cols, arrived, spare, parity)


def in_vmem(count):
    return [pl.BlockSpec(memory_space=pltpu.VMEM)] * count


def far(array):
    return pltpu.with_memory_space_constraint(array, pltpu.HBM)


def held(shape):
    return pltpu.VMEM(shape, jnp.float32)


def call(kernel, name, fixed, kept, fresh, spare):
    def body(*refs):
        inputs, outputs = refs[: len(fixed)], refs[len(fixed) + len(kept) : -1]
        kernel(inputs, outputs[: len(kept)], outputs[len(kept) :], refs[-1])

    return pl.pallas_call(
        body,
        out_shape=tuple(held(shape) for shape in [*(a.shape for a in kept), *fresh]),
        in_specs=in_vmem(len(fixed) + len(kept)),
        out_specs=tuple(in_vmem(len(fresh) + len(kept))),
        scratch_shapes=[held(spare)],
        input_output_aliases={len(fixed) + n: n for n in range(len(kept))},
        compiler_params=pltpu.CompilerParams(vmem_limit_bytes=VMEM_LIMIT),
        name=name,
    )(*fixed, *kept)


def preparing(size, rows, lanes):
    return [
        pltpu.VMEM((size, size, lanes), jnp.bfloat16),
        held((rows * rows, lanes)),
        pltpu.SemaphoreType.DMA((CHUNKS,)),
    ]


def first_call(block, residual, columns, rows):
    vectors, size, lanes = residual.shape
    several = (vectors, rows, lanes)
    in_hbm = pl.BlockSpec(memory_space=pltpu.HBM)
    return pl.pallas_call(
        first_kernel,
        out_shape=(
            held((size, rows, lanes)), held(several), held(several), held((rows, lanes)),
            *(pltpu.VMEM(one.shape, one.dtype) for one in columns),
        ),
        in_specs=[in_hbm, *in_vmem(1), *[in_hbm] * 4],
        out_specs=tuple(in_vmem(8)),
        scratch_shapes=[*preparing(size, rows, lanes), pltpu.SemaphoreType.DMA((4,))],
        compiler_params=pltpu.CompilerParams(vmem_limit_bytes=PREPARE_LIMIT),
        name="first",
    )(far(block), residual, *(far(one) for one in columns))


def later_call(block, face, base):
    size, _, lanes = block.shape[-3:]
    rows = base.shape[1]
    return pl.pallas_call(
        functools.partial(later_kernel, face),
        out_shape=(held((size, rows, lanes)), held(base.shape)),
        in_specs=[pl.BlockSpec(memory_space=pltpu.HBM), *in_vmem(1)],
        out_specs=tuple(in_vmem(2)),
        scratch_shapes=preparing(size, rows, lanes),
        input_output_aliases={1: 1},
        compiler_params=pltpu.CompilerParams(vmem_limit_bytes=PREPARE_LIMIT),
        name="later",
    )(far(block), base)


def per_device(
    residual_in, diag_inverse, up_block, side_blocks, up_cols, down_cols, left_cols, right_cols
):
    vectors, size, lanes = residual_in.shape[2:]
    rows = size + -size % SUBLANES
    columns = [one.reshape(1, lanes) for one in (up_cols, down_cols, left_cols, right_cols)]
    count = lax.axis_size("sweep")
    parts = lax.axis_size("span")
    ticks = 4 * count + 2 * (vectors - 1)
    sent, urgent = lateral_plan(count, vectors)
    even_pairs = [(p, p + 1) for p in range(0, parts - 1, 2)]
    odd_pairs = [(p, p + 1) for p in range(1, parts - 1, 2)]

    def closed(pairs, members):
        alone = [one for one in members if all(one not in two for two in pairs)]
        return [*pairs, *((b, a) for a, b in pairs), *((one, one) for one in alone)]

    def device(slab, part):
        return slab * parts + part

    diag, base, source, blank, *columns = first_call(diag_inverse[0, 0], residual_in[0, 0], columns, rows)
    latest, out = pl.pallas_call(
        lambda *refs: None,
        out_shape=(held((vectors, rows, lanes)), held((vectors, size, lanes))),
        out_specs=tuple(in_vmem(2)),
        name="room",
    )()
    incoming = arrived = blank
    late_blocks = [(up_block, 0), *((side_blocks, face) for face in range(3))]
    mats = [diag, blank, blank, blank, blank]

    def tasks_at(tick):
        return [task_at(tick, place, count, vectors, lambda which, a, b: a if which else b) for place in range(count)]

    for tick in range(ticks):
        tasks = tasks_at(tick)
        used = 1 + sum(mat is not blank for mat in mats[1:])
        turning = any(turns(one) for one in tasks)
        *kept, value, cross = call(
            lambda fixed, kept, fresh, spare, used=used, tick=tick, tasks=tasks: task_kernel(
                tick, tasks, sent[tick], fixed, [*kept[:used], *[None] * (5 - used), *kept[used:]], fresh, spare
            ),
            "task",
            (*columns, source, incoming, arrived if turning else blank),
            (*mats[:used], base, latest, out),
            ((rows, lanes), (rows, lanes)),
            (rows, lanes),
        )
        mats[:used] = kept[:used]
        base, latest, out = kept[used:]

        previous = arrived
        if any(urgent[tick]) or any(one[0] and one[2] > 0 for one in tasks_at(tick + 1)):
            swap = [(s, s + 1) for s in range(tick & 1, count - 1, 2)]
            alone = [s for s in range(count) if all(s not in two for two in swap)]
            pairs = [(device(a, p), device(b, p)) for a, b in swap for p in range(parts)]
            pairs += [(device(s, a), device(s, b)) for s in alone for a, b in even_pairs]
            incoming = lax.ppermute(value, ("sweep", "span"), closed(pairs, range(count * parts)))
        if any(one >= 0 for one in sent[tick]):
            pairs = [
                (device(s, a), device(s, b))
                for s in range(count)
                for a, b in (odd_pairs if sent[tick][s] >= 0 and (urgent[tick][s] or not tick & 1) else even_pairs)
            ]
            arrived = lax.ppermute(cross, ("sweep", "span"), closed(pairs, range(count * parts)))
        came = [-1 if not tick or urgent[tick - 1][s] else sent[tick - 1][s] for s in range(count)]
        if any(one >= 0 for one in came):
            mats[3], mats[4], base = call(
                functools.partial(side_kernel, tick & 1, came),
                "side",
                (columns[2], columns[3], previous),
                (mats[3], mats[4], base),
                (),
                (rows, lanes),
            )
        if tick < len(late_blocks):
            mats[1 + tick], base = later_call(*late_blocks[tick], base)
    return out[None, None]


def solution(mesh):
    return jax.shard_map(
        per_device,
        mesh=mesh,
        in_specs=(
            P("sweep", "span", None, None, None),
            P("sweep", "span", None, None, None),
            P("sweep", "span", None, None, None),
            P("sweep", "span", None, None, None, None),
            P("sweep", "span", None),
            P("sweep", "span", None),
            P("sweep", "span", None),
            P("sweep", "span", None),
        ),
        out_specs=P("sweep", "span", None, None, None),
        check_vma=False,
    )
```

```python
import functools

import jax
import jax.numpy as jnp
from jax import lax
from jax.experimental import pallas as pl
from jax.experimental.pallas import tpu as pltpu
from jax.sharding import PartitionSpec as P

SUBLANES = 8
VMEM_LIMIT = 2 * 1024 * 1024
PREPARE_LIMIT = 12 * 1024 * 1024
LATERAL_START = 4
CHUNKS = 4


def task_at(tick, place, count, vectors, choose=jnp.where):
    forward = ((tick - place) & 1) == 0
    rank = choose(forward, place, count - 1 - place)
    since = tick - rank - choose(forward, 0, count)
    late = since >= 2 * count
    since = choose(late, since - 2 * count, since)
    active = (since >= 0) & (since < 2 * vectors)
    half = choose(forward, 0, 1) + choose(late, 2, 0)
    return active, choose(active, since >> 1, 0), rank, forward, half


def turns(task):
    active, _, rank, _, half = task
    return active & (rank == 0) & (half > 0)


def lateral_plan(count, vectors):
    ticks = 4 * count + 2 * (vectors - 1)
    sent = [[None] * count for _ in range(ticks)]
    urgent = [[False] * count for _ in range(ticks)]
    for slab in range(count):
        left = ([], [])
        for half in range(3):
            rank = count - 1 - slab if half & 1 else slab
            for vector in range(vectors):
                made = 2 * vector + half * count + rank
                used = 2 * vector + (half + 1) * count + count - 1 - rank
                if used == made + 1:
                    sent[made][slab] = (1, (vector,))
                    urgent[made][slab] = True
                    continue
                left[1].append((used, made, vector))
                if used == made + 3:
                    sent[made + 1][slab] = (0, (vector,))
                else:
                    left[0].append((used, made, vector))
        for tick in range(LATERAL_START, ticks, 2):
            ready = [sorted(one for one in waiting if one[1] <= tick)[:2] for waiting in left]
            if not any(ready):
                continue
            pairs = 0 if ready[0] and (not ready[1] or ready[0][0][0] <= ready[1][0][0]) else 1
            assert tick <= ready[pairs][0][0] - 2
            sent[tick][slab] = (pairs, tuple(one[2] for one in ready[pairs]))
            for one in ready[pairs]:
                left[pairs].remove(one)
        assert not any(left)
    return sent, urgent


def numbers(plan, entry):
    if entry < 0:
        return [-1 if one is None else one[0] for one in plan]
    return [-1 if one is None or len(one[1]) <= entry else one[1][entry] for one in plan]


def pick(values, place):
    result = jnp.int32(values[0])
    for at, value in enumerate(values):
        if value != values[0]:
            result = jnp.where(place == at, value, result)
    return result


def product(matrix, vector, rows, unroll=20):
    def body(step, total):
        for inner in range(unroll):
            j = step * unroll + inner
            total = total + matrix[j] * vector[pl.ds(j, 1), :]
        return total

    start = jnp.zeros((rows, matrix.shape[2]), jnp.float32)
    return lax.fori_loop(0, matrix.shape[0] // unroll, body, start)


def gathered(value, columns):
    index = jnp.broadcast_to(columns, value.shape)
    return jnp.take_along_axis(value, index, axis=1, mode="promise_in_bounds")


def take_lateral(base, vector, left, right, left_cols, right_cols, arrived, spare, pairs):
    rows = spare.shape[0]
    part = lax.axis_index("span")
    on_right = (part & 1) == pairs

    @pl.when(on_right & (part < lax.axis_size("span") - 1))
    def _():
        spare[...] = gathered(arrived, right_cols[...])
        base[vector] = base[vector] - product(right, spare, rows)

    @pl.when((on_right ^ True) & (part > 0))
    def _():
        spare[...] = gathered(arrived, left_cols[...])
        base[vector] = base[vector] - product(left, spare, rows)


def prepare(block, ready, narrow, wide, sems):
    size, _, lanes = block.shape
    rows = ready.shape[1]
    share = size // CHUNKS
    copies = [
        pltpu.make_async_copy(block.at[pl.ds(n * share, share)], narrow.at[pl.ds(n * share, share)], sems.at[n])
        for n in range(CHUNKS)
    ]
    for copy in copies:
        copy.start()
    wide[pl.ds(size * rows, (rows - size) * rows), :] = jnp.zeros(((rows - size) * rows, lanes), jnp.float32)

    def widen(i, _):
        wide[pl.ds(pl.multiple_of(i * rows, SUBLANES), size), :] = narrow[i].astype(jnp.float32)
        return 0

    for n, copy in enumerate(copies):
        copy.wait()
        lax.fori_loop(n * share, (n + 1) * share, widen, 0, unroll=5)

    def turn(j, _):
        for i in range(0, rows, SUBLANES):
            ready[j, pl.ds(i, SUBLANES), :] = wide[pl.ds(i * rows + j, SUBLANES, stride=rows), :]
        return 0

    lax.fori_loop(0, size, turn, 0, unroll=4)


def first_kernel(block, residual, *refs):
    hbm_columns, (ready, base, source, blank, *columns), (narrow, wide, sems, column_sems) = (
        refs[:4], refs[4:12], refs[12:]
    )
    copies = [
        pltpu.make_async_copy(there, here, column_sems.at[n])
        for n, (there, here) in enumerate(zip(hbm_columns, columns))
    ]
    for copy in copies:
        copy.start()
    prepare(block, ready, narrow, wide, sems)
    vectors, size, lanes = residual.shape
    rows = base.shape[1]
    base[:, pl.ds(rows - SUBLANES, SUBLANES), :] = jnp.zeros((vectors, SUBLANES, lanes), jnp.float32)
    base[:, pl.ds(0, size), :] = residual[...]
    source[...] = base[...]
    blank[...] = jnp.zeros_like(blank)
    for copy in copies:
        copy.wait()


def later_kernel(face, block, base_in, ready, base, narrow, wide, sems):
    prepare(block.at[(0,) * (len(block.shape) - 4) + (face,)], ready, narrow, wide, sems)


def task_kernel(
    tick, tasks, sent, columns_and_inputs, kept, values, spare
):
    up_cols, down_cols, left_cols, right_cols, source, incoming, arrived = columns_and_inputs
    value, *cross = values
    diag, up, down, left, right, base, latest, out = kept
    rows = spare.shape[0]
    vectors, size, _ = out.shape
    place = lax.axis_index("sweep")
    task = task_at(tick, place, lax.axis_size("sweep"), vectors)
    active, vector, rank, forward, half = task

    if any(turns(one) for one in tasks):

        @pl.when(turns(task))
        def _():
            take_lateral(base, vector, left, right, left_cols, right_cols, incoming[...], spare, 0)
            take_lateral(base, vector, left, right, left_cols, right_cols, arrived[0], spare, 1)

    @pl.when(active)
    def _():
        known = base[vector]
        value[...] = known
        base[vector] = source[vector]

        def take_chain(matrix, columns):
            spare[...] = gathered(incoming[...], columns[...])
            term = product(matrix, spare, rows)
            value[...] = known - term
            base[vector] = source[vector] - term

        if any(one[0] and one[2] > 0 and one[3] for one in tasks):

            @pl.when((rank > 0) & forward)
            def _():
                take_chain(up, up_cols)

        if any(one[0] and one[2] > 0 and not one[3] for one in tasks):

            @pl.when((rank > 0) & (forward ^ True))
            def _():
                take_chain(down, down_cols)

        spare[...] = value[...]
        fresh = product(diag, spare, rows)
        value[...] = fresh
        latest[vector] = fresh

        if any(one[0] and one[4] == 3 for one in tasks):

            @pl.when(half == 3)
            def _():
                out[vector] = fresh[:size]

    if cross:
        fill(cross[0], latest, sent, place)


def fill(cross, latest, plan, place):
    for entry in range(cross.shape[0]):
        chosen = numbers(plan, entry)
        if any(one >= 0 for one in chosen):
            vector = pick(chosen, place)

            @pl.when(vector >= 0)
            def _():
                cross[entry] = latest[vector]


def side_kernel(came, plan, columns_and_inputs, kept, values, spare):
    left_cols, right_cols, *arrived = columns_and_inputs
    left, right, base, latest = kept
    place = lax.axis_index("sweep")
    if values:
        fill(values[0], latest, plan, place)
    if arrived:
        pairs = pick(numbers(came, -1), place)
        for entry in range(arrived[0].shape[0]):
            chosen = numbers(came, entry)
            if any(one >= 0 for one in chosen):
                vector = pick(chosen, place)

                @pl.when(vector >= 0)
                def _():
                    take_lateral(
                        base, vector, left, right, left_cols, right_cols, arrived[0][entry], spare, pairs
                    )


def in_vmem(count):
    return [pl.BlockSpec(memory_space=pltpu.VMEM)] * count


def far(array):
    return pltpu.with_memory_space_constraint(array, pltpu.HBM)


def held(shape):
    return pltpu.VMEM(shape, jnp.float32)


def call(kernel, name, fixed, kept, fresh, spare):
    def body(*refs):
        inputs, outputs = refs[: len(fixed)], refs[len(fixed) + len(kept) : -1]
        kernel(inputs, outputs[: len(kept)], outputs[len(kept) :], refs[-1])

    return pl.pallas_call(
        body,
        out_shape=tuple(held(shape) for shape in [*(a.shape for a in kept), *fresh]),
        in_specs=in_vmem(len(fixed) + len(kept)),
        out_specs=tuple(in_vmem(len(fresh) + len(kept))),
        scratch_shapes=[held(spare)],
        input_output_aliases={len(fixed) + n: n for n in range(len(kept))},
        compiler_params=pltpu.CompilerParams(vmem_limit_bytes=VMEM_LIMIT),
        name=name,
    )(*fixed, *kept)


def preparing(size, rows, lanes):
    return [
        pltpu.VMEM((size, size, lanes), jnp.bfloat16),
        held((rows * rows, lanes)),
        pltpu.SemaphoreType.DMA((CHUNKS,)),
    ]


def first_call(block, residual, columns, rows):
    vectors, size, lanes = residual.shape
    several = (vectors, rows, lanes)
    in_hbm = pl.BlockSpec(memory_space=pltpu.HBM)
    return pl.pallas_call(
        first_kernel,
        out_shape=(
            held((size, rows, lanes)), held(several), held(several), held((rows, lanes)),
            *(pltpu.VMEM(one.shape, one.dtype) for one in columns),
        ),
        in_specs=[in_hbm, *in_vmem(1), *[in_hbm] * 4],
        out_specs=tuple(in_vmem(8)),
        scratch_shapes=[*preparing(size, rows, lanes), pltpu.SemaphoreType.DMA((4,))],
        compiler_params=pltpu.CompilerParams(vmem_limit_bytes=PREPARE_LIMIT),
        name="first",
    )(far(block), residual, *(far(one) for one in columns))


def later_call(block, face, base):
    size, _, lanes = block.shape[-3:]
    rows = base.shape[1]
    return pl.pallas_call(
        functools.partial(later_kernel, face),
        out_shape=(held((size, rows, lanes)), held(base.shape)),
        in_specs=[pl.BlockSpec(memory_space=pltpu.HBM), *in_vmem(1)],
        out_specs=tuple(in_vmem(2)),
        scratch_shapes=preparing(size, rows, lanes),
        input_output_aliases={1: 1},
        compiler_params=pltpu.CompilerParams(vmem_limit_bytes=PREPARE_LIMIT),
        name="later",
    )(far(block), base)


def per_device(
    residual_in, diag_inverse, up_block, side_blocks, up_cols, down_cols, left_cols, right_cols
):
    vectors, size, lanes = residual_in.shape[2:]
    rows = size + -size % SUBLANES
    columns = [one.reshape(1, lanes) for one in (up_cols, down_cols, left_cols, right_cols)]
    count = lax.axis_size("sweep")
    parts = lax.axis_size("span")
    ticks = 4 * count + 2 * (vectors - 1)
    sent, urgent = lateral_plan(count, vectors)
    even_pairs = [(p, p + 1) for p in range(0, parts - 1, 2)]
    odd_pairs = [(p, p + 1) for p in range(1, parts - 1, 2)]

    def closed(pairs, members):
        alone = [one for one in members if all(one not in two for two in pairs)]
        return [*pairs, *((b, a) for a, b in pairs), *((one, one) for one in alone)]

    def device(slab, part):
        return slab * parts + part

    diag, base, source, blank, *columns = first_call(diag_inverse[0, 0], residual_in[0, 0], columns, rows)
    latest, out = pl.pallas_call(
        lambda *refs: None,
        out_shape=(held((vectors, rows, lanes)), held((vectors, size, lanes))),
        out_specs=tuple(in_vmem(2)),
        name="room",
    )()
    incoming = arrived = blank
    late_blocks = [(up_block, 0), *((side_blocks, face) for face in range(3))]
    mats = [diag, blank, blank, blank, blank]

    def tasks_at(tick):
        return [task_at(tick, place, count, vectors, lambda which, a, b: a if which else b) for place in range(count)]

    for tick in range(ticks):
        tasks = tasks_at(tick)
        plan = sent[tick]
        used = 1 + sum(mat is not blank for mat in mats[1:])
        turning = any(turns(one) for one in tasks)
        at_once = any(plan) and tick & 1 == 1
        results = call(
            lambda fixed, kept, fresh, spare, used=used, tick=tick, tasks=tasks: task_kernel(
                tick, tasks, sent[tick], fixed, [*kept[:used], *[None] * (5 - used), *kept[used:]], fresh, spare
            ),
            "task",
            (*columns, source, incoming, arrived if turning else blank),
            (*mats[:used], base, latest, out),
            ((rows, lanes), *([(1, rows, lanes)] if at_once else [])),
            (rows, lanes),
        )
        mats[:used] = results[:used]
        base, latest, out, value, *cross = results[used:]

        if any(urgent[tick]) or any(one[0] and one[2] > 0 for one in tasks_at(tick + 1)):
            swap = [(s, s + 1) for s in range(tick & 1, count - 1, 2)]
            alone = [s for s in range(count) if all(s not in two for two in swap)]
            pairs = [(device(a, p), device(b, p)) for a, b in swap for p in range(parts)]
            pairs += [(device(s, a), device(s, b)) for s in alone for a, b in even_pairs]
            incoming = lax.ppermute(value, ("sweep", "span"), closed(pairs, range(count * parts)))
        came = [None if not tick or urgent[tick - 1][s] else sent[tick - 1][s] for s in range(count)]
        later = any(plan) and not at_once
        if any(came) or later:
            mats[3], mats[4], base, latest, *made = call(
                functools.partial(side_kernel, came, plan),
                "side",
                (columns[2], columns[3], *([arrived] if any(came) else [])),
                (mats[3], mats[4], base, latest),
                ((2, rows, lanes),) if later else (),
                (rows, lanes),
            )
            cross += made
        if any(plan):
            pairs = [
                (device(s, a), device(s, b))
                for s in range(count)
                if plan[s] is not None
                for a, b in (odd_pairs if plan[s][0] else even_pairs)
            ]
            arrived = lax.ppermute(cross[0], ("sweep", "span"), closed(pairs, range(count * parts)))
        if tick < len(late_blocks):
            mats[1 + tick], base = later_call(*late_blocks[tick], base)
    return out[None, None]


def solution(mesh):
    return jax.shard_map(
        per_device,
        mesh=mesh,
        in_specs=(
            P("sweep", "span", None, None, None),
            P("sweep", "span", None, None, None),
            P("sweep", "span", None, None, None),
            P("sweep", "span", None, None, None, None),
            P("sweep", "span", None),
            P("sweep", "span", None),
            P("sweep", "span", None),
            P("sweep", "span", None),
        ),
        out_specs=P("sweep", "span", None, None, None),
        check_vma=False,
    )
```

```python
import functools

import jax
import jax.numpy as jnp
from jax import lax
from jax.experimental import pallas as pl
from jax.experimental.pallas import tpu as pltpu
from jax.sharding import PartitionSpec as P

SUBLANES = 8
VMEM_LIMIT = 2 * 1024 * 1024
PREPARE_LIMIT = 12 * 1024 * 1024
LATERAL_START = 4
CHUNKS = 4


def task_at(tick, place, count, vectors, choose=jnp.where):
    forward = ((tick - place) & 1) == 0
    rank = choose(forward, place, count - 1 - place)
    since = tick - rank - choose(forward, 0, count)
    late = since >= 2 * count
    since = choose(late, since - 2 * count, since)
    active = (since >= 0) & (since < 2 * vectors)
    half = choose(forward, 0, 1) + choose(late, 2, 0)
    return active, choose(active, since >> 1, 0), rank, forward, half


def turns(task):
    active, _, rank, _, half = task
    return active & (rank == 0) & (half > 0)


def lateral_plan(count, vectors):
    ticks = 4 * count + 2 * (vectors - 1)
    sent = [[None] * count for _ in range(ticks)]
    urgent = [[False] * count for _ in range(ticks)]
    for slab in range(count):
        left = ([], [])
        for half in range(3):
            rank = count - 1 - slab if half & 1 else slab
            for vector in range(vectors):
                made = 2 * vector + half * count + rank
                used = 2 * vector + (half + 1) * count + count - 1 - rank
                if used == made + 1:
                    sent[made][slab] = (1, (vector,))
                    urgent[made][slab] = True
                    continue
                left[1].append((used, made, vector))
                if used == made + 3:
                    sent[made + 1][slab] = (0, (vector,))
                else:
                    left[0].append((used, made, vector))
        for tick in range(LATERAL_START, ticks, 2):
            ready = [sorted(one for one in waiting if one[1] <= tick)[:2] for waiting in left]
            if not any(ready):
                continue
            pairs = 0 if ready[0] and (not ready[1] or ready[0][0][0] <= ready[1][0][0]) else 1
            assert tick <= ready[pairs][0][0] - 2
            sent[tick][slab] = (pairs, tuple(one[2] for one in ready[pairs]))
            for one in ready[pairs]:
                left[pairs].remove(one)
        assert not any(left)
    return sent, urgent


def numbers(plan, entry):
    if entry < 0:
        return [-1 if one is None else one[0] for one in plan]
    return [-1 if one is None or len(one[1]) <= entry else one[1][entry] for one in plan]


def pick(values, place):
    result = jnp.int32(values[0])
    for at, value in enumerate(values):
        if value != values[0]:
            result = jnp.where(place == at, value, result)
    return result


def product(matrix, vector, rows, unroll=20):
    def body(step, total):
        for inner in range(unroll):
            j = step * unroll + inner
            total = total + matrix[j] * vector[pl.ds(j, 1), :]
        return total

    start = jnp.zeros((rows, matrix.shape[2]), jnp.float32)
    return lax.fori_loop(0, matrix.shape[0] // unroll, body, start)


def gathered(value, columns):
    index = jnp.broadcast_to(columns, value.shape)
    return jnp.take_along_axis(value, index, axis=1, mode="promise_in_bounds")


def take_lateral(base, vector, left, right, left_cols, right_cols, arrived, spare, pairs):
    rows = spare.shape[0]
    part = lax.axis_index("span")
    on_right = (part & 1) == pairs

    @pl.when(on_right & (part < lax.axis_size("span") - 1))
    def _():
        spare[...] = gathered(arrived, right_cols[...])
        base[vector] = base[vector] - product(right, spare, rows)

    @pl.when((on_right ^ True) & (part > 0))
    def _():
        spare[...] = gathered(arrived, left_cols[...])
        base[vector] = base[vector] - product(left, spare, rows)


def prepare(block, ready, narrow, wide, sems):
    size, _, lanes = block.shape
    rows = ready.shape[1]
    share = size // CHUNKS
    copies = [
        pltpu.make_async_copy(block.at[pl.ds(n * share, share)], narrow.at[pl.ds(n * share, share)], sems.at[n])
        for n in range(CHUNKS)
    ]
    for copy in copies:
        copy.start()
    wide[pl.ds(size * rows, (rows - size) * rows), :] = jnp.zeros(((rows - size) * rows, lanes), jnp.float32)

    def widen(i, _):
        wide[pl.ds(pl.multiple_of(i * rows, SUBLANES), size), :] = narrow[i].astype(jnp.float32)
        return 0

    for n, copy in enumerate(copies):
        copy.wait()
        lax.fori_loop(n * share, (n + 1) * share, widen, 0, unroll=5)

    def turn(j, _):
        for i in range(0, rows, SUBLANES):
            ready[j, pl.ds(i, SUBLANES), :] = wide[pl.ds(i * rows + j, SUBLANES, stride=rows), :]
        return 0

    lax.fori_loop(0, size, turn, 0, unroll=4)


def first_kernel(block, residual, *refs):
    hbm_columns, (ready, base, source, blank, *columns), (narrow, wide, sems, column_sems) = (
        refs[:4], refs[4:12], refs[12:]
    )
    copies = [
        pltpu.make_async_copy(there, here, column_sems.at[n])
        for n, (there, here) in enumerate(zip(hbm_columns, columns))
    ]
    for copy in copies:
        copy.start()
    prepare(block, ready, narrow, wide, sems)
    vectors, size, lanes = residual.shape
    rows = base.shape[1]
    base[:, pl.ds(rows - SUBLANES, SUBLANES), :] = jnp.zeros((vectors, SUBLANES, lanes), jnp.float32)
    base[:, pl.ds(0, size), :] = residual[...]
    source[...] = base[...]
    blank[...] = jnp.zeros_like(blank)
    for copy in copies:
        copy.wait()


def later_kernel(face, block, base_in, ready, base, narrow, wide, sems):
    prepare(block.at[(0,) * (len(block.shape) - 4) + (face,)], ready, narrow, wide, sems)


def task_kernel(
    tick, tasks, sent, columns_and_inputs, kept, values, spare
):
    up_cols, down_cols, left_cols, right_cols, source, incoming, arrived = columns_and_inputs
    value, *cross = values
    diag, up, down, left, right, base, latest, out = kept
    rows = spare.shape[0]
    vectors, size, _ = out.shape
    place = lax.axis_index("sweep")
    task = task_at(tick, place, lax.axis_size("sweep"), vectors)
    active, vector, rank, forward, half = task

    if any(turns(one) for one in tasks):

        @pl.when(turns(task))
        def _():
            take_lateral(base, vector, left, right, left_cols, right_cols, incoming[...], spare, 0)
            take_lateral(base, vector, left, right, left_cols, right_cols, arrived[0], spare, 1)

    @pl.when(active)
    def _():
        known = base[vector]
        value[...] = known
        base[vector] = source[vector]

        def take_chain(matrix, columns):
            spare[...] = gathered(incoming[...], columns[...])
            term = product(matrix, spare, rows)
            value[...] = known - term
            base[vector] = source[vector] - term

        if any(one[0] and one[2] > 0 and one[3] for one in tasks):

            @pl.when((rank > 0) & forward)
            def _():
                take_chain(up, up_cols)

        if any(one[0] and one[2] > 0 and not one[3] for one in tasks):

            @pl.when((rank > 0) & (forward ^ True))
            def _():
                take_chain(down, down_cols)

        spare[...] = value[...]
        fresh = product(diag, spare, rows)
        value[...] = fresh
        latest[vector] = fresh

        if any(one[0] and one[4] == 3 for one in tasks):

            @pl.when(half == 3)
            def _():
                out[vector] = fresh[:size]

    if cross:
        fill(cross[0], latest, sent, place)


def fill(cross, latest, plan, place):
    for entry in range(cross.shape[0]):
        chosen = numbers(plan, entry)
        if any(one >= 0 for one in chosen):
            vector = pick(chosen, place)

            @pl.when(vector >= 0)
            def _():
                cross[entry] = latest[vector]


def side_kernel(came, plan, columns_and_inputs, kept, values, spare):
    left_cols, right_cols, *arrived = columns_and_inputs
    left, right, base, latest = kept
    place = lax.axis_index("sweep")
    if values:
        fill(values[0], latest, plan, place)
    if arrived:
        pairs = pick(numbers(came, -1), place)
        for entry in range(arrived[0].shape[0]):
            chosen = numbers(came, entry)
            if any(one >= 0 for one in chosen):
                vector = pick(chosen, place)

                @pl.when(vector >= 0)
                def _():
                    take_lateral(
                        base, vector, left, right, left_cols, right_cols, arrived[0][entry], spare, pairs
                    )


def in_vmem(count):
    return [pl.BlockSpec(memory_space=pltpu.VMEM)] * count


def far(array):
    return pltpu.with_memory_space_constraint(array, pltpu.HBM)


def held(shape):
    return pltpu.VMEM(shape, jnp.float32)


def call(kernel, name, fixed, kept, fresh, spare):
    def body(*refs):
        inputs, outputs = refs[: len(fixed)], refs[len(fixed) + len(kept) : -1]
        kernel(inputs, outputs[: len(kept)], outputs[len(kept) :], refs[-1])

    return pl.pallas_call(
        body,
        out_shape=tuple(held(shape) for shape in [*(a.shape for a in kept), *fresh]),
        in_specs=in_vmem(len(fixed) + len(kept)),
        out_specs=tuple(in_vmem(len(fresh) + len(kept))),
        scratch_shapes=[held(spare)],
        input_output_aliases={len(fixed) + n: n for n in range(len(kept))},
        compiler_params=pltpu.CompilerParams(vmem_limit_bytes=VMEM_LIMIT),
        name=name,
    )(*fixed, *kept)


def preparing(size, rows, lanes):
    return [
        pltpu.VMEM((size, size, lanes), jnp.bfloat16),
        held((rows * rows, lanes)),
        pltpu.SemaphoreType.DMA((CHUNKS,)),
    ]


def first_call(block, residual, columns, rows):
    vectors, size, lanes = residual.shape
    several = (vectors, rows, lanes)
    in_hbm = pl.BlockSpec(memory_space=pltpu.HBM)
    return pl.pallas_call(
        first_kernel,
        out_shape=(
            held((size, rows, lanes)), held(several), held(several), held((rows, lanes)),
            *(pltpu.VMEM(one.shape, one.dtype) for one in columns),
        ),
        in_specs=[in_hbm, *in_vmem(1), *[in_hbm] * 4],
        out_specs=tuple(in_vmem(8)),
        scratch_shapes=[*preparing(size, rows, lanes), pltpu.SemaphoreType.DMA((4,))],
        compiler_params=pltpu.CompilerParams(vmem_limit_bytes=PREPARE_LIMIT),
        name="first",
    )(far(block), residual, *(far(one) for one in columns))


def later_call(block, face, base):
    size, _, lanes = block.shape[-3:]
    rows = base.shape[1]
    return pl.pallas_call(
        functools.partial(later_kernel, face),
        out_shape=(held((size, rows, lanes)), held(base.shape)),
        in_specs=[pl.BlockSpec(memory_space=pltpu.HBM), *in_vmem(1)],
        out_specs=tuple(in_vmem(2)),
        scratch_shapes=preparing(size, rows, lanes),
        input_output_aliases={1: 1},
        compiler_params=pltpu.CompilerParams(vmem_limit_bytes=PREPARE_LIMIT),
        name="later",
    )(far(block), base)


def per_device(
    residual_in, diag_inverse, up_block, side_blocks, up_cols, down_cols, left_cols, right_cols
):
    vectors, size, lanes = residual_in.shape[2:]
    rows = size + -size % SUBLANES
    columns = [one.reshape(1, lanes) for one in (up_cols, down_cols, left_cols, right_cols)]
    count = lax.axis_size("sweep")
    parts = lax.axis_size("span")
    ticks = 4 * count + 2 * (vectors - 1)
    sent, urgent = lateral_plan(count, vectors)
    even_pairs = [(p, p + 1) for p in range(0, parts - 1, 2)]
    odd_pairs = [(p, p + 1) for p in range(1, parts - 1, 2)]

    def closed(pairs, members):
        alone = [one for one in members if all(one not in two for two in pairs)]
        return [*pairs, *((b, a) for a, b in pairs), *((one, one) for one in alone)]

    def device(slab, part):
        return slab * parts + part

    diag, base, source, blank, *columns = first_call(diag_inverse[0, 0], residual_in[0, 0], columns, rows)
    latest, out = pl.pallas_call(
        lambda *refs: None,
        out_shape=(held((vectors, rows, lanes)), held((vectors, size, lanes))),
        out_specs=tuple(in_vmem(2)),
        name="room",
    )()
    incoming = arrived = blank
    late_blocks = [(up_block, 0), *((side_blocks, face) for face in range(3))]
    mats = [diag, blank, blank, blank, blank]

    def tasks_at(tick):
        return [task_at(tick, place, count, vectors, lambda which, a, b: a if which else b) for place in range(count)]

    for tick in range(ticks):
        tasks = tasks_at(tick)
        plan = sent[tick]
        used = 1 + sum(mat is not blank for mat in mats[1:])
        turning = any(turns(one) for one in tasks)
        at_once = any(plan) and tick & 1 == 1
        results = call(
            lambda fixed, kept, fresh, spare, used=used, tick=tick, tasks=tasks: task_kernel(
                tick, tasks, sent[tick], fixed, [*kept[:used], *[None] * (5 - used), *kept[used:]], fresh, spare
            ),
            "task",
            (*columns, source, incoming, arrived if turning else blank),
            (*mats[:used], base, latest, out),
            ((rows, lanes), *([(1, rows, lanes)] if at_once else [])),
            (rows, lanes),
        )
        mats[:used] = results[:used]
        base, latest, out, value, *cross = results[used:]

        if any(urgent[tick]) or any(one[0] and one[2] > 0 for one in tasks_at(tick + 1)):
            pairs = [
                (device(s, p), device(s + 1 if one[3] else s - 1, p))
                for s, one in enumerate(tasks)
                if one[0] and one[2] < count - 1
                for p in range(parts)
            ]
            pairs += [
                (device(s, x), device(s, y)) for s in range(count) if urgent[tick][s] for a, b in even_pairs for x, y in ((a, b), (b, a))
            ]
            incoming = lax.ppermute(value, ("sweep", "span"), pairs)
        came = [None if not tick or urgent[tick - 1][s] else sent[tick - 1][s] for s in range(count)]
        later = any(plan) and not at_once
        if any(came) or later:
            mats[3], mats[4], base, latest, *made = call(
                functools.partial(side_kernel, came, plan),
                "side",
                (columns[2], columns[3], *([arrived] if any(came) else [])),
                (mats[3], mats[4], base, latest),
                ((2, rows, lanes),) if later else (),
                (rows, lanes),
            )
            cross += made
        if any(plan):
            pairs = [
                (device(s, a), device(s, b))
                for s in range(count)
                if plan[s] is not None
                for a, b in (odd_pairs if plan[s][0] else even_pairs)
            ]
            arrived = lax.ppermute(cross[0], ("sweep", "span"), closed(pairs, range(count * parts)))
        if tick < len(late_blocks):
            mats[1 + tick], base = later_call(*late_blocks[tick], base)
    return out[None, None]


def solution(mesh):
    return jax.shard_map(
        per_device,
        mesh=mesh,
        in_specs=(
            P("sweep", "span", None, None, None),
            P("sweep", "span", None, None, None),
            P("sweep", "span", None, None, None),
            P("sweep", "span", None, None, None, None),
            P("sweep", "span", None),
            P("sweep", "span", None),
            P("sweep", "span", None),
            P("sweep", "span", None),
        ),
        out_specs=P("sweep", "span", None, None, None),
        check_vma=False,
    )
```

```python
import functools

import jax
import jax.numpy as jnp
from jax import lax
from jax.experimental import pallas as pl
from jax.experimental.pallas import tpu as pltpu
from jax.sharding import PartitionSpec as P

SUBLANES = 8
VMEM_LIMIT = 2 * 1024 * 1024
PREPARE_LIMIT = 12 * 1024 * 1024
LATERAL_START = 4
CHUNKS = 4


def task_at(tick, place, count, vectors, choose=jnp.where):
    forward = ((tick - place) & 1) == 0
    rank = choose(forward, place, count - 1 - place)
    since = tick - rank - choose(forward, 0, count)
    late = since >= 2 * count
    since = choose(late, since - 2 * count, since)
    active = (since >= 0) & (since < 2 * vectors)
    half = choose(forward, 0, 1) + choose(late, 2, 0)
    return active, choose(active, since >> 1, 0), rank, forward, half


def turns(task):
    active, _, rank, _, half = task
    return active & (rank == 0) & (half > 0)


def lateral_plan(count, vectors):
    ticks = 4 * count + 2 * (vectors - 1)
    sent = [[None] * count for _ in range(ticks)]
    urgent = [[False] * count for _ in range(ticks)]
    for slab in range(count):
        left = ([], [])
        for half in range(3):
            rank = count - 1 - slab if half & 1 else slab
            for vector in range(vectors):
                made = 2 * vector + half * count + rank
                used = 2 * vector + (half + 1) * count + count - 1 - rank
                if used == made + 1:
                    sent[made][slab] = (1, (vector,))
                    urgent[made][slab] = True
                    continue
                left[1].append((used, made, vector))
                if used == made + 3:
                    sent[made + 1][slab] = (0, (vector,))
                else:
                    left[0].append((used, made, vector))
        for tick in range(LATERAL_START, ticks, 2):
            ready = [sorted(one for one in waiting if one[1] <= tick)[:2] for waiting in left]
            if not any(ready):
                continue
            pairs = 0 if ready[0] and (not ready[1] or ready[0][0][0] <= ready[1][0][0]) else 1
            assert tick <= ready[pairs][0][0] - 2
            sent[tick][slab] = (pairs, tuple(one[2] for one in ready[pairs]))
            for one in ready[pairs]:
                left[pairs].remove(one)
        assert not any(left)
    return sent, urgent


def numbers(plan, entry):
    if entry < 0:
        return [-1 if one is None else one[0] for one in plan]
    return [-1 if one is None or len(one[1]) <= entry else one[1][entry] for one in plan]


def pick(values, place):
    result = jnp.int32(values[0])
    for at, value in enumerate(values):
        if value != values[0]:
            result = jnp.where(place == at, value, result)
    return result


def product(matrix, vector, rows, unroll=25):
    def body(step, total):
        for inner in range(unroll):
            j = step * unroll + inner
            total = total + matrix[j] * vector[pl.ds(j, 1), :]
        return total

    start = jnp.zeros((rows, matrix.shape[2]), jnp.float32)
    return lax.fori_loop(0, matrix.shape[0] // unroll, body, start)


def gathered(value, columns):
    index = jnp.broadcast_to(columns, value.shape)
    return jnp.take_along_axis(value, index, axis=1, mode="promise_in_bounds")


def take_lateral(base, vector, left, right, left_cols, right_cols, arrived, spare, pairs):
    rows = spare.shape[0]
    part = lax.axis_index("span")
    on_right = (part & 1) == pairs

    @pl.when(on_right & (part < lax.axis_size("span") - 1))
    def _():
        spare[...] = gathered(arrived, right_cols[...])
        base[vector] = base[vector] - product(right, spare, rows)

    @pl.when((on_right ^ True) & (part > 0))
    def _():
        spare[...] = gathered(arrived, left_cols[...])
        base[vector] = base[vector] - product(left, spare, rows)


def prepare(block, ready, narrow, wide, sems):
    size, _, lanes = block.shape
    rows = ready.shape[1]
    share = size // CHUNKS
    copies = [
        pltpu.make_async_copy(block.at[pl.ds(n * share, share)], narrow.at[pl.ds(n * share, share)], sems.at[n])
        for n in range(CHUNKS)
    ]
    for copy in copies:
        copy.start()
    wide[pl.ds(size * rows, (rows - size) * rows), :] = jnp.zeros(((rows - size) * rows, lanes), jnp.float32)

    def widen(i, _):
        wide[pl.ds(pl.multiple_of(i * rows, SUBLANES), size), :] = narrow[i].astype(jnp.float32)
        return 0

    for n, copy in enumerate(copies):
        copy.wait()
        lax.fori_loop(n * share, (n + 1) * share, widen, 0, unroll=5)

    def turn(j, _):
        for i in range(0, rows, SUBLANES):
            ready[j, pl.ds(i, SUBLANES), :] = wide[pl.ds(i * rows + j, SUBLANES, stride=rows), :]
        return 0

    lax.fori_loop(0, size, turn, 0, unroll=4)


def first_kernel(block, residual, *refs):
    hbm_columns, (ready, base, source, blank, *columns), (narrow, wide, sems, column_sems) = (
        refs[:4], refs[4:12], refs[12:]
    )
    copies = [
        pltpu.make_async_copy(there, here, column_sems.at[n])
        for n, (there, here) in enumerate(zip(hbm_columns, columns))
    ]
    for copy in copies:
        copy.start()
    prepare(block, ready, narrow, wide, sems)
    vectors, size, lanes = residual.shape
    rows = base.shape[1]
    base[:, pl.ds(rows - SUBLANES, SUBLANES), :] = jnp.zeros((vectors, SUBLANES, lanes), jnp.float32)
    base[:, pl.ds(0, size), :] = residual[...]
    source[...] = base[...]
    blank[...] = jnp.zeros_like(blank)
    for copy in copies:
        copy.wait()


def later_kernel(face, block, base_in, ready, base, narrow, wide, sems):
    prepare(block.at[(0,) * (len(block.shape) - 4) + (face,)], ready, narrow, wide, sems)


def task_kernel(
    tick, tasks, sent, columns_and_inputs, kept, values, spare
):
    up_cols, down_cols, left_cols, right_cols, source, incoming, arrived = columns_and_inputs
    value, *cross = values
    diag, up, down, left, right, base, latest, out = kept
    rows = spare.shape[0]
    vectors, size, _ = out.shape
    place = lax.axis_index("sweep")
    task = task_at(tick, place, lax.axis_size("sweep"), vectors)
    active, vector, rank, forward, half = task

    if any(turns(one) for one in tasks):

        @pl.when(turns(task))
        def _():
            take_lateral(base, vector, left, right, left_cols, right_cols, incoming[...], spare, 0)
            take_lateral(base, vector, left, right, left_cols, right_cols, arrived[0], spare, 1)

    @pl.when(active)
    def _():
        known = base[vector]
        value[...] = known
        base[vector] = source[vector]

        def take_chain(matrix, columns):
            spare[...] = gathered(incoming[...], columns[...])
            term = product(matrix, spare, rows)
            value[...] = known - term
            base[vector] = source[vector] - term

        if any(one[0] and one[2] > 0 and one[3] for one in tasks):

            @pl.when((rank > 0) & forward)
            def _():
                take_chain(up, up_cols)

        if any(one[0] and one[2] > 0 and not one[3] for one in tasks):

            @pl.when((rank > 0) & (forward ^ True))
            def _():
                take_chain(down, down_cols)

        spare[...] = value[...]
        fresh = product(diag, spare, rows)
        value[...] = fresh
        latest[vector] = fresh

        if any(one[0] and one[4] == 3 for one in tasks):

            @pl.when(half == 3)
            def _():
                out[vector] = fresh[:size]

    if cross:
        fill(cross[0], latest, sent, place)


def fill(cross, latest, plan, place):
    for entry in range(cross.shape[0]):
        chosen = numbers(plan, entry)
        if any(one >= 0 for one in chosen):
            vector = pick(chosen, place)

            @pl.when(vector >= 0)
            def _():
                cross[entry] = latest[vector]


def side_kernel(came, plan, columns_and_inputs, kept, values, spare):
    left_cols, right_cols, *arrived = columns_and_inputs
    left, right, base, latest = kept
    place = lax.axis_index("sweep")
    if values:
        fill(values[0], latest, plan, place)
    if arrived:
        pairs = pick(numbers(came, -1), place)
        for entry in range(arrived[0].shape[0]):
            chosen = numbers(came, entry)
            if any(one >= 0 for one in chosen):
                vector = pick(chosen, place)

                @pl.when(vector >= 0)
                def _():
                    take_lateral(
                        base, vector, left, right, left_cols, right_cols, arrived[0][entry], spare, pairs
                    )


def in_vmem(count):
    return [pl.BlockSpec(memory_space=pltpu.VMEM)] * count


def far(array):
    return pltpu.with_memory_space_constraint(array, pltpu.HBM)


def held(shape):
    return pltpu.VMEM(shape, jnp.float32)


def call(kernel, name, fixed, kept, fresh, spare):
    def body(*refs):
        inputs, outputs = refs[: len(fixed)], refs[len(fixed) + len(kept) : -1]
        kernel(inputs, outputs[: len(kept)], outputs[len(kept) :], refs[-1])

    return pl.pallas_call(
        body,
        out_shape=tuple(held(shape) for shape in [*(a.shape for a in kept), *fresh]),
        in_specs=in_vmem(len(fixed) + len(kept)),
        out_specs=tuple(in_vmem(len(fresh) + len(kept))),
        scratch_shapes=[held(spare)],
        input_output_aliases={len(fixed) + n: n for n in range(len(kept))},
        compiler_params=pltpu.CompilerParams(vmem_limit_bytes=VMEM_LIMIT),
        name=name,
    )(*fixed, *kept)


def preparing(size, rows, lanes):
    return [
        pltpu.VMEM((size, size, lanes), jnp.bfloat16),
        held((rows * rows, lanes)),
        pltpu.SemaphoreType.DMA((CHUNKS,)),
    ]


def first_call(block, residual, columns, rows):
    vectors, size, lanes = residual.shape
    several = (vectors, rows, lanes)
    in_hbm = pl.BlockSpec(memory_space=pltpu.HBM)
    return pl.pallas_call(
        first_kernel,
        out_shape=(
            held((size, rows, lanes)), held(several), held(several), held((rows, lanes)),
            *(pltpu.VMEM(one.shape, one.dtype) for one in columns),
        ),
        in_specs=[in_hbm, *in_vmem(1), *[in_hbm] * 4],
        out_specs=tuple(in_vmem(8)),
        scratch_shapes=[*preparing(size, rows, lanes), pltpu.SemaphoreType.DMA((4,))],
        compiler_params=pltpu.CompilerParams(vmem_limit_bytes=PREPARE_LIMIT),
        name="first",
    )(far(block), residual, *(far(one) for one in columns))


def later_call(block, face, base):
    size, _, lanes = block.shape[-3:]
    rows = base.shape[1]
    return pl.pallas_call(
        functools.partial(later_kernel, face),
        out_shape=(held((size, rows, lanes)), held(base.shape)),
        in_specs=[pl.BlockSpec(memory_space=pltpu.HBM), *in_vmem(1)],
        out_specs=tuple(in_vmem(2)),
        scratch_shapes=preparing(size, rows, lanes),
        input_output_aliases={1: 1},
        compiler_params=pltpu.CompilerParams(vmem_limit_bytes=PREPARE_LIMIT),
        name="later",
    )(far(block), base)


def per_device(
    residual_in, diag_inverse, up_block, side_blocks, up_cols, down_cols, left_cols, right_cols
):
    vectors, size, lanes = residual_in.shape[2:]
    rows = size + -size % SUBLANES
    columns = [one.reshape(1, lanes) for one in (up_cols, down_cols, left_cols, right_cols)]
    count = lax.axis_size("sweep")
    parts = lax.axis_size("span")
    ticks = 4 * count + 2 * (vectors - 1)
    sent, urgent = lateral_plan(count, vectors)
    even_pairs = [(p, p + 1) for p in range(0, parts - 1, 2)]
    odd_pairs = [(p, p + 1) for p in range(1, parts - 1, 2)]

    def closed(pairs, members):
        alone = [one for one in members if all(one not in two for two in pairs)]
        return [*pairs, *((b, a) for a, b in pairs), *((one, one) for one in alone)]

    def device(slab, part):
        return slab * parts + part

    diag, base, source, blank, *columns = first_call(diag_inverse[0, 0], residual_in[0, 0], columns, rows)
    latest, out = pl.pallas_call(
        lambda *refs: None,
        out_shape=(held((vectors, rows, lanes)), held((vectors, size, lanes))),
        out_specs=tuple(in_vmem(2)),
        name="room",
    )()
    incoming = arrived = blank
    late_blocks = [(up_block, 0), *((side_blocks, face) for face in range(3))]
    mats = [diag, blank, blank, blank, blank]

    def tasks_at(tick):
        return [task_at(tick, place, count, vectors, lambda which, a, b: a if which else b) for place in range(count)]

    for tick in range(ticks):
        tasks = tasks_at(tick)
        plan = sent[tick]
        used = 1 + sum(mat is not blank for mat in mats[1:])
        turning = any(turns(one) for one in tasks)
        at_once = any(plan) and tick & 1 == 1
        results = call(
            lambda fixed, kept, fresh, spare, used=used, tick=tick, tasks=tasks: task_kernel(
                tick, tasks, sent[tick], fixed, [*kept[:used], *[None] * (5 - used), *kept[used:]], fresh, spare
            ),
            "task",
            (*columns, source, incoming, arrived if turning else blank),
            (*mats[:used], base, latest, out),
            ((rows, lanes), *([(1, rows, lanes)] if at_once else [])),
            (rows, lanes),
        )
        mats[:used] = results[:used]
        base, latest, out, value, *cross = results[used:]

        if any(urgent[tick]) or any(one[0] and one[2] > 0 for one in tasks_at(tick + 1)):
            pairs = []
            swap = [(s, s + 1) for s in range(tick & 1, count - 1, 2)]
            for a, b in swap:
                forth, back = (0 if tasks[one][0] else 1 for one in (a, b))
                if forth and back:
                    forth = back = 0
                for p in range(parts):
                    pairs += [(device(a, p), device(b, p ^ forth)), (device(b, p), device(a, p ^ back))]
            alone = [s for s in range(count) if all(s not in two for two in swap)]
            pairs += [(device(s, x), device(s, y)) for s in alone for a, b in even_pairs for x, y in ((a, b), (b, a))]
            incoming = lax.ppermute(value, ("sweep", "span"), pairs)
        came = [None if not tick or urgent[tick - 1][s] else sent[tick - 1][s] for s in range(count)]
        later = any(plan) and not at_once
        if any(came) or later:
            mats[3], mats[4], base, latest, *made = call(
                functools.partial(side_kernel, came, plan),
                "side",
                (columns[2], columns[3], *([arrived] if any(came) else [])),
                (mats[3], mats[4], base, latest),
                ((2, rows, lanes),) if later else (),
                (rows, lanes),
            )
            cross += made
        if any(plan):
            pairs = [
                (device(s, a), device(s, b))
                for s in range(count)
                if plan[s] is not None
                for a, b in (odd_pairs if plan[s][0] else even_pairs)
            ]
            arrived = lax.ppermute(cross[0], ("sweep", "span"), closed(pairs, range(count * parts)))
        if tick < len(late_blocks):
            mats[1 + tick], base = later_call(*late_blocks[tick], base)
    return out[None, None]


def solution(mesh):
    return jax.shard_map(
        per_device,
        mesh=mesh,
        in_specs=(
            P("sweep", "span", None, None, None),
            P("sweep", "span", None, None, None),
            P("sweep", "span", None, None, None),
            P("sweep", "span", None, None, None, None),
            P("sweep", "span", None),
            P("sweep", "span", None),
            P("sweep", "span", None),
            P("sweep", "span", None),
        ),
        out_specs=P("sweep", "span", None, None, None),
        check_vma=False,
    )
```

```python
import functools

import jax
import jax.numpy as jnp
from jax import lax
from jax.experimental import pallas as pl
from jax.experimental.pallas import tpu as pltpu
from jax.sharding import PartitionSpec as P

SUBLANES = 8
VMEM_LIMIT = 2 * 1024 * 1024
PREPARE_LIMIT = 12 * 1024 * 1024
LATERAL_START = 4
CHUNKS = 4


def task_at(tick, place, count, vectors, choose=jnp.where):
    forward = ((tick - place) & 1) == 0
    rank = choose(forward, place, count - 1 - place)
    since = tick - rank - choose(forward, 0, count)
    late = since >= 2 * count
    since = choose(late, since - 2 * count, since)
    active = (since >= 0) & (since < 2 * vectors)
    half = choose(forward, 0, 1) + choose(late, 2, 0)
    return active, choose(active, since >> 1, 0), rank, forward, half


def turns(task):
    active, _, rank, _, half = task
    return active & (rank == 0) & (half > 0)


def lateral_plan(count, vectors):
    ticks = 4 * count + 2 * (vectors - 1)
    sent = [[None] * count for _ in range(ticks)]
    urgent = [[False] * count for _ in range(ticks)]
    for slab in range(count):
        left = ([], [])
        for half in range(3):
            rank = count - 1 - slab if half & 1 else slab
            for vector in range(vectors):
                made = 2 * vector + half * count + rank
                used = 2 * vector + (half + 1) * count + count - 1 - rank
                if used == made + 1:
                    sent[made][slab] = (0, (vector,))
                    urgent[made][slab] = True
                    continue
                left[1].append((used, made, vector))
                if used == made + 3:
                    sent[made + 1][slab] = (0, (vector,))
                else:
                    left[0].append((used, made, vector))
        for tick in range(LATERAL_START, ticks, 2):
            ready = [sorted(one for one in waiting if one[1] <= tick)[:2] for waiting in left]
            if not any(ready):
                continue
            pairs = 0 if ready[0] and (not ready[1] or ready[0][0][0] <= ready[1][0][0]) else 1
            assert tick <= ready[pairs][0][0] - 2
            sent[tick][slab] = (pairs, tuple(one[2] for one in ready[pairs]))
            for one in ready[pairs]:
                left[pairs].remove(one)
        assert not any(left)
    return sent, urgent


def numbers(plan, entry):
    if entry < 0:
        return [-1 if one is None else one[0] for one in plan]
    return [-1 if one is None or len(one[1]) <= entry else one[1][entry] for one in plan]


def pick(values, place):
    result = jnp.int32(values[0])
    for at, value in enumerate(values):
        if value != values[0]:
            result = jnp.where(place == at, value, result)
    return result


def product(matrix, vector, rows, unroll=25):
    def body(step, total):
        for inner in range(unroll):
            j = step * unroll + inner
            total = total + matrix[j] * vector[pl.ds(j, 1), :]
        return total

    start = jnp.zeros((rows, matrix.shape[2]), jnp.float32)
    return lax.fori_loop(0, matrix.shape[0] // unroll, body, start)


def gathered(value, columns):
    index = jnp.broadcast_to(columns, value.shape)
    return jnp.take_along_axis(value, index, axis=1, mode="promise_in_bounds")


def take_lateral(base, vector, left, right, left_cols, right_cols, arrived, spare, pairs):
    rows = spare.shape[0]
    part = lax.axis_index("span")
    on_right = (part & 1) == pairs

    @pl.when(on_right & (part < lax.axis_size("span") - 1))
    def _():
        spare[...] = gathered(arrived, right_cols[...])
        base[vector] = base[vector] - product(right, spare, rows)

    @pl.when((on_right ^ True) & (part > 0))
    def _():
        spare[...] = gathered(arrived, left_cols[...])
        base[vector] = base[vector] - product(left, spare, rows)


def prepare(block, ready, narrow, wide, sems):
    size, _, lanes = block.shape
    rows = ready.shape[1]
    share = size // CHUNKS
    copies = [
        pltpu.make_async_copy(block.at[pl.ds(n * share, share)], narrow.at[pl.ds(n * share, share)], sems.at[n])
        for n in range(CHUNKS)
    ]
    for copy in copies:
        copy.start()
    wide[pl.ds(size * rows, (rows - size) * rows), :] = jnp.zeros(((rows - size) * rows, lanes), jnp.float32)

    def widen(i, _):
        wide[pl.ds(pl.multiple_of(i * rows, SUBLANES), size), :] = narrow[i].astype(jnp.float32)
        return 0

    for n, copy in enumerate(copies):
        copy.wait()
        lax.fori_loop(n * share, (n + 1) * share, widen, 0, unroll=5)

    def turn(j, _):
        for i in range(0, rows, SUBLANES):
            ready[j, pl.ds(i, SUBLANES), :] = wide[pl.ds(i * rows + j, SUBLANES, stride=rows), :]
        return 0

    lax.fori_loop(0, size, turn, 0, unroll=4)


def first_kernel(block, residual, *refs):
    hbm_columns, (ready, base, source, blank, *columns), (narrow, wide, sems, column_sems) = (
        refs[:4], refs[4:12], refs[12:]
    )
    copies = [
        pltpu.make_async_copy(there, here, column_sems.at[n])
        for n, (there, here) in enumerate(zip(hbm_columns, columns))
    ]
    for copy in copies:
        copy.start()
    prepare(block, ready, narrow, wide, sems)
    vectors, size, lanes = residual.shape
    rows = base.shape[1]
    base[:, pl.ds(rows - SUBLANES, SUBLANES), :] = jnp.zeros((vectors, SUBLANES, lanes), jnp.float32)
    base[:, pl.ds(0, size), :] = residual[...]
    source[...] = base[...]
    blank[...] = jnp.zeros_like(blank)
    for copy in copies:
        copy.wait()


def later_kernel(face, block, base_in, ready, base, narrow, wide, sems):
    prepare(block.at[(0,) * (len(block.shape) - 4) + (face,)], ready, narrow, wide, sems)


def task_kernel(
    tick, tasks, sent, columns_and_inputs, kept, values, spare
):
    up_cols, down_cols, left_cols, right_cols, source, incoming, arrived = columns_and_inputs
    value, *cross = values
    diag, up, down, left, right, base, latest, out = kept
    rows = spare.shape[0]
    vectors, size, _ = out.shape
    place = lax.axis_index("sweep")
    task = task_at(tick, place, lax.axis_size("sweep"), vectors)
    active, vector, rank, forward, half = task

    if any(turns(one) for one in tasks):

        @pl.when(turns(task))
        def _():
            take_lateral(base, vector, left, right, left_cols, right_cols, incoming[...], spare, 1)
            take_lateral(base, vector, left, right, left_cols, right_cols, arrived[0], spare, 0)

    @pl.when(active)
    def _():
        known = base[vector]
        value[...] = known
        base[vector] = source[vector]

        def take_chain(matrix, columns):
            spare[...] = gathered(incoming[...], columns[...])
            term = product(matrix, spare, rows)
            value[...] = known - term
            base[vector] = source[vector] - term

        if any(one[0] and one[2] > 0 and one[3] for one in tasks):

            @pl.when((rank > 0) & forward)
            def _():
                take_chain(up, up_cols)

        if any(one[0] and one[2] > 0 and not one[3] for one in tasks):

            @pl.when((rank > 0) & (forward ^ True))
            def _():
                take_chain(down, down_cols)

        spare[...] = value[...]
        fresh = product(diag, spare, rows)
        value[...] = fresh
        latest[vector] = fresh

        if any(one[0] and one[4] == 3 for one in tasks):

            @pl.when(half == 3)
            def _():
                out[vector] = fresh[:size]

    if cross:
        fill(cross[0], latest, sent, place)


def fill(cross, latest, plan, place):
    for entry in range(cross.shape[0]):
        chosen = numbers(plan, entry)
        if any(one >= 0 for one in chosen):
            vector = pick(chosen, place)

            @pl.when(vector >= 0)
            def _():
                cross[entry] = latest[vector]


def side_kernel(came, plan, columns_and_inputs, kept, values, spare):
    left_cols, right_cols, *arrived = columns_and_inputs
    left, right, base, latest = kept
    place = lax.axis_index("sweep")
    if values:
        fill(values[0], latest, plan, place)
    if arrived:
        pairs = pick(numbers(came, -1), place)
        for entry in range(arrived[0].shape[0]):
            chosen = numbers(came, entry)
            if any(one >= 0 for one in chosen):
                vector = pick(chosen, place)

                @pl.when(vector >= 0)
                def _():
                    take_lateral(
                        base, vector, left, right, left_cols, right_cols, arrived[0][entry], spare, pairs
                    )


def in_vmem(count):
    return [pl.BlockSpec(memory_space=pltpu.VMEM)] * count


def far(array):
    return pltpu.with_memory_space_constraint(array, pltpu.HBM)


def held(shape):
    return pltpu.VMEM(shape, jnp.float32)


def call(kernel, name, fixed, kept, fresh, spare):
    def body(*refs):
        inputs, outputs = refs[: len(fixed)], refs[len(fixed) + len(kept) : -1]
        kernel(inputs, outputs[: len(kept)], outputs[len(kept) :], refs[-1])

    return pl.pallas_call(
        body,
        out_shape=tuple(held(shape) for shape in [*(a.shape for a in kept), *fresh]),
        in_specs=in_vmem(len(fixed) + len(kept)),
        out_specs=tuple(in_vmem(len(fresh) + len(kept))),
        scratch_shapes=[held(spare)],
        input_output_aliases={len(fixed) + n: n for n in range(len(kept))},
        compiler_params=pltpu.CompilerParams(vmem_limit_bytes=VMEM_LIMIT),
        name=name,
    )(*fixed, *kept)


def preparing(size, rows, lanes):
    return [
        pltpu.VMEM((size, size, lanes), jnp.bfloat16),
        held((rows * rows, lanes)),
        pltpu.SemaphoreType.DMA((CHUNKS,)),
    ]


def first_call(block, residual, columns, rows):
    vectors, size, lanes = residual.shape
    several = (vectors, rows, lanes)
    in_hbm = pl.BlockSpec(memory_space=pltpu.HBM)
    return pl.pallas_call(
        first_kernel,
        out_shape=(
            held((size, rows, lanes)), held(several), held(several), held((rows, lanes)),
            *(pltpu.VMEM(one.shape, one.dtype) for one in columns),
        ),
        in_specs=[in_hbm, *in_vmem(1), *[in_hbm] * 4],
        out_specs=tuple(in_vmem(8)),
        scratch_shapes=[*preparing(size, rows, lanes), pltpu.SemaphoreType.DMA((4,))],
        compiler_params=pltpu.CompilerParams(vmem_limit_bytes=PREPARE_LIMIT),
        name="first",
    )(far(block), residual, *(far(one) for one in columns))


def later_call(block, face, base):
    size, _, lanes = block.shape[-3:]
    rows = base.shape[1]
    return pl.pallas_call(
        functools.partial(later_kernel, face),
        out_shape=(held((size, rows, lanes)), held(base.shape)),
        in_specs=[pl.BlockSpec(memory_space=pltpu.HBM), *in_vmem(1)],
        out_specs=tuple(in_vmem(2)),
        scratch_shapes=preparing(size, rows, lanes),
        input_output_aliases={1: 1},
        compiler_params=pltpu.CompilerParams(vmem_limit_bytes=PREPARE_LIMIT),
        name="later",
    )(far(block), base)


def per_device(
    residual_in, diag_inverse, up_block, side_blocks, up_cols, down_cols, left_cols, right_cols
):
    vectors, size, lanes = residual_in.shape[2:]
    rows = size + -size % SUBLANES
    columns = [one.reshape(1, lanes) for one in (up_cols, down_cols, left_cols, right_cols)]
    count = lax.axis_size("sweep")
    parts = lax.axis_size("span")
    ticks = 4 * count + 2 * (vectors - 1)
    sent, urgent = lateral_plan(count, vectors)
    even_pairs = [(p, p + 1) for p in range(0, parts - 1, 2)]
    odd_pairs = [(p, p + 1) for p in range(1, parts - 1, 2)]

    def closed(pairs, members):
        alone = [one for one in members if all(one not in two for two in pairs)]
        return [*pairs, *((b, a) for a, b in pairs), *((one, one) for one in alone)]

    def device(slab, part):
        return slab * parts + part

    diag, base, source, blank, *columns = first_call(diag_inverse[0, 0], residual_in[0, 0], columns, rows)
    latest, out = pl.pallas_call(
        lambda *refs: None,
        out_shape=(held((vectors, rows, lanes)), held((vectors, size, lanes))),
        out_specs=tuple(in_vmem(2)),
        name="room",
    )()
    incoming = arrived = blank
    late_blocks = [(up_block, 0), *((side_blocks, face) for face in range(3))]
    mats = [diag, blank, blank, blank, blank]

    def tasks_at(tick):
        return [task_at(tick, place, count, vectors, lambda which, a, b: a if which else b) for place in range(count)]

    for tick in range(ticks):
        tasks = tasks_at(tick)
        plan = sent[tick]
        used = 1 + sum(mat is not blank for mat in mats[1:])
        turning = any(turns(one) for one in tasks)
        at_once = any(plan) and tick & 1 == 1
        results = call(
            lambda fixed, kept, fresh, spare, used=used, tick=tick, tasks=tasks: task_kernel(
                tick, tasks, sent[tick], fixed, [*kept[:used], *[None] * (5 - used), *kept[used:]], fresh, spare
            ),
            "task",
            (*columns, source, incoming, arrived if turning else blank),
            (*mats[:used], base, latest, out),
            ((rows, lanes), *([(1, rows, lanes)] if at_once else [])),
            (rows, lanes),
        )
        mats[:used] = results[:used]
        base, latest, out, value, *cross = results[used:]

        if any(urgent[tick]) or any(one[0] and one[2] > 0 for one in tasks_at(tick + 1)):
            pairs = []
            swap = [(s, s + 1) for s in range(tick & 1, count - 1, 2)]
            for a, b in swap:
                forth, back = (0 if tasks[one][0] else 1 for one in (a, b))
                if forth and back:
                    forth = back = 0
                for p in range(parts):
                    pairs += [(device(a, p), device(b, p ^ forth)), (device(b, p), device(a, p ^ back))]
            alone = [s for s in range(count) if all(s not in two for two in swap)]
            for s in alone:
                chosen = odd_pairs if urgent[tick][s] else even_pairs
                pairs += [(device(s, x), device(s, y)) for x, y in closed(chosen, range(parts))]
            incoming = lax.ppermute(value, ("sweep", "span"), pairs)
        came = [None if not tick or urgent[tick - 1][s] else sent[tick - 1][s] for s in range(count)]
        later = any(plan) and not at_once
        if any(came) or later:
            mats[3], mats[4], base, latest, *made = call(
                functools.partial(side_kernel, came, plan),
                "side",
                (columns[2], columns[3], *([arrived] if any(came) else [])),
                (mats[3], mats[4], base, latest),
                ((2, rows, lanes),) if later else (),
                (rows, lanes),
            )
            cross += made
        if any(plan):
            pairs = [
                (device(s, a), device(s, b))
                for s in range(count)
                if plan[s] is not None
                for a, b in (odd_pairs if plan[s][0] else even_pairs)
            ]
            arrived = lax.ppermute(cross[0], ("sweep", "span"), closed(pairs, range(count * parts)))
        if tick < len(late_blocks):
            mats[1 + tick], base = later_call(*late_blocks[tick], base)
    return out[None, None]


def solution(mesh):
    return jax.shard_map(
        per_device,
        mesh=mesh,
        in_specs=(
            P("sweep", "span", None, None, None),
            P("sweep", "span", None, None, None),
            P("sweep", "span", None, None, None),
            P("sweep", "span", None, None, None, None),
            P("sweep", "span", None),
            P("sweep", "span", None),
            P("sweep", "span", None),
            P("sweep", "span", None),
        ),
        out_specs=P("sweep", "span", None, None, None),
        check_vma=False,
    )
```

```python
import functools

import jax
import jax.numpy as jnp
from jax import lax
from jax.experimental import pallas as pl
from jax.experimental.pallas import tpu as pltpu
from jax.sharding import PartitionSpec as P

SUBLANES = 8
VMEM_LIMIT = 2 * 1024 * 1024
PREPARE_LIMIT = 12 * 1024 * 1024
LATERAL_START = 4
CHUNKS = 4


def task_at(tick, place, count, vectors, choose=jnp.where):
    forward = ((tick - place) & 1) == 0
    rank = choose(forward, place, count - 1 - place)
    since = tick - rank - choose(forward, 0, count)
    late = since >= 2 * count
    since = choose(late, since - 2 * count, since)
    active = (since >= 0) & (since < 2 * vectors)
    half = choose(forward, 0, 1) + choose(late, 2, 0)
    return active, choose(active, since >> 1, 0), rank, forward, half


def turns(task):
    active, _, rank, _, half = task
    return active & (rank == 0) & (half > 0)


def lateral_plan(count, vectors):
    ticks = 4 * count + 2 * (vectors - 1)
    sent = [[None] * count for _ in range(ticks)]
    urgent = [[False] * count for _ in range(ticks)]
    for slab in range(count):
        left = ([], [])
        for half in range(3):
            rank = count - 1 - slab if half & 1 else slab
            for vector in range(vectors):
                made = 2 * vector + half * count + rank
                used = 2 * vector + (half + 1) * count + count - 1 - rank
                if used == made + 1:
                    sent[made][slab] = (0, (vector,))
                    urgent[made][slab] = True
                    continue
                left[1].append((used, made, vector))
                if used == made + 3:
                    sent[made + 1][slab] = (0, (vector,))
                else:
                    left[0].append((used, made, vector))
        for tick in range(LATERAL_START, ticks, 2):
            ready = [sorted(one for one in waiting if one[1] <= tick)[:2] for waiting in left]
            if not any(ready):
                continue
            pairs = 0 if ready[0] and (not ready[1] or ready[0][0][0] <= ready[1][0][0]) else 1
            assert tick <= ready[pairs][0][0] - 2
            sent[tick][slab] = (pairs, tuple(one[2] for one in ready[pairs]))
            for one in ready[pairs]:
                left[pairs].remove(one)
        assert not any(left)
    return sent, urgent


def numbers(plan, entry):
    if entry < 0:
        return [-1 if one is None else one[0] for one in plan]
    return [-1 if one is None or len(one[1]) <= entry else one[1][entry] for one in plan]


def pick(values, place):
    result = jnp.int32(values[0])
    for at, value in enumerate(values):
        if value != values[0]:
            result = jnp.where(place == at, value, result)
    return result


def product(matrix, vector, rows, unroll=25):
    def body(step, total):
        for inner in range(unroll):
            j = step * unroll + inner
            total = total + matrix[j] * vector[pl.ds(j, 1), :]
        return total

    start = jnp.zeros((rows, matrix.shape[2]), jnp.float32)
    return lax.fori_loop(0, matrix.shape[0] // unroll, body, start)


def gathered(value, columns):
    index = jnp.broadcast_to(columns, value.shape)
    return jnp.take_along_axis(value, index, axis=1, mode="promise_in_bounds")


def take_lateral(base, vector, left, right, left_cols, right_cols, arrived, spare, pairs):
    rows = spare.shape[0]
    part = lax.axis_index("span")
    on_right = (part & 1) == pairs

    @pl.when(on_right & (part < lax.axis_size("span") - 1))
    def _():
        spare[...] = gathered(arrived, right_cols[...])
        base[vector] = base[vector] - product(right, spare, rows)

    @pl.when((on_right ^ True) & (part > 0))
    def _():
        spare[...] = gathered(arrived, left_cols[...])
        base[vector] = base[vector] - product(left, spare, rows)


def prepare(block, ready, narrow, wide, sems):
    size, _, lanes = block.shape
    rows = ready.shape[1]
    share = size // CHUNKS
    copies = [
        pltpu.make_async_copy(block.at[pl.ds(n * share, share)], narrow.at[pl.ds(n * share, share)], sems.at[n])
        for n in range(CHUNKS)
    ]
    for copy in copies:
        copy.start()
    wide[pl.ds(size * rows, (rows - size) * rows), :] = jnp.zeros(((rows - size) * rows, lanes), jnp.float32)

    def widen(i, _):
        wide[pl.ds(pl.multiple_of(i * rows, SUBLANES), size), :] = narrow[i].astype(jnp.float32)
        return 0

    for n, copy in enumerate(copies):
        copy.wait()
        lax.fori_loop(n * share, (n + 1) * share, widen, 0, unroll=5)

    def turn(j, _):
        for i in range(0, rows, SUBLANES):
            ready[j, pl.ds(i, SUBLANES), :] = wide[pl.ds(i * rows + j, SUBLANES, stride=rows), :]
        return 0

    lax.fori_loop(0, size, turn, 0, unroll=4)


def first_kernel(block, residual, *refs):
    hbm_columns, (ready, base, source, blank, *columns), (narrow, wide, sems, column_sems) = (
        refs[:4], refs[4:12], refs[12:]
    )
    copies = [
        pltpu.make_async_copy(there, here, column_sems.at[n])
        for n, (there, here) in enumerate(zip(hbm_columns, columns))
    ]
    for copy in copies:
        copy.start()
    prepare(block, ready, narrow, wide, sems)
    vectors, size, lanes = residual.shape
    rows = base.shape[1]
    base[:, pl.ds(rows - SUBLANES, SUBLANES), :] = jnp.zeros((vectors, SUBLANES, lanes), jnp.float32)
    base[:, pl.ds(0, size), :] = residual[...]
    source[...] = base[...]
    blank[...] = jnp.zeros_like(blank)
    for copy in copies:
        copy.wait()


def later_kernel(face, block, base_in, ready, base, narrow, wide, sems):
    prepare(block.at[(0,) * (len(block.shape) - 4) + (face,)], ready, narrow, wide, sems)


def task_kernel(
    tick, tasks, sent, columns_and_inputs, kept, values, spare
):
    up_cols, down_cols, left_cols, right_cols, source, incoming, arrived = columns_and_inputs
    value, *cross = values
    diag, up, down, left, right, base, latest, out = kept
    rows = spare.shape[0]
    vectors, size, _ = out.shape
    place = lax.axis_index("sweep")
    task = task_at(tick, place, lax.axis_size("sweep"), vectors)
    active, vector, rank, forward, half = task

    if any(turns(one) for one in tasks):

        @pl.when(turns(task))
        def _():
            take_lateral(base, vector, left, right, left_cols, right_cols, incoming[...], spare, 1)
            take_lateral(base, vector, left, right, left_cols, right_cols, arrived[0], spare, 0)

    @pl.when(active)
    def _():
        known = base[vector]
        value[...] = known
        base[vector] = source[vector]

        def take_chain(matrix, columns):
            spare[...] = gathered(incoming[...], columns[...])
            term = product(matrix, spare, rows)
            value[...] = known - term
            base[vector] = source[vector] - term

        if any(one[0] and one[2] > 0 and one[3] for one in tasks):

            @pl.when((rank > 0) & forward)
            def _():
                take_chain(up, up_cols)

        if any(one[0] and one[2] > 0 and not one[3] for one in tasks):

            @pl.when((rank > 0) & (forward ^ True))
            def _():
                take_chain(down, down_cols)

        spare[...] = value[...]
        fresh = product(diag, spare, rows)
        value[...] = fresh
        latest[vector] = fresh

        if any(one[0] and one[4] == 3 for one in tasks):

            @pl.when(half == 3)
            def _():
                out[vector] = fresh[:size]

    if cross:
        fill(cross[0], latest, sent, place)


def fill(cross, latest, plan, place):
    for entry in range(cross.shape[0]):
        chosen = numbers(plan, entry)
        if any(one >= 0 for one in chosen):
            vector = pick(chosen, place)

            @pl.when(vector >= 0)
            def _():
                cross[entry] = latest[vector]


def side_kernel(came, plan, columns_and_inputs, kept, values, spare):
    left_cols, right_cols, *arrived = columns_and_inputs
    left, right, base, latest = kept
    place = lax.axis_index("sweep")
    if values:
        fill(values[0], latest, plan, place)
    if arrived:
        pairs = pick(numbers(came, -1), place)
        for entry in range(arrived[0].shape[0]):
            chosen = numbers(came, entry)
            if any(one >= 0 for one in chosen):
                vector = pick(chosen, place)

                @pl.when(vector >= 0)
                def _():
                    take_lateral(
                        base, vector, left, right, left_cols, right_cols, arrived[0][entry], spare, pairs
                    )


def in_vmem(count):
    return [pl.BlockSpec(memory_space=pltpu.VMEM)] * count


def far(array):
    return pltpu.with_memory_space_constraint(array, pltpu.HBM)


def held(shape):
    return pltpu.VMEM(shape, jnp.float32)


def call(kernel, name, fixed, kept, fresh, spare):
    def body(*refs):
        inputs, outputs = refs[: len(fixed)], refs[len(fixed) + len(kept) : -1]
        kernel(inputs, outputs[: len(kept)], outputs[len(kept) :], refs[-1])

    return pl.pallas_call(
        body,
        out_shape=tuple(held(shape) for shape in [*(a.shape for a in kept), *fresh]),
        in_specs=in_vmem(len(fixed) + len(kept)),
        out_specs=tuple(in_vmem(len(fresh) + len(kept))),
        scratch_shapes=[held(spare)],
        input_output_aliases={len(fixed) + n: n for n in range(len(kept))},
        compiler_params=pltpu.CompilerParams(vmem_limit_bytes=VMEM_LIMIT),
        name=name,
    )(*fixed, *kept)


def preparing(size, rows, lanes):
    return [
        pltpu.VMEM((size, size, lanes), jnp.bfloat16),
        held((rows * rows, lanes)),
        pltpu.SemaphoreType.DMA((CHUNKS,)),
    ]


def first_call(block, residual, columns, rows):
    vectors, size, lanes = residual.shape
    several = (vectors, rows, lanes)
    in_hbm = pl.BlockSpec(memory_space=pltpu.HBM)
    return pl.pallas_call(
        first_kernel,
        out_shape=(
            held((size, rows, lanes)), held(several), held(several), held((rows, lanes)),
            *(pltpu.VMEM(one.shape, one.dtype) for one in columns),
        ),
        in_specs=[in_hbm, *in_vmem(1), *[in_hbm] * 4],
        out_specs=tuple(in_vmem(8)),
        scratch_shapes=[*preparing(size, rows, lanes), pltpu.SemaphoreType.DMA((4,))],
        compiler_params=pltpu.CompilerParams(vmem_limit_bytes=PREPARE_LIMIT),
        name="first",
    )(far(block), residual, *(far(one) for one in columns))


def later_call(block, face, base):
    size, _, lanes = block.shape[-3:]
    rows = base.shape[1]
    return pl.pallas_call(
        functools.partial(later_kernel, face),
        out_shape=(held((size, rows, lanes)), held(base.shape)),
        in_specs=[pl.BlockSpec(memory_space=pltpu.HBM), *in_vmem(1)],
        out_specs=tuple(in_vmem(2)),
        scratch_shapes=preparing(size, rows, lanes),
        input_output_aliases={1: 1},
        compiler_params=pltpu.CompilerParams(vmem_limit_bytes=PREPARE_LIMIT),
        name="later",
    )(far(block), base)


def per_device(
    residual_in, diag_inverse, up_block, side_blocks, up_cols, down_cols, left_cols, right_cols
):
    vectors, size, lanes = residual_in.shape[2:]
    rows = size + -size % SUBLANES
    columns = [one.reshape(1, lanes) for one in (up_cols, down_cols, left_cols, right_cols)]
    count = lax.axis_size("sweep")
    parts = lax.axis_size("span")
    ticks = 4 * count + 2 * (vectors - 1)
    sent, urgent = lateral_plan(count, vectors)
    even_pairs = [(p, p + 1) for p in range(0, parts - 1, 2)]
    odd_pairs = [(p, p + 1) for p in range(1, parts - 1, 2)]

    def closed(pairs, members):
        alone = [one for one in members if all(one not in two for two in pairs)]
        return [*pairs, *((b, a) for a, b in pairs), *((one, one) for one in alone)]

    def device(slab, part):
        return slab * parts + part

    diag, base, source, blank, *columns = first_call(diag_inverse[0, 0], residual_in[0, 0], columns, rows)
    latest, out = pl.pallas_call(
        lambda *refs: None,
        out_shape=(held((vectors, rows, lanes)), held((vectors, size, lanes))),
        out_specs=tuple(in_vmem(2)),
        name="room",
    )()
    incoming = arrived = blank
    late_blocks = [(up_block, 0), *((side_blocks, face) for face in range(3))]
    mats = [diag, blank, blank, blank, blank]

    def tasks_at(tick):
        return [task_at(tick, place, count, vectors, lambda which, a, b: a if which else b) for place in range(count)]

    for tick in range(ticks):
        tasks = tasks_at(tick)
        plan = sent[tick]
        used = 1 + sum(mat is not blank for mat in mats[1:])
        turning = any(turns(one) for one in tasks)
        at_once = any(plan) and tick & 1 == 1
        results = call(
            lambda fixed, kept, fresh, spare, used=used, tick=tick, tasks=tasks: task_kernel(
                tick, tasks, sent[tick], fixed, [*kept[:used], *[None] * (5 - used), *kept[used:]], fresh, spare
            ),
            "task",
            (*columns, source, incoming, arrived if turning else blank),
            (*mats[:used], base, latest, out),
            ((rows, lanes), *([(1, rows, lanes)] if at_once else [])),
            (rows, lanes),
        )
        mats[:used] = results[:used]
        base, latest, out, value, *cross = results[used:]

        if any(urgent[tick]) or any(one[0] and one[2] > 0 for one in tasks_at(tick + 1)):
            pairs = []
            swap = [(s, s + 1) for s in range(tick & 1, count - 1, 2)]
            for a, b in swap:
                forth, back = (0 if tasks[one][0] else 1 for one in (a, b))
                if forth and back:
                    forth = back = 0
                for p in range(parts):
                    pairs += [(device(a, p), device(b, p ^ forth)), (device(b, p), device(a, p ^ back))]
            alone = [s for s in range(count) if all(s not in two for two in swap)]
            for s in alone:
                chosen = odd_pairs if urgent[tick][s] else even_pairs
                pairs += [(device(s, x), device(s, y)) for x, y in closed(chosen, range(parts))]
            incoming = lax.ppermute(value, ("sweep", "span"), sorted(pairs))
        came = [None if not tick or urgent[tick - 1][s] else sent[tick - 1][s] for s in range(count)]
        later = any(plan) and not at_once
        if any(came) or later:
            mats[3], mats[4], base, latest, *made = call(
                functools.partial(side_kernel, came, plan),
                "side",
                (columns[2], columns[3], *([arrived] if any(came) else [])),
                (mats[3], mats[4], base, latest),
                ((2, rows, lanes),) if later else (),
                (rows, lanes),
            )
            cross += made
        if any(plan):
            pairs = [
                (device(s, a), device(s, b))
                for s in range(count)
                if plan[s] is not None
                for a, b in (odd_pairs if plan[s][0] else even_pairs)
            ]
            arrived = lax.ppermute(cross[0], ("sweep", "span"), sorted(closed(pairs, range(count * parts))))
        if tick < len(late_blocks):
            mats[1 + tick], base = later_call(*late_blocks[tick], base)
    return out[None, None]


def solution(mesh):
    return jax.shard_map(
        per_device,
        mesh=mesh,
        in_specs=(
            P("sweep", "span", None, None, None),
            P("sweep", "span", None, None, None),
            P("sweep", "span", None, None, None),
            P("sweep", "span", None, None, None, None),
            P("sweep", "span", None),
            P("sweep", "span", None),
            P("sweep", "span", None),
            P("sweep", "span", None),
        ),
        out_specs=P("sweep", "span", None, None, None),
        check_vma=False,
    )
```

```python
import functools

import jax
import jax.numpy as jnp
from jax import lax
from jax.experimental import pallas as pl
from jax.experimental.pallas import tpu as pltpu
from jax.sharding import PartitionSpec as P

SUBLANES = 8
VMEM_LIMIT = 2 * 1024 * 1024
PREPARE_LIMIT = 12 * 1024 * 1024
LATERAL_START = 4
CHUNKS = 4


def task_at(tick, place, count, vectors, choose=jnp.where):
    forward = ((tick - place) & 1) == 0
    rank = choose(forward, place, count - 1 - place)
    since = tick - rank - choose(forward, 0, count)
    late = since >= 2 * count
    since = choose(late, since - 2 * count, since)
    active = (since >= 0) & (since < 2 * vectors)
    half = choose(forward, 0, 1) + choose(late, 2, 0)
    return active, choose(active, since >> 1, 0), rank, forward, half


def turns(task):
    active, _, rank, _, half = task
    return active & (rank == 0) & (half > 0)


def lateral_plan(count, vectors):
    ticks = 4 * count + 2 * (vectors - 1)
    sent = [[None] * count for _ in range(ticks)]
    urgent = [[False] * count for _ in range(ticks)]
    for slab in range(count):
        left = ([], [])
        for half in range(3):
            rank = count - 1 - slab if half & 1 else slab
            for vector in range(vectors):
                made = 2 * vector + half * count + rank
                used = 2 * vector + (half + 1) * count + count - 1 - rank
                if used == made + 1:
                    sent[made][slab] = (1, (vector,))
                    urgent[made][slab] = True
                    continue
                left[1].append((used, made, vector))
                if used == made + 3:
                    sent[made + 1][slab] = (0, (vector,))
                else:
                    left[0].append((used, made, vector))
        for tick in range(LATERAL_START, ticks, 2):
            ready = [sorted(one for one in waiting if one[1] <= tick)[:2] for waiting in left]
            if not any(ready):
                continue
            pairs = 0 if ready[0] and (not ready[1] or ready[0][0][0] <= ready[1][0][0]) else 1
            assert tick <= ready[pairs][0][0] - 2
            sent[tick][slab] = (pairs, tuple(one[2] for one in ready[pairs]))
            for one in ready[pairs]:
                left[pairs].remove(one)
        assert not any(left)
    return sent, urgent


def numbers(plan, entry):
    if entry < 0:
        return [-1 if one is None else one[0] for one in plan]
    return [-1 if one is None or len(one[1]) <= entry else one[1][entry] for one in plan]


def pick(values, place):
    result = jnp.int32(values[0])
    for at, value in enumerate(values):
        if value != values[0]:
            result = jnp.where(place == at, value, result)
    return result


def product(matrix, vector, rows):
    count = matrix.shape[0]
    group = 3 * SUBLANES

    def add(first, amount, total):
        tile = vector[pl.ds(first, SUBLANES), :]
        for row in range(amount):
            total = total + matrix[first + row] * tile[row : row + 1, :]
        return total

    def body(step, total):
        for n in range(0, group, SUBLANES):
            total = add(pl.multiple_of(step * group + n, SUBLANES), SUBLANES, total)
        return total

    total = lax.fori_loop(0, count // group, body, jnp.zeros((rows, matrix.shape[2]), jnp.float32))
    for first in range(count - count % group, count, SUBLANES):
        total = add(first, min(SUBLANES, count - first), total)
    return total


def gathered(value, columns):
    index = jnp.broadcast_to(columns, value.shape)
    return jnp.take_along_axis(value, index, axis=1, mode="promise_in_bounds")


def take_lateral(base, vector, left, right, left_cols, right_cols, arrived, spare, pairs):
    rows = spare.shape[0]
    part = lax.axis_index("span")
    on_right = (part & 1) == pairs

    @pl.when(on_right & (part < lax.axis_size("span") - 1))
    def _():
        spare[...] = gathered(arrived, right_cols[...])
        base[vector] = base[vector] - product(right, spare, rows)

    @pl.when((on_right ^ True) & (part > 0))
    def _():
        spare[...] = gathered(arrived, left_cols[...])
        base[vector] = base[vector] - product(left, spare, rows)


def prepare(block, ready, narrow, wide, sems):
    size, _, lanes = block.shape
    rows = ready.shape[1]
    share = size // CHUNKS
    copies = [
        pltpu.make_async_copy(block.at[pl.ds(n * share, share)], narrow.at[pl.ds(n * share, share)], sems.at[n])
        for n in range(CHUNKS)
    ]
    for copy in copies:
        copy.start()
    wide[pl.ds(size * rows, (rows - size) * rows), :] = jnp.zeros(((rows - size) * rows, lanes), jnp.float32)

    def widen(i, _):
        wide[pl.ds(pl.multiple_of(i * rows, SUBLANES), size), :] = narrow[i].astype(jnp.float32)
        return 0

    for n, copy in enumerate(copies):
        copy.wait()
        lax.fori_loop(n * share, (n + 1) * share, widen, 0, unroll=5)

    def turn(j, _):
        for i in range(0, rows, SUBLANES):
            ready[j, pl.ds(i, SUBLANES), :] = wide[pl.ds(i * rows + j, SUBLANES, stride=rows), :]
        return 0

    lax.fori_loop(0, size, turn, 0, unroll=4)


def first_kernel(block, residual, *refs):
    hbm_columns, (ready, base, source, blank, *columns), (narrow, wide, sems, column_sems) = (
        refs[:4], refs[4:12], refs[12:]
    )
    copies = [
        pltpu.make_async_copy(there, here, column_sems.at[n])
        for n, (there, here) in enumerate(zip(hbm_columns, columns))
    ]
    for copy in copies:
        copy.start()
    prepare(block, ready, narrow, wide, sems)
    vectors, size, lanes = residual.shape
    rows = base.shape[1]
    base[:, pl.ds(rows - SUBLANES, SUBLANES), :] = jnp.zeros((vectors, SUBLANES, lanes), jnp.float32)
    base[:, pl.ds(0, size), :] = residual[...]
    source[...] = base[...]
    blank[...] = jnp.zeros_like(blank)
    for copy in copies:
        copy.wait()


def later_kernel(face, block, base_in, ready, base, narrow, wide, sems):
    prepare(block.at[(0,) * (len(block.shape) - 4) + (face,)], ready, narrow, wide, sems)


def task_kernel(
    tick, tasks, sent, columns_and_inputs, kept, values, spare
):
    up_cols, down_cols, left_cols, right_cols, source, incoming, arrived = columns_and_inputs
    value, *cross = values
    diag, up, down, left, right, base, latest, out = kept
    rows = spare.shape[0]
    vectors, size, _ = out.shape
    place = lax.axis_index("sweep")
    task = task_at(tick, place, lax.axis_size("sweep"), vectors)
    active, vector, rank, forward, half = task

    if any(turns(one) for one in tasks):

        @pl.when(turns(task))
        def _():
            take_lateral(base, vector, left, right, left_cols, right_cols, arrived[0], spare, 1)

    @pl.when(active)
    def _():
        known = base[vector]
        value[...] = known
        base[vector] = source[vector]

        def take_chain(matrix, columns):
            spare[...] = gathered(incoming[...], columns[...])
            term = product(matrix, spare, rows)
            value[...] = known - term
            base[vector] = source[vector] - term

        if any(one[0] and one[2] > 0 and one[3] for one in tasks):

            @pl.when((rank > 0) & forward)
            def _():
                take_chain(up, up_cols)

        if any(one[0] and one[2] > 0 and not one[3] for one in tasks):

            @pl.when((rank > 0) & (forward ^ True))
            def _():
                take_chain(down, down_cols)

        spare[...] = value[...]
        fresh = product(diag, spare, rows)
        value[...] = fresh
        latest[vector] = fresh

        if any(one[0] and one[4] == 3 for one in tasks):

            @pl.when(half == 3)
            def _():
                out[vector] = fresh[:size]

    if cross:
        fill(cross[0], latest, sent, place)


def fill(cross, latest, plan, place):
    for entry in range(cross.shape[0]):
        chosen = numbers(plan, entry)
        if any(one >= 0 for one in chosen):
            vector = pick(chosen, place)

            @pl.when(vector >= 0)
            def _():
                cross[entry] = latest[vector]


def side_kernel(came, plan, columns_and_inputs, kept, values, spare):
    left_cols, right_cols, *arrived = columns_and_inputs
    left, right, base, latest = kept
    place = lax.axis_index("sweep")
    if values:
        fill(values[0], latest, plan, place)
    if arrived:
        pairs = pick(numbers(came, -1), place)
        for entry in range(arrived[0].shape[0]):
            chosen = numbers(came, entry)
            if any(one >= 0 for one in chosen):
                vector = pick(chosen, place)

                @pl.when(vector >= 0)
                def _():
                    take_lateral(
                        base, vector, left, right, left_cols, right_cols, arrived[0][entry], spare, pairs
                    )


def turn_kernel(tick, vectors, columns_and_inputs, kept, values, spare):
    left_cols, right_cols, incoming = columns_and_inputs
    left, right, base = kept
    task = task_at(tick, lax.axis_index("sweep"), lax.axis_size("sweep"), vectors)

    @pl.when(turns(task))
    def _():
        take_lateral(base, task[1], left, right, left_cols, right_cols, incoming[...], spare, 0)


def in_vmem(count):
    return [pl.BlockSpec(memory_space=pltpu.VMEM)] * count


def far(array):
    return pltpu.with_memory_space_constraint(array, pltpu.HBM)


def held(shape):
    return pltpu.VMEM(shape, jnp.float32)


def call(kernel, name, fixed, kept, fresh, spare):
    def body(*refs):
        inputs, outputs = refs[: len(fixed)], refs[len(fixed) + len(kept) : -1]
        kernel(inputs, outputs[: len(kept)], outputs[len(kept) :], refs[-1])

    return pl.pallas_call(
        body,
        out_shape=tuple(held(shape) for shape in [*(a.shape for a in kept), *fresh]),
        in_specs=in_vmem(len(fixed) + len(kept)),
        out_specs=tuple(in_vmem(len(fresh) + len(kept))),
        scratch_shapes=[held(spare)],
        input_output_aliases={len(fixed) + n: n for n in range(len(kept))},
        compiler_params=pltpu.CompilerParams(vmem_limit_bytes=VMEM_LIMIT),
        name=name,
    )(*fixed, *kept)


def preparing(size, rows, lanes):
    return [
        pltpu.VMEM((size, size, lanes), jnp.bfloat16),
        held((rows * rows, lanes)),
        pltpu.SemaphoreType.DMA((CHUNKS,)),
    ]


def first_call(block, residual, columns, rows):
    vectors, size, lanes = residual.shape
    several = (vectors, rows, lanes)
    in_hbm = pl.BlockSpec(memory_space=pltpu.HBM)
    return pl.pallas_call(
        first_kernel,
        out_shape=(
            held((size, rows, lanes)), held(several), held(several), held((rows, lanes)),
            *(pltpu.VMEM(one.shape, one.dtype) for one in columns),
        ),
        in_specs=[in_hbm, *in_vmem(1), *[in_hbm] * 4],
        out_specs=tuple(in_vmem(8)),
        scratch_shapes=[*preparing(size, rows, lanes), pltpu.SemaphoreType.DMA((4,))],
        compiler_params=pltpu.CompilerParams(vmem_limit_bytes=PREPARE_LIMIT),
        name="first",
    )(far(block), residual, *(far(one) for one in columns))


def later_call(block, face, base):
    size, _, lanes = block.shape[-3:]
    rows = base.shape[1]
    return pl.pallas_call(
        functools.partial(later_kernel, face),
        out_shape=(held((size, rows, lanes)), held(base.shape)),
        in_specs=[pl.BlockSpec(memory_space=pltpu.HBM), *in_vmem(1)],
        out_specs=tuple(in_vmem(2)),
        scratch_shapes=preparing(size, rows, lanes),
        input_output_aliases={1: 1},
        compiler_params=pltpu.CompilerParams(vmem_limit_bytes=PREPARE_LIMIT),
        name="later",
    )(far(block), base)


def per_device(
    residual_in, diag_inverse, up_block, side_blocks, up_cols, down_cols, left_cols, right_cols
):
    vectors, size, lanes = residual_in.shape[2:]
    rows = size + -size % SUBLANES
    columns = [one.reshape(1, lanes) for one in (up_cols, down_cols, left_cols, right_cols)]
    count = lax.axis_size("sweep")
    parts = lax.axis_size("span")
    ticks = 4 * count + 2 * (vectors - 1)
    sent, urgent = lateral_plan(count, vectors)
    even_pairs = [(p, p + 1) for p in range(0, parts - 1, 2)]
    odd_pairs = [(p, p + 1) for p in range(1, parts - 1, 2)]

    def closed(pairs, members):
        alone = [one for one in members if all(one not in two for two in pairs)]
        return [*pairs, *((b, a) for a, b in pairs), *((one, one) for one in alone)]

    def device(slab, part):
        return slab * parts + part

    diag, base, source, blank, *columns = first_call(diag_inverse[0, 0], residual_in[0, 0], columns, rows)
    latest, out = pl.pallas_call(
        lambda *refs: None,
        out_shape=(held((vectors, rows, lanes)), held((vectors, size, lanes))),
        out_specs=tuple(in_vmem(2)),
        name="room",
    )()
    incoming = arrived = blank
    late_blocks = [(up_block, 0), *((side_blocks, face) for face in range(3))]
    mats = [diag, blank, blank, blank, blank]

    def tasks_at(tick):
        return [task_at(tick, place, count, vectors, lambda which, a, b: a if which else b) for place in range(count)]

    for tick in range(ticks):
        tasks = tasks_at(tick)
        plan = sent[tick]
        used = 1 + sum(mat is not blank for mat in mats[1:])
        turning = any(turns(one) for one in tasks)
        at_once = any(plan) and tick & 1 == 1
        results = call(
            lambda fixed, kept, fresh, spare, used=used, tick=tick, tasks=tasks: task_kernel(
                tick, tasks, sent[tick], fixed, [*kept[:used], *[None] * (5 - used), *kept[used:]], fresh, spare
            ),
            "task",
            (*columns, source, incoming, arrived if turning else blank),
            (*mats[:used], base, latest, out),
            ((rows, lanes), *([(1, rows, lanes)] if at_once else [])),
            (rows, lanes),
        )
        mats[:used] = results[:used]
        base, latest, out, value, *cross = results[used:]

        if any(urgent[tick]) or any(one[0] and one[2] > 0 for one in tasks_at(tick + 1)):
            pairs = []
            swap = [(s, s + 1) for s in range(tick & 1, count - 1, 2)]
            for a, b in swap:
                forth, back = (0 if tasks[one][0] else 1 for one in (a, b))
                if forth and back:
                    forth = back = 0
                for p in range(parts):
                    pairs += [(device(a, p), device(b, p ^ forth)), (device(b, p), device(a, p ^ back))]
            alone = [s for s in range(count) if all(s not in two for two in swap)]
            pairs += [(device(s, x), device(s, y)) for s in alone for a, b in even_pairs for x, y in ((a, b), (b, a))]
            incoming = lax.ppermute(value, ("sweep", "span"), pairs)
        came = [None if not tick or urgent[tick - 1][s] else sent[tick - 1][s] for s in range(count)]
        later = any(plan) and not at_once
        if any(came) or later:
            mats[3], mats[4], base, latest, *made = call(
                functools.partial(side_kernel, came, plan),
                "side",
                (columns[2], columns[3], *([arrived] if any(came) else [])),
                (mats[3], mats[4], base, latest),
                ((2, rows, lanes),) if later else (),
                (rows, lanes),
            )
            cross += made
        if any(plan):
            pairs = [
                (device(s, a), device(s, b))
                for s in range(count)
                if plan[s] is not None
                for a, b in (odd_pairs if plan[s][0] else even_pairs)
            ]
            arrived = lax.ppermute(cross[0], ("sweep", "span"), closed(pairs, range(count * parts)))
        if any(urgent[tick]):
            mats[3], mats[4], base = call(
                functools.partial(turn_kernel, tick + 1, vectors),
                "turn",
                (columns[2], columns[3], incoming),
                (mats[3], mats[4], base),
                (),
                (rows, lanes),
            )
        if tick < len(late_blocks):
            mats[1 + tick], base = later_call(*late_blocks[tick], base)
    return out[None, None]


def solution(mesh):
    return jax.shard_map(
        per_device,
        mesh=mesh,
        in_specs=(
            P("sweep", "span", None, None, None),
            P("sweep", "span", None, None, None),
            P("sweep", "span", None, None, None),
            P("sweep", "span", None, None, None, None),
            P("sweep", "span", None),
            P("sweep", "span", None),
            P("sweep", "span", None),
            P("sweep", "span", None),
        ),
        out_specs=P("sweep", "span", None, None, None),
        check_vma=False,
    )
```

```python
import functools

import jax
import jax.numpy as jnp
from jax import lax
from jax.experimental import pallas as pl
from jax.experimental.pallas import tpu as pltpu
from jax.sharding import PartitionSpec as P

SUBLANES = 8
VMEM_LIMIT = 2 * 1024 * 1024
PREPARE_LIMIT = 12 * 1024 * 1024
LATERAL_START = 4
CHUNKS = 4
DIAG, UP, DOWN, LEFT, RIGHT = range(5)


def task_at(tick, place, count, vectors, choose=jnp.where):
    forward = ((tick - place) & 1) == 0
    rank = choose(forward, place, count - 1 - place)
    since = tick - rank - choose(forward, 0, count)
    late = since >= 2 * count
    since = choose(late, since - 2 * count, since)
    active = (since >= 0) & (since < 2 * vectors)
    half = choose(forward, 0, 1) + choose(late, 2, 0)
    return active, choose(active, since >> 1, 0), rank, forward, half


def turns(task):
    active, _, rank, _, half = task
    return active & (rank == 0) & (half > 0)


def lateral_plan(count, vectors):
    ticks = 4 * count + 2 * (vectors - 1)
    sent = [[None] * count for _ in range(ticks)]
    urgent = [[False] * count for _ in range(ticks)]
    for slab in range(count):
        left = ([], [])
        for half in range(3):
            rank = count - 1 - slab if half & 1 else slab
            for vector in range(vectors):
                made = 2 * vector + half * count + rank
                used = 2 * vector + (half + 1) * count + count - 1 - rank
                if used == made + 1:
                    sent[made][slab] = (1, (vector,))
                    urgent[made][slab] = True
                    continue
                left[1].append((used, made, vector))
                if used == made + 3:
                    sent[made + 1][slab] = (0, (vector,))
                else:
                    left[0].append((used, made, vector))
        for tick in range(LATERAL_START, ticks, 2):
            ready = [sorted(one for one in waiting if one[1] <= tick)[:2] for waiting in left]
            if not any(ready):
                continue
            pairs = 0 if ready[0] and (not ready[1] or ready[0][0][0] <= ready[1][0][0]) else 1
            assert tick <= ready[pairs][0][0] - 2
            sent[tick][slab] = (pairs, tuple(one[2] for one in ready[pairs]))
            for one in ready[pairs]:
                left[pairs].remove(one)
        assert not any(left)
    return sent, urgent


def numbers(plan, entry):
    if entry < 0:
        return [-1 if one is None else one[0] for one in plan]
    return [-1 if one is None or len(one[1]) <= entry else one[1][entry] for one in plan]


def pick(values, place):
    result = jnp.int32(values[0])
    for at, value in enumerate(values):
        if value != values[0]:
            result = jnp.where(place == at, value, result)
    return result


def product(matrix, vector, rows):
    count = matrix.shape[0]
    group = 3 * SUBLANES

    def add(first, amount, total):
        tile = vector[pl.ds(first, SUBLANES), :]
        for row in range(amount):
            total = total + matrix[first + row] * tile[row : row + 1, :]
        return total

    def body(step, total):
        for n in range(0, group, SUBLANES):
            total = add(pl.multiple_of(step * group + n, SUBLANES), SUBLANES, total)
        return total

    total = lax.fori_loop(0, count // group, body, jnp.zeros((rows, matrix.shape[2]), jnp.float32))
    for first in range(count - count % group, count, SUBLANES):
        total = add(first, min(SUBLANES, count - first), total)
    return total


def gathered(value, columns):
    index = jnp.broadcast_to(columns, value.shape)
    return jnp.take_along_axis(value, index, axis=1, mode="promise_in_bounds")


def take_lateral(base, vector, blocks, left_cols, right_cols, arrived, spare, pairs):
    part = lax.axis_index("span")
    on_right = (part & 1) == pairs

    @pl.when(jnp.where(on_right, part < lax.axis_size("span") - 1, part > 0))
    def _():
        spare[...] = gathered(arrived, jnp.where(on_right, right_cols[...], left_cols[...]))
        base[vector] = base[vector] - product(blocks.at[jnp.where(on_right, RIGHT, LEFT)], spare, spare.shape[0])


def prepare(block, ready, narrow, wide, sems):
    size, _, lanes = block.shape
    rows = ready.shape[1]
    share = size // CHUNKS
    copies = [
        pltpu.make_async_copy(block.at[pl.ds(n * share, share)], narrow.at[pl.ds(n * share, share)], sems.at[n])
        for n in range(CHUNKS)
    ]
    for copy in copies:
        copy.start()
    wide[pl.ds(size * rows, (rows - size) * rows), :] = jnp.zeros(((rows - size) * rows, lanes), jnp.float32)

    def widen(i, _):
        wide[pl.ds(pl.multiple_of(i * rows, SUBLANES), size), :] = narrow[i].astype(jnp.float32)
        return 0

    for n, copy in enumerate(copies):
        copy.wait()
        lax.fori_loop(n * share, (n + 1) * share, widen, 0, unroll=5)

    def turn(j, _):
        for i in range(0, rows, SUBLANES):
            ready[j, pl.ds(i, SUBLANES), :] = wide[pl.ds(i * rows + j, SUBLANES, stride=rows), :]
        return 0

    lax.fori_loop(0, size, turn, 0, unroll=4)


def first_kernel(block, residual, *refs):
    hbm_columns, (blocks, base, source, blank, *columns), (narrow, wide, sems, column_sems) = (
        refs[:4], refs[4:12], refs[12:]
    )
    copies = [
        pltpu.make_async_copy(there, here, column_sems.at[n])
        for n, (there, here) in enumerate(zip(hbm_columns, columns))
    ]
    for copy in copies:
        copy.start()
    prepare(block, blocks.at[DIAG], narrow, wide, sems)
    vectors, size, lanes = residual.shape
    rows = base.shape[1]
    base[:, pl.ds(rows - SUBLANES, SUBLANES), :] = jnp.zeros((vectors, SUBLANES, lanes), jnp.float32)
    base[:, pl.ds(0, size), :] = residual[...]
    source[...] = base[...]
    blank[...] = jnp.zeros_like(blank)
    for copy in copies:
        copy.wait()


def later_kernel(face, slot, block, blocks_in, blocks, narrow, wide, sems):
    prepare(block.at[(0,) * (len(block.shape) - 4) + (face,)], blocks.at[slot], narrow, wide, sems)


def task_kernel(
    tick, tasks, sent, columns_and_inputs, kept, values, spare
):
    up_cols, down_cols, left_cols, right_cols, source, incoming, arrived = columns_and_inputs
    value, *cross = values
    blocks, base, latest, out = kept
    rows = spare.shape[0]
    vectors, size, _ = out.shape
    place = lax.axis_index("sweep")
    task = task_at(tick, place, lax.axis_size("sweep"), vectors)
    active, vector, rank, forward, half = task

    if any(turns(one) for one in tasks):

        @pl.when(turns(task))
        def _():
            take_lateral(base, vector, blocks, left_cols, right_cols, arrived[0], spare, 1)

    @pl.when(active)
    def _():
        known = base[vector]
        value[...] = known
        base[vector] = source[vector]

        if any(one[0] and one[2] > 0 for one in tasks):

            @pl.when(rank > 0)
            def _():
                spare[...] = gathered(incoming[...], jnp.where(forward, up_cols[...], down_cols[...]))
                term = product(blocks.at[jnp.where(forward, UP, DOWN)], spare, rows)
                value[...] = known - term
                base[vector] = source[vector] - term

        spare[...] = value[...]
        fresh = product(blocks.at[DIAG], spare, rows)
        value[...] = fresh
        latest[vector] = fresh

        if any(one[0] and one[4] == 3 for one in tasks):

            @pl.when(half == 3)
            def _():
                out[vector] = fresh[:size]

    if cross:
        fill(cross[0], latest, sent, place)


def fill(cross, latest, plan, place):
    for entry in range(cross.shape[0]):
        chosen = numbers(plan, entry)
        if any(one >= 0 for one in chosen):
            vector = pick(chosen, place)

            @pl.when(vector >= 0)
            def _():
                cross[entry] = latest[vector]


def side_kernel(came, plan, columns_and_inputs, kept, values, spare):
    left_cols, right_cols, *arrived = columns_and_inputs
    blocks, base, latest = kept
    place = lax.axis_index("sweep")
    if values:
        fill(values[0], latest, plan, place)
    if arrived:
        pairs = pick(numbers(came, -1), place)
        for entry in range(arrived[0].shape[0]):
            chosen = numbers(came, entry)
            if any(one >= 0 for one in chosen):
                vector = pick(chosen, place)

                @pl.when(vector >= 0)
                def _():
                    take_lateral(
                        base, vector, blocks, left_cols, right_cols, arrived[0][entry], spare, pairs
                    )


def turn_kernel(tick, vectors, columns_and_inputs, kept, values, spare):
    left_cols, right_cols, incoming = columns_and_inputs
    blocks, base = kept
    task = task_at(tick, lax.axis_index("sweep"), lax.axis_size("sweep"), vectors)

    @pl.when(turns(task))
    def _():
        take_lateral(base, task[1], blocks, left_cols, right_cols, incoming[...], spare, 0)


def in_vmem(count):
    return [pl.BlockSpec(memory_space=pltpu.VMEM)] * count


def far(array):
    return pltpu.with_memory_space_constraint(array, pltpu.HBM)


def held(shape):
    return pltpu.VMEM(shape, jnp.float32)


def call(kernel, name, fixed, kept, fresh, spare):
    def body(*refs):
        inputs, outputs = refs[: len(fixed)], refs[len(fixed) + len(kept) : -1]
        kernel(inputs, outputs[: len(kept)], outputs[len(kept) :], refs[-1])

    return pl.pallas_call(
        body,
        out_shape=tuple(held(shape) for shape in [*(a.shape for a in kept), *fresh]),
        in_specs=in_vmem(len(fixed) + len(kept)),
        out_specs=tuple(in_vmem(len(fresh) + len(kept))),
        scratch_shapes=[held(spare)],
        input_output_aliases={len(fixed) + n: n for n in range(len(kept))},
        compiler_params=pltpu.CompilerParams(vmem_limit_bytes=VMEM_LIMIT),
        name=name,
    )(*fixed, *kept)


def preparing(size, rows, lanes):
    return [
        pltpu.VMEM((size, size, lanes), jnp.bfloat16),
        held((rows * rows, lanes)),
        pltpu.SemaphoreType.DMA((CHUNKS,)),
    ]


def first_call(block, residual, columns, rows):
    vectors, size, lanes = residual.shape
    several = (vectors, rows, lanes)
    in_hbm = pl.BlockSpec(memory_space=pltpu.HBM)
    return pl.pallas_call(
        first_kernel,
        out_shape=(
            held((5, size, rows, lanes)), held(several), held(several), held((rows, lanes)),
            *(pltpu.VMEM(one.shape, one.dtype) for one in columns),
        ),
        in_specs=[in_hbm, *in_vmem(1), *[in_hbm] * 4],
        out_specs=tuple(in_vmem(8)),
        scratch_shapes=[*preparing(size, rows, lanes), pltpu.SemaphoreType.DMA((4,))],
        compiler_params=pltpu.CompilerParams(vmem_limit_bytes=PREPARE_LIMIT),
        name="first",
    )(far(block), residual, *(far(one) for one in columns))


def later_call(block, face, slot, blocks):
    return pl.pallas_call(
        functools.partial(later_kernel, face, slot),
        out_shape=held(blocks.shape),
        in_specs=[pl.BlockSpec(memory_space=pltpu.HBM), *in_vmem(1)],
        out_specs=in_vmem(1)[0],
        scratch_shapes=preparing(*blocks.shape[1:]),
        input_output_aliases={1: 0},
        compiler_params=pltpu.CompilerParams(vmem_limit_bytes=PREPARE_LIMIT),
        name="later",
    )(far(block), blocks)


def per_device(
    residual_in, diag_inverse, up_block, side_blocks, up_cols, down_cols, left_cols, right_cols
):
    vectors, size, lanes = residual_in.shape[2:]
    rows = size + -size % SUBLANES
    columns = [one.reshape(1, lanes) for one in (up_cols, down_cols, left_cols, right_cols)]
    count = lax.axis_size("sweep")
    parts = lax.axis_size("span")
    ticks = 4 * count + 2 * (vectors - 1)
    sent, urgent = lateral_plan(count, vectors)
    even_pairs = [(p, p + 1) for p in range(0, parts - 1, 2)]
    odd_pairs = [(p, p + 1) for p in range(1, parts - 1, 2)]

    def closed(pairs, members):
        alone = [one for one in members if all(one not in two for two in pairs)]
        return [*pairs, *((b, a) for a, b in pairs), *((one, one) for one in alone)]

    def device(slab, part):
        return slab * parts + part

    blocks, base, source, blank, *columns = first_call(diag_inverse[0, 0], residual_in[0, 0], columns, rows)
    latest, out = pl.pallas_call(
        lambda *refs: None,
        out_shape=(held((vectors, rows, lanes)), held((vectors, size, lanes))),
        out_specs=tuple(in_vmem(2)),
        name="room",
    )()
    incoming = arrived = blank
    late_blocks = [(up_block, 0, UP), *((side_blocks, face, DOWN + face) for face in range(3))]

    def tasks_at(tick):
        return [task_at(tick, place, count, vectors, lambda which, a, b: a if which else b) for place in range(count)]

    for tick in range(ticks):
        tasks = tasks_at(tick)
        plan = sent[tick]
        turning = any(turns(one) for one in tasks)
        at_once = any(plan) and tick & 1 == 1
        blocks, base, latest, out, value, *cross = call(
            functools.partial(task_kernel, tick, tasks, plan),
            "task",
            (*columns, source, incoming, arrived if turning else blank),
            (blocks, base, latest, out),
            ((rows, lanes), *([(1, rows, lanes)] if at_once else [])),
            (rows, lanes),
        )

        if any(urgent[tick]) or any(one[0] and one[2] > 0 for one in tasks_at(tick + 1)):
            pairs = []
            swap = [(s, s + 1) for s in range(tick & 1, count - 1, 2)]
            for a, b in swap:
                forth, back = (0 if tasks[one][0] else 1 for one in (a, b))
                if forth and back:
                    forth = back = 0
                for p in range(parts):
                    pairs += [(device(a, p), device(b, p ^ forth)), (device(b, p), device(a, p ^ back))]
            alone = [s for s in range(count) if all(s not in two for two in swap)]
            pairs += [(device(s, x), device(s, y)) for s in alone for a, b in even_pairs for x, y in ((a, b), (b, a))]
            incoming = lax.ppermute(value, ("sweep", "span"), pairs)
        came = [None if not tick or urgent[tick - 1][s] else sent[tick - 1][s] for s in range(count)]
        later = any(plan) and not at_once
        if any(came) or later:
            blocks, base, latest, *made = call(
                functools.partial(side_kernel, came, plan),
                "side",
                (columns[2], columns[3], *([arrived] if any(came) else [])),
                (blocks, base, latest),
                ((2, rows, lanes),) if later else (),
                (rows, lanes),
            )
            cross += made
        if any(plan):
            pairs = [
                (device(s, a), device(s, b))
                for s in range(count)
                if plan[s] is not None
                for a, b in (odd_pairs if plan[s][0] else even_pairs)
            ]
            arrived = lax.ppermute(cross[0], ("sweep", "span"), closed(pairs, range(count * parts)))
        if any(urgent[tick]):
            blocks, base = call(
                functools.partial(turn_kernel, tick + 1, vectors),
                "turn",
                (columns[2], columns[3], incoming),
                (blocks, base),
                (),
                (rows, lanes),
            )
        if tick < len(late_blocks):
            blocks = later_call(*late_blocks[tick], blocks)
    return out[None, None]


def solution(mesh):
    return jax.shard_map(
        per_device,
        mesh=mesh,
        in_specs=(
            P("sweep", "span", None, None, None),
            P("sweep", "span", None, None, None),
            P("sweep", "span", None, None, None),
            P("sweep", "span", None, None, None, None),
            P("sweep", "span", None),
            P("sweep", "span", None),
            P("sweep", "span", None),
            P("sweep", "span", None),
        ),
        out_specs=P("sweep", "span", None, None, None),
        check_vma=False,
    )
```

```python
import functools

import jax
import jax.numpy as jnp
from jax import lax
from jax.experimental import pallas as pl
from jax.experimental.pallas import tpu as pltpu
from jax.sharding import PartitionSpec as P

SUBLANES = 8
VMEM_LIMIT = 2 * 1024 * 1024
PREPARE_LIMIT = 12 * 1024 * 1024
LATERAL_START = 4
CHUNKS = 4
DIAG, UP, DOWN, LEFT, RIGHT = range(5)


def task_at(tick, place, count, vectors, choose=jnp.where):
    forward = ((tick - place) & 1) == 0
    rank = choose(forward, place, count - 1 - place)
    since = tick - rank - choose(forward, 0, count)
    late = since >= 2 * count
    since = choose(late, since - 2 * count, since)
    active = (since >= 0) & (since < 2 * vectors)
    half = choose(forward, 0, 1) + choose(late, 2, 0)
    return active, choose(active, since >> 1, 0), rank, forward, half


def turns(task):
    active, _, rank, _, half = task
    return active & (rank == 0) & (half > 0)


def lateral_plan(count, vectors):
    ticks = 4 * count + 2 * (vectors - 1)
    sent = [[None] * count for _ in range(ticks)]
    urgent = [[False] * count for _ in range(ticks)]
    for slab in range(count):
        left = ([], [])
        for half in range(3):
            rank = count - 1 - slab if half & 1 else slab
            for vector in range(vectors):
                made = 2 * vector + half * count + rank
                used = 2 * vector + (half + 1) * count + count - 1 - rank
                if used == made + 1:
                    sent[made][slab] = (1, (vector,))
                    urgent[made][slab] = True
                    continue
                left[1].append((used, made, vector))
                if used == made + 3:
                    sent[made + 1][slab] = (0, (vector,))
                else:
                    left[0].append((used, made, vector))
        for tick in range(LATERAL_START, ticks, 2):
            ready = [sorted(one for one in waiting if one[1] <= tick)[:2] for waiting in left]
            if not any(ready):
                continue
            pairs = 0 if ready[0] and (not ready[1] or ready[0][0][0] <= ready[1][0][0]) else 1
            assert tick <= ready[pairs][0][0] - 2
            sent[tick][slab] = (pairs, tuple(one[2] for one in ready[pairs]))
            for one in ready[pairs]:
                left[pairs].remove(one)
        assert not any(left)
    return sent, urgent


def numbers(plan, entry):
    if entry < 0:
        return [-1 if one is None else one[0] for one in plan]
    return [-1 if one is None or len(one[1]) <= entry else one[1][entry] for one in plan]


def pick(values, place):
    result = jnp.int32(values[0])
    for at, value in enumerate(values):
        if value != values[0]:
            result = jnp.where(place == at, value, result)
    return result


def product(matrix, vector, rows):
    count = matrix.shape[0]
    group = 3 * SUBLANES

    def add(first, amount, total):
        tile = vector[pl.ds(first, SUBLANES), :]
        for row in range(amount):
            total = total + matrix[first + row] * tile[row : row + 1, :]
        return total

    def body(step, total):
        for n in range(0, group, SUBLANES):
            total = add(pl.multiple_of(step * group + n, SUBLANES), SUBLANES, total)
        return total

    total = lax.fori_loop(0, count // group, body, jnp.zeros((rows, matrix.shape[2]), jnp.float32))
    for first in range(count - count % group, count, SUBLANES):
        total = add(first, min(SUBLANES, count - first), total)
    return total


def gathered(value, columns):
    index = jnp.broadcast_to(columns, value.shape)
    return jnp.take_along_axis(value, index, axis=1, mode="promise_in_bounds")


def take_lateral(base, vector, blocks, left_cols, right_cols, arrived, spare, pairs):
    part = lax.axis_index("span")
    on_right = (part & 1) == pairs

    @pl.when(jnp.where(on_right, part < lax.axis_size("span") - 1, part > 0))
    def _():
        spare[...] = gathered(arrived, jnp.where(on_right, right_cols[...], left_cols[...]))
        base[vector] = base[vector] - product(blocks.at[jnp.where(on_right, RIGHT, LEFT)], spare, spare.shape[0])


def prepare(block, ready, narrow, wide, sems):
    size, _, lanes = block.shape
    rows = ready.shape[1]
    share = size // CHUNKS
    copies = [
        pltpu.make_async_copy(block.at[pl.ds(n * share, share)], narrow.at[pl.ds(n * share, share)], sems.at[n])
        for n in range(CHUNKS)
    ]
    for copy in copies:
        copy.start()
    wide[pl.ds(size * rows, (rows - size) * rows), :] = jnp.zeros(((rows - size) * rows, lanes), jnp.float32)

    def widen(i, _):
        wide[pl.ds(pl.multiple_of(i * rows, SUBLANES), size), :] = narrow[i].astype(jnp.float32)
        return 0

    for n, copy in enumerate(copies):
        copy.wait()
        lax.fori_loop(n * share, (n + 1) * share, widen, 0, unroll=5)

    def turn(j, _):
        for i in range(0, rows, SUBLANES):
            ready[j, pl.ds(i, SUBLANES), :] = wide[pl.ds(i * rows + j, SUBLANES, stride=rows), :]
        return 0

    lax.fori_loop(0, size, turn, 0, unroll=4)


def first_kernel(block, residual, *refs):
    hbm_columns, (blocks, base, source, blank, *columns), (narrow, wide, sems, column_sems) = (
        refs[:4], refs[4:12], refs[12:]
    )
    copies = [
        pltpu.make_async_copy(there, here, column_sems.at[n])
        for n, (there, here) in enumerate(zip(hbm_columns, columns))
    ]
    for copy in copies:
        copy.start()
    prepare(block, blocks.at[DIAG], narrow, wide, sems)
    vectors, size, lanes = residual.shape
    rows = base.shape[1]
    base[:, pl.ds(rows - SUBLANES, SUBLANES), :] = jnp.zeros((vectors, SUBLANES, lanes), jnp.float32)
    base[:, pl.ds(0, size), :] = residual[...]
    source[...] = base[...]
    blank[...] = jnp.zeros_like(blank)
    for copy in copies:
        copy.wait()


def later_kernel(face, slot, block, blocks_in, blocks, narrow, wide, sems):
    prepare(block.at[(0,) * (len(block.shape) - 4) + (face,)], blocks.at[slot], narrow, wide, sems)


def task_kernel(
    tick, tasks, sent, columns_and_inputs, kept, values, spare
):
    up_cols, down_cols, left_cols, right_cols, source, incoming, arrived = columns_and_inputs
    value, *cross = values
    blocks, base, latest, out = kept
    rows = spare.shape[0]
    vectors, size, _ = out.shape
    place = lax.axis_index("sweep")
    task = task_at(tick, place, lax.axis_size("sweep"), vectors)
    active, vector, rank, forward, half = task

    if any(turns(one) for one in tasks):

        @pl.when(turns(task))
        def _():
            take_lateral(base, vector, blocks, left_cols, right_cols, arrived[0], spare, 1)

    @pl.when(active)
    def _():
        known = base[vector]
        value[...] = known
        base[vector] = source[vector]

        if any(one[0] and one[2] > 0 for one in tasks):

            @pl.when(rank > 0)
            def _():
                spare[...] = gathered(incoming[...], jnp.where(forward, up_cols[...], down_cols[...]))
                term = product(blocks.at[jnp.where(forward, UP, DOWN)], spare, rows)
                value[...] = known - term
                base[vector] = source[vector] - term

        spare[...] = value[...]
        fresh = product(blocks.at[DIAG], spare, rows)
        value[...] = fresh
        latest[vector] = fresh

        if any(one[0] and one[4] == 3 for one in tasks):

            @pl.when(half == 3)
            def _():
                out[vector] = fresh[:size]

    if cross:
        fill(cross[0], latest, sent, place)


def fill(cross, latest, plan, place):
    for entry in range(cross.shape[0]):
        chosen = numbers(plan, entry)
        if any(one >= 0 for one in chosen):
            vector = pick(chosen, place)

            @pl.when(vector >= 0)
            def _():
                cross[entry] = latest[vector]


def side_kernel(came, columns_and_inputs, kept, values, spare):
    left_cols, right_cols, arrived = columns_and_inputs
    blocks, base = kept
    place = lax.axis_index("sweep")
    pairs = pick(numbers(came, -1), place)
    for entry in range(arrived.shape[0]):
        chosen = numbers(came, entry)
        if any(one >= 0 for one in chosen):
            vector = pick(chosen, place)

            @pl.when(vector >= 0)
            def _():
                take_lateral(base, vector, blocks, left_cols, right_cols, arrived[entry], spare, pairs)


def turn_kernel(tick, vectors, columns_and_inputs, kept, values, spare):
    left_cols, right_cols, incoming = columns_and_inputs
    blocks, base = kept
    task = task_at(tick, lax.axis_index("sweep"), lax.axis_size("sweep"), vectors)

    @pl.when(turns(task))
    def _():
        take_lateral(base, task[1], blocks, left_cols, right_cols, incoming[...], spare, 0)


def in_vmem(count):
    return [pl.BlockSpec(memory_space=pltpu.VMEM)] * count


def far(array):
    return pltpu.with_memory_space_constraint(array, pltpu.HBM)


def held(shape):
    return pltpu.VMEM(shape, jnp.float32)


def call(kernel, name, fixed, kept, fresh, spare):
    def body(*refs):
        inputs, outputs = refs[: len(fixed)], refs[len(fixed) + len(kept) : -1]
        kernel(inputs, outputs[: len(kept)], outputs[len(kept) :], refs[-1])

    return pl.pallas_call(
        body,
        out_shape=tuple(held(shape) for shape in [*(a.shape for a in kept), *fresh]),
        in_specs=in_vmem(len(fixed) + len(kept)),
        out_specs=tuple(in_vmem(len(fresh) + len(kept))),
        scratch_shapes=[held(spare)],
        input_output_aliases={len(fixed) + n: n for n in range(len(kept))},
        compiler_params=pltpu.CompilerParams(vmem_limit_bytes=VMEM_LIMIT),
        name=name,
    )(*fixed, *kept)


def preparing(size, rows, lanes):
    return [
        pltpu.VMEM((size, size, lanes), jnp.bfloat16),
        held((rows * rows, lanes)),
        pltpu.SemaphoreType.DMA((CHUNKS,)),
    ]


def first_call(block, residual, columns, rows):
    vectors, size, lanes = residual.shape
    several = (vectors, rows, lanes)
    in_hbm = pl.BlockSpec(memory_space=pltpu.HBM)
    return pl.pallas_call(
        first_kernel,
        out_shape=(
            held((5, size, rows, lanes)), held(several), held(several), held((rows, lanes)),
            *(pltpu.VMEM(one.shape, one.dtype) for one in columns),
        ),
        in_specs=[in_hbm, *in_vmem(1), *[in_hbm] * 4],
        out_specs=tuple(in_vmem(8)),
        scratch_shapes=[*preparing(size, rows, lanes), pltpu.SemaphoreType.DMA((4,))],
        compiler_params=pltpu.CompilerParams(vmem_limit_bytes=PREPARE_LIMIT),
        name="first",
    )(far(block), residual, *(far(one) for one in columns))


def later_call(block, face, slot, blocks):
    return pl.pallas_call(
        functools.partial(later_kernel, face, slot),
        out_shape=held(blocks.shape),
        in_specs=[pl.BlockSpec(memory_space=pltpu.HBM), *in_vmem(1)],
        out_specs=in_vmem(1)[0],
        scratch_shapes=preparing(*blocks.shape[1:]),
        input_output_aliases={1: 0},
        compiler_params=pltpu.CompilerParams(vmem_limit_bytes=PREPARE_LIMIT),
        name="later",
    )(far(block), blocks)


def per_device(
    residual_in, diag_inverse, up_block, side_blocks, up_cols, down_cols, left_cols, right_cols
):
    vectors, size, lanes = residual_in.shape[2:]
    rows = size + -size % SUBLANES
    columns = [one.reshape(1, lanes) for one in (up_cols, down_cols, left_cols, right_cols)]
    count = lax.axis_size("sweep")
    parts = lax.axis_size("span")
    ticks = 4 * count + 2 * (vectors - 1)
    sent, urgent = lateral_plan(count, vectors)
    even_pairs = [(p, p + 1) for p in range(0, parts - 1, 2)]
    odd_pairs = [(p, p + 1) for p in range(1, parts - 1, 2)]

    def closed(pairs, members):
        alone = [one for one in members if all(one not in two for two in pairs)]
        return [*pairs, *((b, a) for a, b in pairs), *((one, one) for one in alone)]

    def device(slab, part):
        return slab * parts + part

    blocks, base, source, blank, *columns = first_call(diag_inverse[0, 0], residual_in[0, 0], columns, rows)
    latest, out = pl.pallas_call(
        lambda *refs: None,
        out_shape=(held((vectors, rows, lanes)), held((vectors, size, lanes))),
        out_specs=tuple(in_vmem(2)),
        name="room",
    )()
    incoming = arrived = blank
    late_blocks = [(up_block, 0, UP), *((side_blocks, face, DOWN + face) for face in range(3))]

    def tasks_at(tick):
        return [task_at(tick, place, count, vectors, lambda which, a, b: a if which else b) for place in range(count)]

    for tick in range(ticks):
        tasks = tasks_at(tick)
        plan = sent[tick]
        turning = any(turns(one) for one in tasks)
        blocks, base, latest, out, value, *cross = call(
            functools.partial(task_kernel, tick, tasks, plan),
            "task",
            (*columns, source, incoming, arrived if turning else blank),
            (blocks, base, latest, out),
            ((rows, lanes), *([(1 if tick & 1 else 2, rows, lanes)] if any(plan) else [])),
            (rows, lanes),
        )

        if any(urgent[tick]) or any(one[0] and one[2] > 0 for one in tasks_at(tick + 1)):
            pairs = []
            swap = [(s, s + 1) for s in range(tick & 1, count - 1, 2)]
            for a, b in swap:
                forth, back = (0 if tasks[one][0] else 1 for one in (a, b))
                if forth and back:
                    forth = back = 0
                for p in range(parts):
                    pairs += [(device(a, p), device(b, p ^ forth)), (device(b, p), device(a, p ^ back))]
            alone = [s for s in range(count) if all(s not in two for two in swap)]
            pairs += [(device(s, x), device(s, y)) for s in alone for a, b in even_pairs for x, y in ((a, b), (b, a))]
            incoming = lax.ppermute(value, ("sweep", "span"), pairs)
        came = [None if not tick or urgent[tick - 1][s] else sent[tick - 1][s] for s in range(count)]
        if any(came):
            blocks, base = call(
                functools.partial(side_kernel, came),
                "side",
                (columns[2], columns[3], arrived),
                (blocks, base),
                (),
                (rows, lanes),
            )
        if any(plan):
            pairs = [
                (device(s, a), device(s, b))
                for s in range(count)
                if plan[s] is not None
                for a, b in (odd_pairs if plan[s][0] else even_pairs)
            ]
            arrived = lax.ppermute(cross[0], ("sweep", "span"), closed(pairs, range(count * parts)))
        if any(urgent[tick]):
            blocks, base = call(
                functools.partial(turn_kernel, tick + 1, vectors),
                "turn",
                (columns[2], columns[3], incoming),
                (blocks, base),
                (),
                (rows, lanes),
            )
        if tick < len(late_blocks):
            blocks = later_call(*late_blocks[tick], blocks)
    return out[None, None]


def solution(mesh):
    return jax.shard_map(
        per_device,
        mesh=mesh,
        in_specs=(
            P("sweep", "span", None, None, None),
            P("sweep", "span", None, None, None),
            P("sweep", "span", None, None, None),
            P("sweep", "span", None, None, None, None),
            P("sweep", "span", None),
            P("sweep", "span", None),
            P("sweep", "span", None),
            P("sweep", "span", None),
        ),
        out_specs=P("sweep", "span", None, None, None),
        check_vma=False,
    )
```

```python
import functools

import jax
import jax.numpy as jnp
from jax import lax
from jax.experimental import pallas as pl
from jax.experimental.pallas import tpu as pltpu
from jax.sharding import PartitionSpec as P

SUBLANES = 8
VMEM_LIMIT = 2 * 1024 * 1024
PREPARE_LIMIT = 12 * 1024 * 1024
LATERAL_START = 4
CHUNKS = 4
DIAG, UP, DOWN, LEFT, RIGHT = range(5)


def task_at(tick, place, count, vectors, choose=jnp.where):
    forward = ((tick - place) & 1) == 0
    rank = choose(forward, place, count - 1 - place)
    since = tick - rank - choose(forward, 0, count)
    late = since >= 2 * count
    since = choose(late, since - 2 * count, since)
    active = (since >= 0) & (since < 2 * vectors)
    half = choose(forward, 0, 1) + choose(late, 2, 0)
    return active, choose(active, since >> 1, 0), rank, forward, half


def turns(task):
    active, _, rank, _, half = task
    return active & (rank == 0) & (half > 0)


def lateral_plan(count, vectors):
    ticks = 4 * count + 2 * (vectors - 1)
    sent = [[None] * count for _ in range(ticks)]
    urgent = [[False] * count for _ in range(ticks)]
    for slab in range(count):
        fixed, waiting, busy = [], ([], []), set()
        for half in range(4):
            rank = count - 1 - slab if half & 1 else slab
            for vector in range(vectors):
                made = 2 * vector + half * count + rank
                used = 2 * vector + (half + 1) * count + count - 1 - rank
                busy.add(made)
                if half == 3:
                    continue
                if used == made + 1:
                    fixed.append((made, (1, (vector,))))
                    urgent[made][slab] = True
                    continue
                waiting[1].append((used, made, vector))
                if used == made + 3:
                    fixed.append((made + 1, (0, (vector,))))
                else:
                    waiting[0].append((used, made, vector))
        even = range(LATERAL_START, ticks, 2)
        found = in_order(waiting, [tick for tick in even if tick not in busy]) or in_order(waiting, even)
        for tick, one in (*fixed, *found):
            sent[tick][slab] = one
    return sent, urgent


def in_order(waiting, slots):
    left = tuple(list(kind) for kind in waiting)
    found = []
    for tick in slots:
        ready = [sorted(one for one in kind if one[1] <= tick)[:2] for kind in left]
        if not any(ready):
            continue
        pairs = 0 if ready[0] and (not ready[1] or ready[0][0][0] <= ready[1][0][0]) else 1
        if tick > ready[pairs][0][0] - 2:
            return None
        found.append((tick, (pairs, tuple(one[2] for one in ready[pairs]))))
        for one in ready[pairs]:
            left[pairs].remove(one)
    return None if any(left) else found


def numbers(plan, entry):
    if entry < 0:
        return [-1 if one is None else one[0] for one in plan]
    return [-1 if one is None or len(one[1]) <= entry else one[1][entry] for one in plan]


def pick(values, place):
    result = jnp.int32(values[0])
    for at, value in enumerate(values):
        if value != values[0]:
            result = jnp.where(place == at, value, result)
    return result


def product(matrix, vector, rows):
    count = matrix.shape[0]
    group = 3 * SUBLANES

    def add(first, amount, total):
        tile = vector[pl.ds(first, SUBLANES), :]
        for row in range(amount):
            total = total + matrix[first + row] * tile[row : row + 1, :]
        return total

    def body(step, total):
        for n in range(0, group, SUBLANES):
            total = add(pl.multiple_of(step * group + n, SUBLANES), SUBLANES, total)
        return total

    total = lax.fori_loop(0, count // group, body, jnp.zeros((rows, matrix.shape[2]), jnp.float32))
    for first in range(count - count % group, count, SUBLANES):
        total = add(first, min(SUBLANES, count - first), total)
    return total


def gathered(value, columns):
    index = jnp.broadcast_to(columns, value.shape)
    return jnp.take_along_axis(value, index, axis=1, mode="promise_in_bounds")


def take_lateral(base, vector, blocks, left_cols, right_cols, arrived, spare, pairs):
    part = lax.axis_index("span")
    on_right = (part & 1) == pairs

    @pl.when(jnp.where(on_right, part < lax.axis_size("span") - 1, part > 0))
    def _():
        spare[...] = gathered(arrived, jnp.where(on_right, right_cols[...], left_cols[...]))
        base[vector] = base[vector] - product(blocks.at[jnp.where(on_right, RIGHT, LEFT)], spare, spare.shape[0])


def prepare(block, ready, narrow, wide, sems):
    size, _, lanes = block.shape
    rows = ready.shape[1]
    share = size // CHUNKS
    copies = [
        pltpu.make_async_copy(block.at[pl.ds(n * share, share)], narrow.at[pl.ds(n * share, share)], sems.at[n])
        for n in range(CHUNKS)
    ]
    for copy in copies:
        copy.start()
    wide[pl.ds(size * rows, (rows - size) * rows), :] = jnp.zeros(((rows - size) * rows, lanes), jnp.float32)

    def widen(i, _):
        wide[pl.ds(pl.multiple_of(i * rows, SUBLANES), size), :] = narrow[i].astype(jnp.float32)
        return 0

    for n, copy in enumerate(copies):
        copy.wait()
        lax.fori_loop(n * share, (n + 1) * share, widen, 0, unroll=5)

    def turn(j, _):
        for i in range(0, rows, SUBLANES):
            ready[j, pl.ds(i, SUBLANES), :] = wide[pl.ds(i * rows + j, SUBLANES, stride=rows), :]
        return 0

    lax.fori_loop(0, size, turn, 0, unroll=4)


def first_kernel(block, residual, *refs):
    hbm_columns, (blocks, base, source, blank, *columns), (narrow, wide, sems, column_sems) = (
        refs[:4], refs[4:12], refs[12:]
    )
    copies = [
        pltpu.make_async_copy(there, here, column_sems.at[n])
        for n, (there, here) in enumerate(zip(hbm_columns, columns))
    ]
    for copy in copies:
        copy.start()
    prepare(block, blocks.at[DIAG], narrow, wide, sems)
    size, vectors, lanes = residual.shape
    rows = base.shape[1]
    base[:, pl.ds(rows - SUBLANES, SUBLANES), :] = jnp.zeros((vectors, SUBLANES, lanes), jnp.float32)
    for vector in range(vectors):
        base[vector, pl.ds(0, size), :] = residual[:, vector, :]
    source[...] = base[...]
    blank[...] = jnp.zeros_like(blank)
    for copy in copies:
        copy.wait()


def later_kernel(face, slot, block, blocks_in, blocks, narrow, wide, sems):
    prepare(block.at[(0,) * (len(block.shape) - 4) + (face,)], blocks.at[slot], narrow, wide, sems)


def task_kernel(
    tick, tasks, sent, columns_and_inputs, kept, values, spare
):
    up_cols, down_cols, left_cols, right_cols, source, incoming, arrived = columns_and_inputs
    value, *cross = values
    blocks, base, latest, out = kept
    rows = spare.shape[0]
    vectors, size, _ = out.shape
    place = lax.axis_index("sweep")
    task = task_at(tick, place, lax.axis_size("sweep"), vectors)
    active, vector, rank, forward, half = task

    if any(turns(one) for one in tasks):

        @pl.when(turns(task))
        def _():
            take_lateral(base, vector, blocks, left_cols, right_cols, arrived[0], spare, 1)

    @pl.when(active)
    def _():
        known = base[vector]
        value[...] = known
        base[vector] = source[vector]

        if any(one[0] and one[2] > 0 for one in tasks):

            @pl.when(rank > 0)
            def _():
                spare[...] = gathered(incoming[...], jnp.where(forward, up_cols[...], down_cols[...]))
                term = product(blocks.at[jnp.where(forward, UP, DOWN)], spare, rows)
                value[...] = known - term
                base[vector] = source[vector] - term

        spare[...] = value[...]
        fresh = product(blocks.at[DIAG], spare, rows)
        value[...] = fresh
        latest[vector] = fresh

        if any(one[0] and one[4] == 3 for one in tasks):

            @pl.when(half == 3)
            def _():
                out[vector] = fresh[:size]

    if cross:
        fill(cross[0], latest, sent, place)


def fill(cross, latest, plan, place):
    for entry in range(cross.shape[0]):
        chosen = numbers(plan, entry)
        if any(one >= 0 for one in chosen):
            vector = pick(chosen, place)

            @pl.when(vector >= 0)
            def _():
                cross[entry] = latest[vector]


def side_kernel(came, columns_and_inputs, kept, values, spare):
    left_cols, right_cols, arrived = columns_and_inputs
    blocks, base = kept
    place = lax.axis_index("sweep")
    pairs = pick(numbers(came, -1), place)
    for entry in range(arrived.shape[0]):
        chosen = numbers(came, entry)
        if any(one >= 0 for one in chosen):
            vector = pick(chosen, place)

            @pl.when(vector >= 0)
            def _():
                take_lateral(base, vector, blocks, left_cols, right_cols, arrived[entry], spare, pairs)


def turn_kernel(tick, vectors, columns_and_inputs, kept, values, spare):
    left_cols, right_cols, incoming = columns_and_inputs
    blocks, base = kept
    task = task_at(tick, lax.axis_index("sweep"), lax.axis_size("sweep"), vectors)

    @pl.when(turns(task))
    def _():
        take_lateral(base, task[1], blocks, left_cols, right_cols, incoming[...], spare, 0)


def in_vmem(count):
    return [pl.BlockSpec(memory_space=pltpu.VMEM)] * count


def far(array):
    return pltpu.with_memory_space_constraint(array, pltpu.HBM)


def held(shape):
    return pltpu.VMEM(shape, jnp.float32)


def call(kernel, name, fixed, kept, fresh, spare):
    def body(*refs):
        inputs, outputs = refs[: len(fixed)], refs[len(fixed) + len(kept) : -1]
        kernel(inputs, outputs[: len(kept)], outputs[len(kept) :], refs[-1])

    return pl.pallas_call(
        body,
        out_shape=tuple(held(shape) for shape in [*(a.shape for a in kept), *fresh]),
        in_specs=in_vmem(len(fixed) + len(kept)),
        out_specs=tuple(in_vmem(len(fresh) + len(kept))),
        scratch_shapes=[held(spare)],
        input_output_aliases={len(fixed) + n: n for n in range(len(kept))},
        compiler_params=pltpu.CompilerParams(vmem_limit_bytes=VMEM_LIMIT),
        name=name,
    )(*fixed, *kept)


def preparing(size, rows, lanes):
    return [
        pltpu.VMEM((size, size, lanes), jnp.bfloat16),
        held((rows * rows, lanes)),
        pltpu.SemaphoreType.DMA((CHUNKS,)),
    ]


def first_call(block, residual, columns, rows):
    size, vectors, lanes = residual.shape
    several = (vectors, rows, lanes)
    in_hbm = pl.BlockSpec(memory_space=pltpu.HBM)
    return pl.pallas_call(
        first_kernel,
        out_shape=(
            held((5, size, rows, lanes)), held(several), held(several), held((rows, lanes)),
            *(pltpu.VMEM(one.shape, one.dtype) for one in columns),
        ),
        in_specs=[in_hbm, *in_vmem(1), *[in_hbm] * 4],
        out_specs=tuple(in_vmem(8)),
        scratch_shapes=[*preparing(size, rows, lanes), pltpu.SemaphoreType.DMA((4,))],
        compiler_params=pltpu.CompilerParams(vmem_limit_bytes=PREPARE_LIMIT),
        name="first",
    )(far(block), residual, *(far(one) for one in columns))


def later_call(block, face, slot, blocks):
    return pl.pallas_call(
        functools.partial(later_kernel, face, slot),
        out_shape=held(blocks.shape),
        in_specs=[pl.BlockSpec(memory_space=pltpu.HBM), *in_vmem(1)],
        out_specs=in_vmem(1)[0],
        scratch_shapes=preparing(*blocks.shape[1:]),
        input_output_aliases={1: 0},
        compiler_params=pltpu.CompilerParams(vmem_limit_bytes=PREPARE_LIMIT),
        name="later",
    )(far(block), blocks)


def per_device(
    residual_in, diag_inverse, up_block, side_blocks, up_cols, down_cols, left_cols, right_cols
):
    vectors, size, lanes = residual_in.shape[2:]
    rows = size + -size % SUBLANES
    columns = [one.reshape(1, lanes) for one in (up_cols, down_cols, left_cols, right_cols)]
    count = lax.axis_size("sweep")
    parts = lax.axis_size("span")
    ticks = 4 * count + 2 * (vectors - 1)
    sent, urgent = lateral_plan(count, vectors)
    even_pairs = [(p, p + 1) for p in range(0, parts - 1, 2)]
    odd_pairs = [(p, p + 1) for p in range(1, parts - 1, 2)]

    def closed(pairs, members):
        alone = [one for one in members if all(one not in two for two in pairs)]
        return [*pairs, *((b, a) for a, b in pairs), *((one, one) for one in alone)]

    def device(slab, part):
        return slab * parts + part

    blocks, base, source, blank, *columns = first_call(
        diag_inverse[0, 0], jnp.transpose(residual_in[0, 0], (1, 0, 2)), columns, rows
    )
    latest, out = pl.pallas_call(
        lambda *refs: None,
        out_shape=(held((vectors, rows, lanes)), held((vectors, size, lanes))),
        out_specs=tuple(in_vmem(2)),
        name="room",
    )()
    incoming = arrived = blank
    late_blocks = [(up_block, 0, UP), *((side_blocks, face, DOWN + face) for face in range(3))]

    def tasks_at(tick):
        return [task_at(tick, place, count, vectors, lambda which, a, b: a if which else b) for place in range(count)]

    for tick in range(ticks):
        tasks = tasks_at(tick)
        plan = sent[tick]
        turning = any(turns(one) for one in tasks)
        blocks, base, latest, out, value, *cross = call(
            functools.partial(task_kernel, tick, tasks, plan),
            "task",
            (*columns, source, incoming, arrived if turning else blank),
            (blocks, base, latest, out),
            ((rows, lanes), *([(1 if tick & 1 else 2, rows, lanes)] if any(plan) else [])),
            (rows, lanes),
        )

        if any(urgent[tick]) or any(one[0] and one[2] > 0 for one in tasks_at(tick + 1)):
            pairs = []
            swap = [(s, s + 1) for s in range(tick & 1, count - 1, 2)]
            for a, b in swap:
                forth, back = (0 if tasks[one][0] else 1 for one in (a, b))
                if forth and back:
                    forth = back = 0
                for p in range(parts):
                    pairs += [(device(a, p), device(b, p ^ forth)), (device(b, p), device(a, p ^ back))]
            alone = [s for s in range(count) if all(s not in two for two in swap)]
            pairs += [(device(s, x), device(s, y)) for s in alone for a, b in even_pairs for x, y in ((a, b), (b, a))]
            incoming = lax.ppermute(value, ("sweep", "span"), pairs)
        came = [None if not tick or urgent[tick - 1][s] else sent[tick - 1][s] for s in range(count)]
        if any(came):
            blocks, base = call(
                functools.partial(side_kernel, came),
                "side",
                (columns[2], columns[3], arrived),
                (blocks, base),
                (),
                (rows, lanes),
            )
        if any(plan):
            pairs = [
                (device(s, a), device(s, b))
                for s in range(count)
                if plan[s] is not None
                for a, b in (odd_pairs if plan[s][0] else even_pairs)
            ]
            arrived = lax.ppermute(cross[0], ("sweep", "span"), closed(pairs, range(count * parts)))
        if any(urgent[tick]):
            blocks, base = call(
                functools.partial(turn_kernel, tick + 1, vectors),
                "turn",
                (columns[2], columns[3], incoming),
                (blocks, base),
                (),
                (rows, lanes),
            )
        if tick < len(late_blocks):
            blocks = later_call(*late_blocks[tick], blocks)
    return out[None, None]


def solution(mesh):
    return jax.shard_map(
        per_device,
        mesh=mesh,
        in_specs=(
            P("sweep", "span", None, None, None),
            P("sweep", "span", None, None, None),
            P("sweep", "span", None, None, None),
            P("sweep", "span", None, None, None, None),
            P("sweep", "span", None),
            P("sweep", "span", None),
            P("sweep", "span", None),
            P("sweep", "span", None),
        ),
        out_specs=P("sweep", "span", None, None, None),
        check_vma=False,
    )
```

```python
import functools

import jax
import jax.numpy as jnp
from jax import lax
from jax.experimental import pallas as pl
from jax.experimental.pallas import tpu as pltpu
from jax.sharding import PartitionSpec as P

SUBLANES = 8
VMEM_LIMIT = 2 * 1024 * 1024
PREPARE_LIMIT = 12 * 1024 * 1024
LATERAL_START = 4
CHUNKS = 4
DIAG, UP, DOWN, LEFT, RIGHT = range(5)


def task_at(tick, place, count, vectors, choose=jnp.where):
    forward = ((tick - place) & 1) == 0
    rank = choose(forward, place, count - 1 - place)
    since = tick - rank - choose(forward, 0, count)
    late = since >= 2 * count
    since = choose(late, since - 2 * count, since)
    active = (since >= 0) & (since < 2 * vectors)
    half = choose(forward, 0, 1) + choose(late, 2, 0)
    return active, choose(active, since >> 1, 0), rank, forward, half


def turns(task):
    active, _, rank, _, half = task
    return active & (rank == 0) & (half > 0)


def lateral_plan(count, vectors):
    ticks = 4 * count + 2 * (vectors - 1)
    sent = [[None] * count for _ in range(ticks)]
    urgent = [[False] * count for _ in range(ticks)]
    for slab in range(count):
        fixed, waiting, busy = [], ([], []), set()
        for half in range(4):
            rank = count - 1 - slab if half & 1 else slab
            for vector in range(vectors):
                made = 2 * vector + half * count + rank
                used = 2 * vector + (half + 1) * count + count - 1 - rank
                busy.add(made)
                if half == 3:
                    continue
                if used == made + 1:
                    fixed.append((made, (1, (vector,))))
                    urgent[made][slab] = True
                    continue
                waiting[1].append((used, made, vector))
                if used == made + 3:
                    fixed.append((made + 1, (0, (vector,))))
                else:
                    waiting[0].append((used, made, vector))
        even = range(LATERAL_START, ticks, 2)
        found = in_order(waiting, [tick for tick in even if tick not in busy]) or in_order(waiting, even)
        for tick, one in (*fixed, *found):
            sent[tick][slab] = one
    return sent, urgent


def in_order(waiting, slots):
    left = tuple(list(kind) for kind in waiting)
    found = []
    for tick in slots:
        ready = [sorted(one for one in kind if one[1] <= tick)[:2] for kind in left]
        if not any(ready):
            continue
        pairs = 0 if ready[0] and (not ready[1] or ready[0][0][0] <= ready[1][0][0]) else 1
        if tick > ready[pairs][0][0] - 2:
            return None
        found.append((tick, (pairs, tuple(one[2] for one in ready[pairs]))))
        for one in ready[pairs]:
            left[pairs].remove(one)
    return None if any(left) else found


def numbers(plan, entry):
    if entry < 0:
        return [-1 if one is None else one[0] for one in plan]
    return [-1 if one is None or len(one[1]) <= entry else one[1][entry] for one in plan]


def pick(values, place):
    result = jnp.int32(values[0])
    for at, value in enumerate(values):
        if value != values[0]:
            result = jnp.where(place == at, value, result)
    return result


def product(matrix, vector, rows):
    count = matrix.shape[0]
    group = 3 * SUBLANES

    def add(first, amount, total):
        tile = vector[pl.ds(first, SUBLANES), :]
        for row in range(amount):
            total = total + matrix[first + row] * tile[row : row + 1, :]
        return total

    def body(step, total):
        for n in range(0, group, SUBLANES):
            total = add(pl.multiple_of(step * group + n, SUBLANES), SUBLANES, total)
        return total

    total = lax.fori_loop(0, count // group, body, jnp.zeros((rows, matrix.shape[2]), jnp.float32))
    for first in range(count - count % group, count, SUBLANES):
        total = add(first, min(SUBLANES, count - first), total)
    return total


def gathered(value, columns):
    index = jnp.broadcast_to(columns, value.shape)
    return jnp.take_along_axis(value, index, axis=1, mode="promise_in_bounds")


def take_lateral(base, vector, blocks, left_cols, right_cols, arrived, spare, pairs):
    part = lax.axis_index("span")
    on_right = (part & 1) == pairs

    @pl.when(jnp.where(on_right, part < lax.axis_size("span") - 1, part > 0))
    def _():
        spare[...] = gathered(arrived, jnp.where(on_right, right_cols[...], left_cols[...]))
        base[vector] = base[vector] - product(blocks.at[jnp.where(on_right, RIGHT, LEFT)], spare, spare.shape[0])


def prepare(block, ready, narrow, wide, sems, low, high):
    size, _, lanes = block.shape
    rows = ready.shape[1]
    bounds = [low + (high - low) * n // CHUNKS for n in range(CHUNKS + 1)]
    shares = list(zip(bounds, bounds[1:]))
    copies = [
        pltpu.make_async_copy(block.at[pl.ds(a, b - a)], narrow.at[pl.ds(a, b - a)], sems.at[n])
        for n, (a, b) in enumerate(shares)
    ]
    for copy in copies:
        copy.start()
    if high == size:
        wide[pl.ds(size * rows, (rows - size) * rows), :] = jnp.zeros(((rows - size) * rows, lanes), jnp.float32)

    def widen(i, _):
        wide[pl.ds(pl.multiple_of(i * rows, SUBLANES), size), :] = narrow[i].astype(jnp.float32)
        return 0

    for (a, b), copy in zip(shares, copies):
        copy.wait()
        lax.fori_loop(a, b, widen, 0, unroll=next(n for n in (5, 4, 1) if (b - a) % n == 0))

    def turn(j, _):
        for i in range(low, high, SUBLANES):
            ready[j, pl.ds(i, SUBLANES), :] = wide[pl.ds(i * rows + j, SUBLANES, stride=rows), :]
        return 0

    lax.fori_loop(0, size, turn, 0, unroll=4)


def first_kernel(block, residual, *refs):
    hbm_columns, (blocks, base, source, blank, *columns), (narrow, wide, sems, column_sems, held_residual) = (
        refs[:4], refs[4:12], refs[12:]
    )
    copies = [
        pltpu.make_async_copy(there, here, column_sems.at[n])
        for n, (there, here) in enumerate(zip((*hbm_columns, residual), (*columns, held_residual)))
    ]
    for copy in copies:
        copy.start()
    size, vectors, lanes = residual.shape
    prepare(block, blocks.at[DIAG], narrow, wide, sems, 0, size)
    for copy in copies:
        copy.wait()
    rows = base.shape[1]
    base[:, pl.ds(rows - SUBLANES, SUBLANES), :] = jnp.zeros((vectors, SUBLANES, lanes), jnp.float32)
    for vector in range(vectors):
        base[vector, pl.ds(0, size), :] = held_residual[:, vector, :]
    source[...] = base[...]
    blank[...] = jnp.zeros_like(blank)


def later_kernel(face, slot, low, high, block, blocks_in, blocks, narrow, wide, sems):
    prepare(block.at[(0,) * (len(block.shape) - 4) + (face,)], blocks.at[slot], narrow, wide, sems, low, high)


def task_kernel(
    tick, tasks, sent, columns_and_inputs, kept, values, spare
):
    up_cols, down_cols, left_cols, right_cols, source, incoming, arrived = columns_and_inputs
    value, *cross = values
    blocks, base, latest, out = kept
    rows = spare.shape[0]
    vectors, size, _ = out.shape
    place = lax.axis_index("sweep")
    task = task_at(tick, place, lax.axis_size("sweep"), vectors)
    active, vector, rank, forward, half = task

    if any(turns(one) for one in tasks):

        @pl.when(turns(task))
        def _():
            take_lateral(base, vector, blocks, left_cols, right_cols, arrived[0], spare, 1)

    @pl.when(active)
    def _():
        known = base[vector]
        value[...] = known
        base[vector] = source[vector]

        if any(one[0] and one[2] > 0 for one in tasks):

            @pl.when(rank > 0)
            def _():
                spare[...] = gathered(incoming[...], jnp.where(forward, up_cols[...], down_cols[...]))
                term = product(blocks.at[jnp.where(forward, UP, DOWN)], spare, rows)
                value[...] = known - term
                base[vector] = source[vector] - term

        spare[...] = value[...]
        fresh = product(blocks.at[DIAG], spare, rows)
        value[...] = fresh
        latest[vector] = fresh

        if any(one[0] and one[4] == 3 for one in tasks):

            @pl.when(half == 3)
            def _():
                out[vector] = fresh[:size]

    if cross:
        fill(cross[0], latest, sent, place)


def fill(cross, latest, plan, place):
    for entry in range(cross.shape[0]):
        chosen = numbers(plan, entry)
        if any(one >= 0 for one in chosen):
            vector = pick(chosen, place)

            @pl.when(vector >= 0)
            def _():
                cross[entry] = latest[vector]


def side_kernel(came, columns_and_inputs, kept, values, spare):
    left_cols, right_cols, arrived = columns_and_inputs
    blocks, base = kept
    place = lax.axis_index("sweep")
    pairs = pick(numbers(came, -1), place)
    for entry in range(arrived.shape[0]):
        chosen = numbers(came, entry)
        if any(one >= 0 for one in chosen):
            vector = pick(chosen, place)

            @pl.when(vector >= 0)
            def _():
                take_lateral(base, vector, blocks, left_cols, right_cols, arrived[entry], spare, pairs)


def turn_kernel(tick, vectors, columns_and_inputs, kept, values, spare):
    left_cols, right_cols, incoming = columns_and_inputs
    blocks, base = kept
    task = task_at(tick, lax.axis_index("sweep"), lax.axis_size("sweep"), vectors)

    @pl.when(turns(task))
    def _():
        take_lateral(base, task[1], blocks, left_cols, right_cols, incoming[...], spare, 0)


def in_vmem(count):
    return [pl.BlockSpec(memory_space=pltpu.VMEM)] * count


def far(array):
    return pltpu.with_memory_space_constraint(array, pltpu.HBM)


def held(shape):
    return pltpu.VMEM(shape, jnp.float32)


def call(kernel, name, fixed, kept, fresh, spare):
    def body(*refs):
        inputs, outputs = refs[: len(fixed)], refs[len(fixed) + len(kept) : -1]
        kernel(inputs, outputs[: len(kept)], outputs[len(kept) :], refs[-1])

    return pl.pallas_call(
        body,
        out_shape=tuple(held(shape) for shape in [*(a.shape for a in kept), *fresh]),
        in_specs=in_vmem(len(fixed) + len(kept)),
        out_specs=tuple(in_vmem(len(fresh) + len(kept))),
        scratch_shapes=[held(spare)],
        input_output_aliases={len(fixed) + n: n for n in range(len(kept))},
        compiler_params=pltpu.CompilerParams(vmem_limit_bytes=VMEM_LIMIT),
        name=name,
    )(*fixed, *kept)


def preparing(size, rows, lanes):
    return [
        pltpu.VMEM((size, size, lanes), jnp.bfloat16),
        held((rows * rows, lanes)),
        pltpu.SemaphoreType.DMA((CHUNKS,)),
    ]


def first_call(block, residual, columns, rows):
    size, vectors, lanes = residual.shape
    several = (vectors, rows, lanes)
    in_hbm = pl.BlockSpec(memory_space=pltpu.HBM)
    return pl.pallas_call(
        first_kernel,
        out_shape=(
            held((5, size, rows, lanes)), held(several), held(several), held((rows, lanes)),
            *(pltpu.VMEM(one.shape, one.dtype) for one in columns),
        ),
        in_specs=[in_hbm] * 6,
        out_specs=tuple(in_vmem(8)),
        scratch_shapes=[
            *preparing(size, rows, lanes), pltpu.SemaphoreType.DMA((5,)), held((size, vectors, lanes))
        ],
        compiler_params=pltpu.CompilerParams(vmem_limit_bytes=PREPARE_LIMIT),
        name="first",
    )(far(block), far(residual), *(far(one) for one in columns))


def later_call(blocks, block, face, slot, low, high):
    return pl.pallas_call(
        functools.partial(later_kernel, face, slot, low, high),
        out_shape=held(blocks.shape),
        in_specs=[pl.BlockSpec(memory_space=pltpu.HBM), *in_vmem(1)],
        out_specs=in_vmem(1)[0],
        scratch_shapes=preparing(*blocks.shape[1:]),
        input_output_aliases={1: 0},
        compiler_params=pltpu.CompilerParams(vmem_limit_bytes=PREPARE_LIMIT),
        name="later",
    )(far(block), blocks)


def per_device(
    residual_in, diag_inverse, up_block, side_blocks, up_cols, down_cols, left_cols, right_cols
):
    vectors, size, lanes = residual_in.shape[2:]
    rows = size + -size % SUBLANES
    columns = [one.reshape(1, lanes) for one in (up_cols, down_cols, left_cols, right_cols)]
    count = lax.axis_size("sweep")
    parts = lax.axis_size("span")
    ticks = 4 * count + 2 * (vectors - 1)
    sent, urgent = lateral_plan(count, vectors)
    even_pairs = [(p, p + 1) for p in range(0, parts - 1, 2)]
    odd_pairs = [(p, p + 1) for p in range(1, parts - 1, 2)]

    def closed(pairs, members):
        alone = [one for one in members if all(one not in two for two in pairs)]
        return [*pairs, *((b, a) for a, b in pairs), *((one, one) for one in alone)]

    def device(slab, part):
        return slab * parts + part

    blocks, base, source, blank, *columns = first_call(
        diag_inverse[0, 0], jnp.transpose(residual_in[0, 0], (1, 0, 2)), columns, rows
    )
    latest, out = pl.pallas_call(
        lambda *refs: None,
        out_shape=(held((vectors, rows, lanes)), held((vectors, size, lanes))),
        out_specs=tuple(in_vmem(2)),
        name="room",
    )()
    incoming = arrived = blank
    middle = size // 2 // SUBLANES * SUBLANES
    late_blocks = [(up_block, 0, UP, 0, size)]
    for slot in (LEFT, RIGHT, DOWN):
        late_blocks += [(side_blocks, slot - DOWN, slot, 0, middle), (side_blocks, slot - DOWN, slot, middle, size)]

    def tasks_at(tick):
        return [task_at(tick, place, count, vectors, lambda which, a, b: a if which else b) for place in range(count)]

    for tick in range(ticks):
        tasks = tasks_at(tick)
        plan = sent[tick]
        turning = any(turns(one) for one in tasks)
        blocks, base, latest, out, value, *cross = call(
            functools.partial(task_kernel, tick, tasks, plan),
            "task",
            (*columns, source, incoming, arrived if turning else blank),
            (blocks, base, latest, out),
            ((rows, lanes), *([(1 if tick & 1 else 2, rows, lanes)] if any(plan) else [])),
            (rows, lanes),
        )

        if any(urgent[tick]) or any(one[0] and one[2] > 0 for one in tasks_at(tick + 1)):
            pairs = []
            swap = [(s, s + 1) for s in range(tick & 1, count - 1, 2)]
            for a, b in swap:
                forth, back = (0 if tasks[one][0] else 1 for one in (a, b))
                if forth and back:
                    forth = back = 0
                for p in range(parts):
                    pairs += [(device(a, p), device(b, p ^ forth)), (device(b, p), device(a, p ^ back))]
            alone = [s for s in range(count) if all(s not in two for two in swap)]
            pairs += [(device(s, x), device(s, y)) for s in alone for a, b in even_pairs for x, y in ((a, b), (b, a))]
            incoming = lax.ppermute(value, ("sweep", "span"), pairs)
        came = [None if not tick or urgent[tick - 1][s] else sent[tick - 1][s] for s in range(count)]
        if any(came):
            blocks, base = call(
                functools.partial(side_kernel, came),
                "side",
                (columns[2], columns[3], arrived),
                (blocks, base),
                (),
                (rows, lanes),
            )
        if any(plan):
            pairs = [
                (device(s, a), device(s, b))
                for s in range(count)
                if plan[s] is not None
                for a, b in (odd_pairs if plan[s][0] else even_pairs)
            ]
            arrived = lax.ppermute(cross[0], ("sweep", "span"), closed(pairs, range(count * parts)))
        if any(urgent[tick]):
            blocks, base = call(
                functools.partial(turn_kernel, tick + 1, vectors),
                "turn",
                (columns[2], columns[3], incoming),
                (blocks, base),
                (),
                (rows, lanes),
            )
        if tick < len(late_blocks):
            blocks = later_call(blocks, *late_blocks[tick])
    return out[None, None]


def solution(mesh):
    return jax.shard_map(
        per_device,
        mesh=mesh,
        in_specs=(
            P("sweep", "span", None, None, None),
            P("sweep", "span", None, None, None),
            P("sweep", "span", None, None, None),
            P("sweep", "span", None, None, None, None),
            P("sweep", "span", None),
            P("sweep", "span", None),
            P("sweep", "span", None),
            P("sweep", "span", None),
        ),
        out_specs=P("sweep", "span", None, None, None),
        check_vma=False,
    )
```

```python
import functools

import jax
import jax.numpy as jnp
from jax import lax
from jax.experimental import pallas as pl
from jax.experimental.pallas import tpu as pltpu
from jax.sharding import PartitionSpec as P

SUBLANES = 8
VMEM_LIMIT = 2 * 1024 * 1024
PREPARE_LIMIT = 12 * 1024 * 1024
LATERAL_START = 6
CHUNKS = 4
DIAG, UP, DOWN, LEFT, RIGHT = range(5)


def task_at(tick, place, count, vectors, choose=jnp.where):
    forward = ((tick - place) & 1) == 0
    rank = choose(forward, place, count - 1 - place)
    since = tick - rank - choose(forward, 0, count)
    late = since >= 2 * count
    since = choose(late, since - 2 * count, since)
    active = (since >= 0) & (since < 2 * vectors)
    half = choose(forward, 0, 1) + choose(late, 2, 0)
    return active, choose(active, since >> 1, 0), rank, forward, half


def turns(task):
    active, _, rank, _, half = task
    return active & (rank == 0) & (half > 0)


def lateral_plan(count, vectors):
    ticks = 4 * count + 2 * (vectors - 1)
    sent = [[None] * count for _ in range(ticks)]
    urgent = [[False] * count for _ in range(ticks)]
    for slab in range(count):
        fixed, waiting, busy = [], ([], []), set()
        for half in range(4):
            rank = count - 1 - slab if half & 1 else slab
            for vector in range(vectors):
                made = 2 * vector + half * count + rank
                used = 2 * vector + (half + 1) * count + count - 1 - rank
                busy.add(made)
                if half == 3:
                    continue
                if used == made + 1:
                    fixed.append((made, (1, (vector,))))
                    urgent[made][slab] = True
                    continue
                waiting[1].append((used, made, vector))
                if used == made + 3:
                    fixed.append((made + 1, (0, (vector,))))
                else:
                    waiting[0].append((used, made, vector))
        even = range(LATERAL_START, ticks, 2)
        found = in_order(waiting, [tick for tick in even if tick not in busy]) or in_order(waiting, even)
        for tick, one in (*fixed, *found):
            sent[tick][slab] = one
    return sent, urgent


def in_order(waiting, slots):
    left = tuple(list(kind) for kind in waiting)
    found = []
    for tick in slots:
        ready = [sorted(one for one in kind if one[1] <= tick)[:2] for kind in left]
        if not any(ready):
            continue
        pairs = 0 if ready[0] and (not ready[1] or ready[0][0][0] <= ready[1][0][0]) else 1
        if tick > ready[pairs][0][0] - 2:
            return None
        found.append((tick, (pairs, tuple(one[2] for one in ready[pairs]))))
        for one in ready[pairs]:
            left[pairs].remove(one)
    return None if any(left) else found


def numbers(plan, entry):
    if entry < 0:
        return [-1 if one is None else one[0] for one in plan]
    return [-1 if one is None or len(one[1]) <= entry else one[1][entry] for one in plan]


def pick(values, place):
    result = jnp.int32(values[0])
    for at, value in enumerate(values):
        if value != values[0]:
            result = jnp.where(place == at, value, result)
    return result


def product(matrix, vector, rows):
    count = matrix.shape[0]
    group = 3 * SUBLANES

    def add(first, amount, total):
        tile = vector[pl.ds(first, SUBLANES), :]
        for row in range(amount):
            total = total + matrix[first + row] * tile[row : row + 1, :]
        return total

    def body(step, total):
        for n in range(0, group, SUBLANES):
            total = add(pl.multiple_of(step * group + n, SUBLANES), SUBLANES, total)
        return total

    total = lax.fori_loop(0, count // group, body, jnp.zeros((rows, matrix.shape[2]), jnp.float32))
    for first in range(count - count % group, count, SUBLANES):
        total = add(first, min(SUBLANES, count - first), total)
    return total


def gathered(value, columns):
    index = jnp.broadcast_to(columns, value.shape)
    return jnp.take_along_axis(value, index, axis=1, mode="promise_in_bounds")


def take_lateral(base, vector, blocks, left_cols, right_cols, arrived, spare, pairs):
    part = lax.axis_index("span")
    on_right = (part & 1) == pairs

    @pl.when(jnp.where(on_right, part < lax.axis_size("span") - 1, part > 0))
    def _():
        spare[...] = gathered(arrived, jnp.where(on_right, right_cols[...], left_cols[...]))
        base[vector] = base[vector] - product(blocks.at[jnp.where(on_right, RIGHT, LEFT)], spare, spare.shape[0])


def prepare(block, ready, narrow, wide, sems, low, high):
    size, _, lanes = block.shape
    rows = ready.shape[1]
    bounds = [low + (high - low) * n // CHUNKS for n in range(CHUNKS + 1)]
    shares = list(zip(bounds, bounds[1:]))
    copies = [
        pltpu.make_async_copy(block.at[pl.ds(a, b - a)], narrow.at[pl.ds(a, b - a)], sems.at[n])
        for n, (a, b) in enumerate(shares)
    ]
    for copy in copies:
        copy.start()
    if high == size:
        wide[pl.ds(size * rows, (rows - size) * rows), :] = jnp.zeros(((rows - size) * rows, lanes), jnp.float32)

    def widen(i, _):
        wide[pl.ds(pl.multiple_of(i * rows, SUBLANES), size), :] = narrow[i].astype(jnp.float32)
        return 0

    for (a, b), copy in zip(shares, copies):
        copy.wait()
        lax.fori_loop(a, b, widen, 0, unroll=next(n for n in (5, 4, 1) if (b - a) % n == 0))

    def turn(j, _):
        for i in range(low, high, SUBLANES):
            ready[j, pl.ds(i, SUBLANES), :] = wide[pl.ds(i * rows + j, SUBLANES, stride=rows), :]
        return 0

    lax.fori_loop(0, size, turn, 0, unroll=4)


def first_kernel(block, residual, *refs):
    hbm_columns, (blocks, base, source, blank, *columns), (narrow, wide, sems, column_sems, held_residual) = (
        refs[:4], refs[4:12], refs[12:]
    )
    copies = [
        pltpu.make_async_copy(there, here, column_sems.at[n])
        for n, (there, here) in enumerate(zip((*hbm_columns, residual), (*columns, held_residual)))
    ]
    for copy in copies:
        copy.start()
    size, vectors, lanes = residual.shape
    prepare(block, blocks.at[DIAG], narrow, wide, sems, 0, size)
    for copy in copies:
        copy.wait()
    rows = base.shape[1]
    base[:, pl.ds(rows - SUBLANES, SUBLANES), :] = jnp.zeros((vectors, SUBLANES, lanes), jnp.float32)
    for vector in range(vectors):
        base[vector, pl.ds(0, size), :] = held_residual[:, vector, :]
    source[...] = base[...]
    blank[...] = jnp.zeros_like(blank)


def later_kernel(face, slot, low, high, block, blocks_in, blocks, narrow, wide, sems):
    prepare(block.at[(0,) * (len(block.shape) - 4) + (face,)], blocks.at[slot], narrow, wide, sems, low, high)


def task_kernel(
    tick, tasks, sent, columns_and_inputs, kept, values, spare
):
    up_cols, down_cols, left_cols, right_cols, source, incoming, arrived = columns_and_inputs
    value, *cross = values
    blocks, base, latest, out = kept
    rows = spare.shape[0]
    vectors, size, _ = out.shape
    place = lax.axis_index("sweep")
    task = task_at(tick, place, lax.axis_size("sweep"), vectors)
    active, vector, rank, forward, half = task

    if any(turns(one) for one in tasks):

        @pl.when(turns(task))
        def _():
            take_lateral(base, vector, blocks, left_cols, right_cols, arrived[0], spare, 1)

    @pl.when(active)
    def _():
        known = base[vector]
        value[...] = known
        base[vector] = source[vector]

        if any(one[0] and one[2] > 0 for one in tasks):

            @pl.when(rank > 0)
            def _():
                spare[...] = gathered(incoming[...], jnp.where(forward, up_cols[...], down_cols[...]))
                term = product(blocks.at[jnp.where(forward, UP, DOWN)], spare, rows)
                value[...] = known - term
                base[vector] = source[vector] - term

        spare[...] = value[...]
        fresh = product(blocks.at[DIAG], spare, rows)
        value[...] = fresh
        latest[vector] = fresh

        if any(one[0] and one[4] == 3 for one in tasks):

            @pl.when(half == 3)
            def _():
                out[vector] = fresh[:size]

    if cross:
        fill(cross[0], latest, sent, place)


def fill(cross, latest, plan, place):
    for entry in range(cross.shape[0]):
        chosen = numbers(plan, entry)
        if any(one >= 0 for one in chosen):
            vector = pick(chosen, place)

            @pl.when(vector >= 0)
            def _():
                cross[entry] = latest[vector]


def side_kernel(came, columns_and_inputs, kept, values, spare):
    left_cols, right_cols, arrived = columns_and_inputs
    blocks, base = kept
    place = lax.axis_index("sweep")
    pairs = pick(numbers(came, -1), place)
    for entry in range(arrived.shape[0]):
        chosen = numbers(came, entry)
        if any(one >= 0 for one in chosen):
            vector = pick(chosen, place)

            @pl.when(vector >= 0)
            def _():
                take_lateral(base, vector, blocks, left_cols, right_cols, arrived[entry], spare, pairs)


def turn_kernel(tick, vectors, columns_and_inputs, kept, values, spare):
    left_cols, right_cols, incoming = columns_and_inputs
    blocks, base = kept
    task = task_at(tick, lax.axis_index("sweep"), lax.axis_size("sweep"), vectors)

    @pl.when(turns(task))
    def _():
        take_lateral(base, task[1], blocks, left_cols, right_cols, incoming[...], spare, 0)


def in_vmem(count):
    return [pl.BlockSpec(memory_space=pltpu.VMEM)] * count


def far(array):
    return pltpu.with_memory_space_constraint(array, pltpu.HBM)


def held(shape):
    return pltpu.VMEM(shape, jnp.float32)


def call(kernel, name, fixed, kept, fresh, spare):
    def body(*refs):
        inputs, outputs = refs[: len(fixed)], refs[len(fixed) + len(kept) : -1]
        kernel(inputs, outputs[: len(kept)], outputs[len(kept) :], refs[-1])

    return pl.pallas_call(
        body,
        out_shape=tuple(held(shape) for shape in [*(a.shape for a in kept), *fresh]),
        in_specs=in_vmem(len(fixed) + len(kept)),
        out_specs=tuple(in_vmem(len(fresh) + len(kept))),
        scratch_shapes=[held(spare)],
        input_output_aliases={len(fixed) + n: n for n in range(len(kept))},
        compiler_params=pltpu.CompilerParams(vmem_limit_bytes=VMEM_LIMIT),
        name=name,
    )(*fixed, *kept)


def preparing(size, rows, lanes):
    return [
        pltpu.VMEM((size, size, lanes), jnp.bfloat16),
        held((rows * rows, lanes)),
        pltpu.SemaphoreType.DMA((CHUNKS,)),
    ]


def first_call(block, residual, columns, rows):
    size, vectors, lanes = residual.shape
    several = (vectors, rows, lanes)
    in_hbm = pl.BlockSpec(memory_space=pltpu.HBM)
    return pl.pallas_call(
        first_kernel,
        out_shape=(
            held((5, size, rows, lanes)), held(several), held(several), held((rows, lanes)),
            *(pltpu.VMEM(one.shape, one.dtype) for one in columns),
        ),
        in_specs=[in_hbm] * 6,
        out_specs=tuple(in_vmem(8)),
        scratch_shapes=[
            *preparing(size, rows, lanes), pltpu.SemaphoreType.DMA((5,)), held((size, vectors, lanes))
        ],
        compiler_params=pltpu.CompilerParams(vmem_limit_bytes=PREPARE_LIMIT),
        name="first",
    )(far(block), far(residual), *(far(one) for one in columns))


def later_call(blocks, block, face, slot, low, high):
    return pl.pallas_call(
        functools.partial(later_kernel, face, slot, low, high),
        out_shape=held(blocks.shape),
        in_specs=[pl.BlockSpec(memory_space=pltpu.HBM), *in_vmem(1)],
        out_specs=in_vmem(1)[0],
        scratch_shapes=preparing(*blocks.shape[1:]),
        input_output_aliases={1: 0},
        compiler_params=pltpu.CompilerParams(vmem_limit_bytes=PREPARE_LIMIT),
        name="later",
    )(far(block), blocks)


def per_device(
    residual_in, diag_inverse, up_block, side_blocks, up_cols, down_cols, left_cols, right_cols
):
    vectors, size, lanes = residual_in.shape[2:]
    rows = size + -size % SUBLANES
    columns = [one.reshape(1, lanes) for one in (up_cols, down_cols, left_cols, right_cols)]
    count = lax.axis_size("sweep")
    parts = lax.axis_size("span")
    ticks = 4 * count + 2 * (vectors - 1)
    sent, urgent = lateral_plan(count, vectors)
    even_pairs = [(p, p + 1) for p in range(0, parts - 1, 2)]
    odd_pairs = [(p, p + 1) for p in range(1, parts - 1, 2)]

    def closed(pairs, members):
        alone = [one for one in members if all(one not in two for two in pairs)]
        return [*pairs, *((b, a) for a, b in pairs), *((one, one) for one in alone)]

    def device(slab, part):
        return slab * parts + part

    blocks, base, source, blank, *columns = first_call(
        diag_inverse[0, 0], jnp.transpose(residual_in[0, 0], (1, 0, 2)), columns, rows
    )
    latest, out = pl.pallas_call(
        lambda *refs: None,
        out_shape=(held((vectors, rows, lanes)), held((vectors, size, lanes))),
        out_specs=tuple(in_vmem(2)),
        name="room",
    )()
    incoming = arrived = blank
    middle = size // 2 // SUBLANES * SUBLANES
    late_blocks = [(up_block, 0, UP, 0, size)]
    for slot in (LEFT, RIGHT):
        late_blocks += [(side_blocks, slot - DOWN, slot, 0, middle), (side_blocks, slot - DOWN, slot, middle, size)]
    late_blocks.append((side_blocks, 0, DOWN, 0, size))

    def tasks_at(tick):
        return [task_at(tick, place, count, vectors, lambda which, a, b: a if which else b) for place in range(count)]

    for tick in range(ticks):
        tasks = tasks_at(tick)
        plan = sent[tick]
        turning = any(turns(one) for one in tasks)
        blocks, base, latest, out, value, *cross = call(
            functools.partial(task_kernel, tick, tasks, plan),
            "task",
            (*columns, source, incoming, arrived if turning else blank),
            (blocks, base, latest, out),
            ((rows, lanes), *([(1 if tick & 1 else 2, rows, lanes)] if any(plan) else [])),
            (rows, lanes),
        )

        if any(urgent[tick]) or any(one[0] and one[2] > 0 for one in tasks_at(tick + 1)):
            pairs = []
            swap = [(s, s + 1) for s in range(tick & 1, count - 1, 2)]
            for a, b in swap:
                forth, back = (0 if tasks[one][0] else 1 for one in (a, b))
                if forth and back:
                    forth = back = 0
                for p in range(parts):
                    pairs += [(device(a, p), device(b, p ^ forth)), (device(b, p), device(a, p ^ back))]
            alone = [s for s in range(count) if all(s not in two for two in swap)]
            pairs += [(device(s, x), device(s, y)) for s in alone for a, b in even_pairs for x, y in ((a, b), (b, a))]
            incoming = lax.ppermute(value, ("sweep", "span"), pairs)
        came = [None if not tick or urgent[tick - 1][s] else sent[tick - 1][s] for s in range(count)]
        if any(came):
            blocks, base = call(
                functools.partial(side_kernel, came),
                "side",
                (columns[2], columns[3], arrived),
                (blocks, base),
                (),
                (rows, lanes),
            )
        if any(plan):
            pairs = [
                (device(s, a), device(s, b))
                for s in range(count)
                if plan[s] is not None
                for a, b in (odd_pairs if plan[s][0] else even_pairs)
            ]
            arrived = lax.ppermute(cross[0], ("sweep", "span"), closed(pairs, range(count * parts)))
        if any(urgent[tick]):
            blocks, base = call(
                functools.partial(turn_kernel, tick + 1, vectors),
                "turn",
                (columns[2], columns[3], incoming),
                (blocks, base),
                (),
                (rows, lanes),
            )
        if tick < len(late_blocks):
            blocks = later_call(blocks, *late_blocks[tick])
    return out[None, None]


def solution(mesh):
    return jax.shard_map(
        per_device,
        mesh=mesh,
        in_specs=(
            P("sweep", "span", None, None, None),
            P("sweep", "span", None, None, None),
            P("sweep", "span", None, None, None),
            P("sweep", "span", None, None, None, None),
            P("sweep", "span", None),
            P("sweep", "span", None),
            P("sweep", "span", None),
            P("sweep", "span", None),
        ),
        out_specs=P("sweep", "span", None, None, None),
        check_vma=False,
    )
```
